256 devices in a mesh: px: 16 (over y, x), py: 16 (over z, core).
Axes of the slice: x: 4, y: 4, z: 8, core: 2. Of those that a mesh axis runs over, the one named last changes fastest.
Arguments:
- point_features: bfloat16 [262144, 64], P(('px', 'py')), may hold values from -6 to 6
- positions: bfloat16 [262144, 3], P(('px', 'py')), may hold values from -1 to 1
- targets: bfloat16 [262144], P(('px', 'py')), may hold values from -6 to 6
- routes: int32 [262144, 1], P(('px', 'py')), may hold values from 0 to 255; in each aligned block of 1024 rows (0 to 1023, 1024 to 2047, ...) at most 8 rows name the same one
- live_counts: int32 [256], P(('px', 'py')), may hold values from 512 to 1024, as said below
- cell_neighbours: int32 [128, 64, 2048], P('px', 'py'), may hold values from 0 to 2047
- cell_counts: int32 [128, 64, 256], P('px', 'py'), may hold values from 1 to 8
- slot_neighbours: int32 [256, 8192], P(('px', 'py')), may hold values from 0 to 8191
- encoder_in: float32 [3, 80], replicated, may hold values from -4 to 4
- encoder_bias: float32 [80], replicated, may hold values from -4 to 4
- encoder_out: bfloat16 [80, 64], replicated, may hold values from -0.625 to 0.625
- decoder_in: float32 [3, 256], replicated, may hold values from -4 to 4
- decoder_bias: float32 [256], replicated, may hold values from -4 to 4
- decoder_out: bfloat16 [256, 64], replicated, may hold values from -0.375 to 0.375
- skip_weight: bfloat16 [64, 64], replicated, may hold values from -0.75 to 0.75
- spectral_weight: bfloat16 [32, 32, 16, 64, 128], P(None, 'px', 'py'), may hold values from -6 to 6
- readout_weight: float32 [64], replicated, may hold values from -3 to 3
Outputs:
- prediction: float32 [256, 2048], P(('px', 'py'))
- spectral_grad: float32 [32, 32, 16, 64, 128], P(None, 'px', 'py')
The draws below stay inside these ranges and needn't reach their ends.
Inputs may be any that keep to these rules, and one draw needn't show every extreme that they name: `routes`: owner of a point, a mesh index px * 16 + py. Among the rows of one block no owner is named by more than 8 rows. `live_counts`: points of a block from this count on are padding and go nowhere. `cell_neighbours`: A slot index source block times 8 plus rank, of the owner of the cell; entries from cell_counts on are unused. `slot_neighbours`: A local cell index of the owner.
All inputs are finite; a program needn't handle non-finite values.
Results may differ from the reference program's by a relative error of at most 0.014.
Values may be sent and summed in bfloat16 or wider, within the bound.
A program may use at most 128 MiB of HBM per device.

```python
import math
import jax
import jax.numpy as jnp
import numpy as np
from jax import lax

C = 64
M = 16
MZ = 16
EHID = 80
DHID = 256
KE = 8
KD = 4
CX = 8
CY = 4
GZ = 256
PTS_DEV = 1024
GX = 128
GY = 64
PTS = 262144
CAP = 8
SLOTS = 2048
CELLS = 8192
N_PX = 16
N_PY = 16
DEVICES = 256


def draw_live_counts(key, part):
    key = jax.random.fold_in(key, 11)
    first_key, second_key = jax.random.split(key)
    devices = N_PX * N_PY
    counted = jax.random.randint(first_key, (devices,), PTS_DEV // 2, PTS_DEV + 1)
    chosen = jax.random.randint(second_key, (), 0, devices)
    return jnp.where(jnp.arange(devices) == chosen, PTS_DEV, counted).astype(jnp.int32)


def with_ends(array, rng, low, high):
    index_at = [jax.random.randint(jax.random.fold_in(rng, axis), (), 0, length) for axis, length in enumerate(array.shape)]
    widest = array.shape.index(max(array.shape))
    beside = index_at[:widest] + [(index_at[widest] + 1) % array.shape[widest]] + index_at[widest + 1:]
    return array.at[tuple(index_at)].set(low).at[tuple(beside)].set(high)


def block_levels(own_key, extent, pieces, smallest, high):
    level, own = 1.0, jax.random.fold_in(own_key, 6)
    for axis_at, blocks in pieces:
        steps = jnp.exp(jax.random.uniform(jax.random.fold_in(own, axis_at), (blocks,), jnp.float32, smallest / len(pieces), high / len(pieces)))
        level = level * jnp.repeat(steps, extent[axis_at] // blocks).reshape([-1 if axis == axis_at else 1 for axis in range(len(extent))])
    return level


def shared_out(key, own, number, rows, number_of, top, limit, lean):
    sequence = jax.random.permutation(key, number_of)
    crowded, usual = portions_of(number_of, rows * top, limit, lean, True), portions_of(number_of, rows * top, limit, lean, False)
    places = jnp.arange(number_of)

    def named(tallies, rotation):
        used = int((tallies > 0).sum())
        fixed = max(1, used // 4)
        shifted = fixed + (places - fixed + rotation * (used - fixed)) % max(1, number_of - fixed)
        return jnp.zeros((number_of,), jnp.int32).at[sequence[jnp.where(places < fixed, places, shifted)]].set(jnp.asarray(tallies, jnp.int32))

    tallies = jnp.where(number % 4 == 0, named(crowded, number // 4), named(usual, number - number // 4 - 1))
    mixed = jax.random.permutation(jax.random.fold_in(own, 3), number_of)
    donor, receiver = mixed[0:number_of // 2 * 2:2], mixed[1:number_of // 2 * 2:2]
    margin = jnp.minimum(tallies[donor] - 1, limit - tallies[receiver]) // 2
    margin = jnp.where((donor == sequence[0]) | (receiver == sequence[0]) | (tallies[receiver] == 0), 0, jnp.maximum(margin, 0))
    shifted = jax.random.randint(jax.random.fold_in(own, 4), (number_of // 2,), 0, 1 << 20) % (margin + 1)
    tallies = tallies.at[donor].add(-shifted).at[receiver].add(shifted)
    members = jnp.searchsorted(jnp.cumsum(tallies), jnp.arange(rows * top), side="right").astype(jnp.int32)
    grid = members.reshape(top, rows).T
    grid = grid[jax.random.permutation(jax.random.fold_in(own, 1), rows)]
    rotation = jax.random.randint(jax.random.fold_in(own, 2), (rows, 1), 0, top)
    return jnp.take_along_axis(grid, (jnp.arange(top)[None, :] + rotation) % top, axis=1)


def portions_of(count, total, limit, slope, full):
    portions = [(1 << 20) // math.isqrt(grade ** slope) + 1 for grade in range(1, count + 1)]
    largest = limit if full else min(limit, max(-(-total // count), total * portions[0] // sum(portions)))
    least = 1 if total - largest >= count - 1 else 0
    counts, surplus = [largest] + [least] * (count - 1), total - largest - least * (count - 1)
    while surplus > 0:
        candidates = [i for i in range(1, count) if counts[i] < largest] or [i for i in range(1, count) if counts[i] < limit]
        mass, left = sum([portions[i] for i in candidates]), surplus
        for i in candidates:
            more = min(limit - counts[i], max(1, left * portions[i] // mass), surplus)
            counts[i] = counts[i] + more
            surplus = surplus - more
    return np.array(counts)


def bell_draw(key, extent, scale, limit, cuts=(), kind=jnp.bfloat16):
    factor_of = block_levels(key, extent, cuts, -0.22, 0.18) if cuts else 1.0
    entries = jax.random.normal(key, extent, jnp.float32) * scale * factor_of
    return jnp.minimum(jnp.maximum(entries, -limit), limit).astype(kind)


def setup_inputs(seed: int = 0) -> dict:
    streams_of = jax.random.split(jax.random.key(seed), 18)
    point_features = bell_draw(streams_of[0], (PTS, C), 1.0, 6.0, ((0, 256),))
    positions = jnp.clip(jax.random.uniform(streams_of[1], (PTS, 3), jnp.float32, -1.0, 1.0) * block_levels(streams_of[1], (PTS, 3), ((0, 256),), -0.4, 0.0), -1.0, 1.0).astype(jnp.bfloat16)
    targets = bell_draw(streams_of[2], (PTS,), 1.0, 6.0, ((0, 256),))
    routes_keys = jax.random.split(jax.random.fold_in(streams_of[3], 1), PTS // PTS_DEV)
    routes_turns = jax.random.permutation(jax.random.fold_in(streams_of[3], 3), PTS // PTS_DEV)
    routes = jax.vmap(lambda own, number: shared_out(jax.random.fold_in(streams_of[3], 2), own, number, PTS_DEV, N_PX * N_PY, 1, CAP, 2))(routes_keys, routes_turns).reshape((PTS, 1))
    live_counts = draw_live_counts(jax.random.fold_in(streams_of[17], 71), 0)
    cell_neighbours = with_ends(jax.random.randint(streams_of[5], (GX, GY, GZ * KE), 0, SLOTS), jax.random.fold_in(streams_of[5], 1), 0, SLOTS - 1).astype(jnp.int32)
    cell_counts = with_ends(jax.random.randint(streams_of[6], (GX, GY, GZ), 1, KE + 1), jax.random.fold_in(streams_of[6], 1), 1, KE).astype(jnp.int32)
    slot_neighbours = with_ends(jax.random.randint(streams_of[7], (DEVICES, SLOTS * KD), 0, CELLS), jax.random.fold_in(streams_of[7], 1), 0, CELLS - 1).astype(jnp.int32)
    encoder_in = bell_draw(streams_of[8], (3, EHID), 1.0, 4.0, (), jnp.float32)
    encoder_bias = bell_draw(streams_of[9], (EHID,), 1.0, 4.0, (), jnp.float32)
    encoder_out = bell_draw(streams_of[10], (EHID, C), EHID ** -0.5, 0.625)
    decoder_in = bell_draw(streams_of[11], (3, DHID), 1.0, 4.0, (), jnp.float32)
    decoder_bias = bell_draw(streams_of[12], (DHID,), 1.0, 4.0, (), jnp.float32)
    decoder_out = bell_draw(streams_of[13], (DHID, C), DHID ** -0.5, 0.375)
    skip_weight = bell_draw(streams_of[14], (C, C), C ** -0.5, 0.75)
    spectral_weight = bell_draw(streams_of[15], (2 * M, 2 * M, MZ, C, 2 * C), 1 ** -0.5, 6.0, ((1, 16), (2, 16)))
    readout_weight = bell_draw(streams_of[16], (C,), 0.5, 3.0, (), jnp.float32)
    return dict(point_features=point_features, positions=positions, targets=targets, routes=routes, live_counts=live_counts, cell_neighbours=cell_neighbours, cell_counts=cell_counts, slot_neighbours=slot_neighbours, encoder_in=encoder_in, encoder_bias=encoder_bias, encoder_out=encoder_out, decoder_in=decoder_in, decoder_bias=decoder_bias, decoder_out=decoder_out, skip_weight=skip_weight, spectral_weight=spectral_weight, readout_weight=readout_weight)


PRECISE = lax.Precision.HIGHEST
HALF_ROOT = 0.7071067811865476
GAUSS_NORM = 0.3989422804014327

def silu_of(values):
    return values / (1.0 + jnp.exp(-values))

def gelu_of(values):
    return 0.5 * values * (1.0 + lax.erf(values * HALF_ROOT))

def gelu_slope(values):
    return 0.5 * (1.0 + lax.erf(values * HALF_ROOT)) + values * jnp.exp(-0.5 * values * values) * GAUSS_NORM

def slot_ranks(target):
    ordering = jnp.argsort(target, stable=True).astype(jnp.int32)
    ordered = target[ordering]
    starts = jnp.searchsorted(ordered, ordered, side='left').astype(jnp.int32)
    within = jnp.arange(target.shape[0], dtype=jnp.int32) - starts
    return jnp.zeros(target.shape, jnp.int32).at[ordering].set(within)

def pack_sends(features, extras, target, counted, capacity, devices):
    living = jnp.arange(target.shape[0], dtype=jnp.int32) < counted
    target = jnp.where(living, target, devices).astype(jnp.int32)
    placement = target * capacity + slot_ranks(target)
    outgoing = jnp.zeros((devices * capacity, features.shape[1]), features.dtype).at[placement].set(features, mode='drop')
    side_data = jnp.zeros((devices * capacity, extras.shape[1]), extras.dtype).at[placement].set(extras, mode='drop')
    return (outgoing, side_data)

def cell_centres(rows_x, rows_y, depth_cells):
    position_ids = jnp.arange(rows_x * rows_y * depth_cells, dtype=jnp.int32)
    along_x = (position_ids // (rows_y * depth_cells)).astype(jnp.float32)
    along_y = (position_ids // depth_cells % rows_y).astype(jnp.float32)
    along_z = (position_ids % depth_cells).astype(jnp.float32)
    return jnp.stack([(along_x + 0.5) * (2.0 / rows_x) - 1.0, (along_y + 0.5) * (2.0 / rows_y) - 1.0, (along_z + 0.5) * (2.0 / depth_cells) - 1.0], 1)

def kernel_hidden(offset, weight_in, bias):
    summed = offset[:, 0:1] * weight_in[0] + offset[:, 1:2] * weight_in[1] + offset[:, 2:3] * weight_in[2] + bias
    return silu_of(summed).astype(jnp.bfloat16)

def encode_cells(slot_features, slot_places, neighbours, counted, centres, weight_in, bias, weight_out):
    per_cell = neighbours.shape[1]
    flat_ids = neighbours.reshape(-1)
    nearby = slot_features[flat_ids]
    offset = slot_places[flat_ids].astype(jnp.float32) - jnp.repeat(centres, per_cell, axis=0)
    hidden = kernel_hidden(offset, weight_in, bias)
    kernel = jnp.dot(hidden, weight_out, preferred_element_type=jnp.float32)
    summands = (kernel * nearby.astype(jnp.float32)).reshape(neighbours.shape[0], per_cell, -1)
    kept_mask = jnp.arange(per_cell, dtype=jnp.int32)[None, :] < counted[:, None]
    summed = lax.optimization_barrier(jnp.sum(jnp.where(kept_mask[:, :, None], summands, 0.0), axis=1))
    return (summed / counted[:, None].astype(jnp.float32)).astype(jnp.bfloat16)

def decode_slots(activated, slot_side, neighbours, centres, weight_in, bias, weight_out, readout_weight):
    per_slot = neighbours.shape[1]
    flat_ids = neighbours.reshape(-1)
    nearby = activated[flat_ids]
    places = slot_side[:, 0:3].astype(jnp.float32)
    offset = jnp.repeat(places, per_slot, axis=0) - centres[flat_ids]
    hidden = kernel_hidden(offset, weight_in, bias)
    kernel = jnp.dot(hidden, weight_out, preferred_element_type=jnp.float32)
    blended = lax.optimization_barrier(jnp.sum((kernel * nearby.astype(jnp.float32)).reshape(neighbours.shape[0], per_slot, -1), axis=1)) / per_slot
    living = slot_side[:, 4].astype(jnp.float32)
    predicted = living * lax.optimization_barrier(jnp.sum(blended * readout_weight, axis=1))
    residue = living * (predicted - slot_side[:, 3].astype(jnp.float32))
    shares = kernel * (jnp.repeat(residue, per_slot) / per_slot)[:, None] * readout_weight
    return (predicted, shares)

def apply_modes(x_real, x_imag, weights):
    channels = x_real.shape[3]
    w_real = weights[..., :channels].astype(jnp.float32)
    w_imag = weights[..., channels:].astype(jnp.float32)

    def mixing(left, right):
        return jnp.einsum('rpqc,rpqco->rpqo', left, right, precision=PRECISE)
    return (mixing(x_real, w_real) - mixing(x_imag, w_imag), mixing(x_real, w_imag) + mixing(x_imag, w_real))

def kept_index(length, modes):
    lowest = jnp.arange(modes, dtype=jnp.int32)
    return jnp.concatenate([lowest, lowest + (length - modes)])

def forward_modes(grid_field):
    scaling = 1.0 / math.sqrt(GX * GY * GZ)
    spectrum = jnp.fft.rfft(grid_field, axis=2)[:, :, :MZ]
    spectrum = jnp.fft.fft(spectrum, axis=1)[:, kept_index(GY, M)]
    spectrum = jnp.fft.fft(spectrum, axis=0)[kept_index(GX, M)] * scaling
    return (jnp.real(spectrum), jnp.imag(spectrum))

def inverse_modes(real_part, imag_part):
    row_ids = kept_index(GX, M)[:, None]
    col_ids = kept_index(GY, M)[None, :]
    shape_full = (GX, GY, GZ // 2 + 1, real_part.shape[3])
    full_real = jnp.zeros(shape_full, real_part.dtype).at[row_ids, col_ids, :MZ].set(real_part)
    full_imag = jnp.zeros(shape_full, imag_part.dtype).at[row_ids, col_ids, :MZ].set(imag_part)
    grid_field = jnp.fft.irfftn(lax.complex(full_real, full_imag), s=(GX, GY, GZ), axes=(0, 1, 2))
    return grid_field * math.sqrt(GX * GY * GZ)

def to_owners(grid_field):
    trailing = grid_field.shape[3]
    blocks = grid_field.reshape(N_PX, CX, N_PY, CY, GZ, trailing)
    blocks = jnp.transpose(blocks, (0, 2, 1, 3, 4, 5))
    return blocks.reshape(N_PX * N_PY, CX * CY * GZ, trailing)

def from_owners(blocks):
    trailing = blocks.shape[2]
    grid_field = blocks.reshape(N_PX, N_PY, CX, CY, GZ, trailing)
    grid_field = jnp.transpose(grid_field, (0, 2, 1, 3, 4, 5))
    return grid_field.reshape(GX, GY, GZ, trailing)

def reference(point_features, positions, targets, routes, live_counts, cell_neighbours, cell_counts, slot_neighbours, encoder_in, encoder_bias, encoder_out, decoder_in, decoder_bias, decoder_out, skip_weight, spectral_weight, readout_weight):
    devices = N_PX * N_PY
    extras = jnp.concatenate([positions, targets[:, None], jnp.ones((positions.shape[0], 1), jnp.bfloat16)], 1)
    feature_blocks = point_features.reshape(devices, PTS_DEV, C)
    extra_blocks = extras.reshape(devices, PTS_DEV, 5)
    route_blocks = routes.reshape(devices, PTS_DEV)

    def pack_one(features, side, target, counted):
        return pack_sends(features, side, target, counted, CAP, devices)
    outgoing, side_data = jax.vmap(pack_one)(feature_blocks, extra_blocks, route_blocks, live_counts)
    slot_features = jnp.transpose(outgoing.reshape(devices, devices, CAP, C), (1, 0, 2, 3)).reshape(devices, SLOTS, C)
    slot_extras = jnp.transpose(side_data.reshape(devices, devices, CAP, 5), (1, 0, 2, 3)).reshape(devices, SLOTS, 5)
    centres = cell_centres(CX, CY, GZ)
    owner_lists = to_owners(cell_neighbours.reshape(GX, GY, GZ * KE, 1).reshape(GX, GY, GZ, KE))
    owner_counts = to_owners(cell_counts[..., None])[..., 0]

    def encode_owner(inputs_now):
        features, side, lists, counted = inputs_now
        return encode_cells(features, side[:, 0:3], lists, counted, centres, encoder_in, encoder_bias, encoder_out)
    latent_blocks = lax.map(encode_owner, (slot_features, slot_extras, owner_lists, owner_counts))
    latent = from_owners(latent_blocks)
    x_real, x_imag = forward_modes(latent.astype(jnp.float32))
    v_real, v_imag = apply_modes(x_real, x_imag, spectral_weight)
    spectral_part = inverse_modes(v_real, v_imag)
    skip_part = jnp.dot(latent.reshape(-1, C), skip_weight, preferred_element_type=jnp.float32).reshape(GX, GY, GZ, C)
    before = spectral_part + skip_part
    activated = gelu_of(before).astype(jnp.bfloat16)
    owner_activated = to_owners(activated)
    owner_slot_lists = slot_neighbours.reshape(devices, SLOTS, KD)

    def decode_owner(inputs_now):
        cells_now, side, lists = inputs_now
        predicted, shares = decode_slots(cells_now, side, lists, centres, decoder_in, decoder_bias, decoder_out, readout_weight)
        grid_part = jax.ops.segment_sum(shares, lists.reshape(-1), num_segments=CELLS)
        return (predicted, grid_part)
    prediction, grad_blocks = lax.map(decode_owner, (owner_activated, slot_extras, owner_slot_lists))
    grid_grad = from_owners(grad_blocks)
    before_grad = grid_grad * gelu_slope(before)
    g_real, g_imag = forward_modes(before_grad)
    depth_ids = jnp.arange(MZ, dtype=jnp.int32)
    doubling = jnp.where(depth_ids == 0, 1.0, 2.0)[None, None, :, None]
    g_real = g_real * doubling
    g_imag = g_imag * doubling
    grad_real = x_real[..., :, None] * g_real[..., None, :] + x_imag[..., :, None] * g_imag[..., None, :]
    grad_imag = x_real[..., :, None] * g_imag[..., None, :] - x_imag[..., :, None] * g_real[..., None, :]
    return (prediction, jnp.concatenate([grad_real, grad_imag], 4))
```

```python
import functools
import math

import jax
import jax.numpy as jnp
import numpy as np
from jax import lax
from jax.experimental import pallas as pl
from jax.experimental.pallas import tpu as pltpu
from jax.sharding import PartitionSpec as P

MESH = pl.DeviceIdType.MESH
HALF_ROOT = 0.7071067811865476
GAUSS_NORM = 0.3989422804014327
BF = jnp.bfloat16
F32 = jnp.float32
GROUP = 16
CHANNELS = 64
COLUMNS = 32
DEPTH = 256
CAPACITY = 8
SLOT_TOTAL = 2048
POINTS = 1024
SCALING = 1.0 / math.sqrt(128 * 64 * 256)
VMEM_LIMIT = 56 * 1024 * 1024
ENC_CHUNK = 512
BLOCK_PAIRS = 1024


def frequencies():
    counted = np.arange(32)
    return np.where(counted < 16, counted, counted - 32)


def wave(length, positions, frequency):
    angles = 2.0 * np.pi * ((positions[:, None] * frequency[None, :]) % length) / length
    return np.cos(angles), np.sin(angles)


def bf16_of(array):
    return np.asarray(array, np.float32).astype(BF)


def kron_forward_y():
    cos, sin = wave(64, np.arange(64), frequencies())
    out = []
    for part in (cos, sin):
        w = part.reshape(16, 4, 16, 2)
        full = np.einsum("cjdp,ik->dpicjk", w, np.eye(8)).transpose(0, 1, 2, 3, 5, 4)
        out.append(full.reshape(256, 512))
    return bf16_of(np.concatenate(out))


def kron_forward_x():
    cos, sin = wave(128, np.arange(128), frequencies())
    out = []
    for part in (cos, sin):
        w = part.reshape(16, 8, 32)
        full = np.einsum("air,ps->rpasi", w, np.eye(2))
        out.append(full.reshape(64, 256))
    return bf16_of(np.concatenate(out))


def kron_inverse_x():
    cos, sin = wave(128, np.arange(128), frequencies())
    out = []
    for part in (cos, sin):
        w = part.reshape(16, 8, 32)
        full = np.einsum("air,ps->apirs", w, np.eye(2))
        out.append(full.reshape(256, 64))
    return bf16_of(np.concatenate(out))


def kron_inverse_y():
    cos, sin = wave(64, np.arange(64), frequencies())
    out = []
    for part in (cos, sin):
        w = part.reshape(16, 4, 16, 2)
        full = np.einsum("cjdp,ik->cijdpk", w, np.eye(8))
        out.append(full.reshape(512, 256))
    return bf16_of(np.concatenate(out))


def depth_waves():
    cos, sin = wave(256, np.arange(16), np.arange(256))
    return bf16_of(np.concatenate([cos, -sin]))


def entry_sums():
    return bf16_of(np.arange(2048)[:, None] // 8 == np.arange(256)[None, :])


def pair_sums():
    return bf16_of(np.arange(1024)[:, None] // 4 == np.arange(256)[None, :])


def nt(left, right):
    return lax.dot_general(left, right, (((1,), (1,)), ((), ())), preferred_element_type=F32)


def mm(left, right):
    return jnp.dot(left, right, preferred_element_type=F32)


def identity(n):
    rows = lax.broadcasted_iota(jnp.int32, (n, n), 0)
    lanes = lax.broadcasted_iota(jnp.int32, (n, n), 1)
    return jnp.where(rows == lanes, 1.0, 0.0).astype(BF)


def lane_sign(shape):
    lanes = lax.broadcasted_iota(jnp.int32, shape, 1)
    return jnp.where(lanes < CHANNELS, 1.0, -1.0)


def turned(cos_part, sin_part, direction):
    swapped = pltpu.roll(sin_part, CHANNELS, 1)
    return cos_part + swapped * (lane_sign(swapped.shape) * direction)


def greet():
    a, c = lax.axis_index("px"), lax.axis_index("py")
    barrier = pltpu.get_barrier_semaphore()

    def greeting(d, carry):
        pl.semaphore_signal(barrier, inc=1, device_id=((a + d) & 15, c), device_id_type=MESH)
        pl.semaphore_signal(barrier, inc=1, device_id=(a, (c + d) & 15), device_id_type=MESH)
        return carry

    lax.fori_loop(1, GROUP, greeting, 0)
    pl.semaphore_wait(barrier, 2 * (GROUP - 1))


def copy_to(axis, d, send, recv, send_sem, recv_sem):
    a, c = lax.axis_index("px"), lax.axis_index("py")
    me = a if axis == "px" else c
    peer = (me + d) & 15
    return pltpu.make_async_remote_copy(
        src_ref=send.at[peer],
        dst_ref=recv.at[me],
        send_sem=send_sem.at[d],
        recv_sem=recv_sem.at[me],
        device_id=(peer, c) if axis == "px" else (a, peer),
        device_id_type=MESH,
    )


def finish(axis, send, recv, send_sem, recv_sem):
    me = lax.axis_index(axis)
    recv[me] = send[me]

    def arrival(d, carry):
        copy_to(axis, d, send, recv, send_sem, recv_sem).wait_send()
        source = (me - d) & 15
        pltpu.make_async_remote_copy(
            src_ref=send.at[source],
            dst_ref=recv.at[source],
            send_sem=send_sem.at[d],
            recv_sem=recv_sem.at[source],
            device_id=(lax.axis_index("px"), lax.axis_index("py")),
            device_id_type=MESH,
        ).wait_recv()
        return carry

    lax.fori_loop(1, GROUP, arrival, 0)


def start_all(axis, send, recv, send_sem, recv_sem):
    def start(d, carry):
        copy_to(axis, d, send, recv, send_sem, recv_sem).start()
        return carry

    lax.fori_loop(1, GROUP, start, 0)


def exchange(axis, send, recv, send_sem, recv_sem):
    start_all(axis, send, recv, send_sem, recv_sem)
    finish(axis, send, recv, send_sem, recv_sem)


def sems():
    return [pltpu.SemaphoreType.DMA((GROUP,)), pltpu.SemaphoreType.DMA((GROUP,))]


def vmem(shape, kind):
    return pltpu.VMEM(shape, kind)


def whole():
    return pl.BlockSpec(memory_space=pltpu.VMEM)


def send_points_kernel(
    x_ref, route_ref, live_ref, out_ref,
    send1, recv1, send2, recv2, regroup, slot_ref, ss1, rs1, ss2, rs2,
):
    greet()
    live = live_ref[0]
    lanes = lax.broadcasted_iota(jnp.int32, (1, POINTS), 1)
    target = jnp.where(lanes < live, route_ref[...], 256)
    owners = lax.broadcasted_iota(jnp.int32, (256, POINTS), 0)
    named = jnp.where(owners == target, 1.0, 0.0)
    named_bf = named.astype(BF)
    rank = jnp.zeros((1, POINTS), F32)
    earlier = jnp.where(
        lax.broadcasted_iota(jnp.int32, (POINTS, POINTS), 0)
        < lax.broadcasted_iota(jnp.int32, (POINTS, POINTS), 1),
        1.0,
        0.0,
    ).astype(BF)
    counted = mm(named_bf, earlier)
    rank = jnp.sum(named * counted, axis=0, keepdims=True)
    slot_ref[...] = jnp.where(
        target < 256, target * CAPACITY + rank.astype(jnp.int32), -1
    )
    a = lax.axis_index("px")

    def pack(d, carry):
        peer = (a + d) & 15
        rows = lax.broadcasted_iota(jnp.int32, (128, POINTS), 0) + peer * 128
        hot = jnp.where(rows == slot_ref[...], 1.0, 0.0).astype(BF)
        send1[peer] = mm(hot, x_ref[...]).astype(BF)

        @pl.when(d > 0)
        def _():
            copy_to("px", d, send1, recv1, ss1, rs1).start()

        return carry

    lax.fori_loop(0, GROUP, pack, 0)
    finish("px", send1, recv1, ss1, rs1)
    for source in range(GROUP):
        regroup[source] = recv1[source].astype(F32).reshape(GROUP, CAPACITY, 128)
    for dest in range(GROUP):
        send2[dest] = regroup[:, dest].reshape(128, 128).astype(BF)
    exchange("py", send2, recv2, ss2, rs2)
    for source in range(GROUP):
        regroup[source] = recv2[source].astype(F32).reshape(GROUP, CAPACITY, 128)
    for source in range(GROUP):
        out_ref[source] = regroup[:, source].reshape(128, 128).astype(BF)


def send_points(x, route, live):
    block = (GROUP, 128, 128)
    return pl.pallas_call(
        send_points_kernel,
        out_shape=jax.ShapeDtypeStruct(block, BF),
        in_specs=[whole(), whole(), pl.BlockSpec(memory_space=pltpu.SMEM)],
        out_specs=whole(),
        scratch_shapes=[
            vmem(block, BF), vmem(block, BF), vmem(block, BF), vmem(block, BF),
            vmem((GROUP, GROUP, CAPACITY, 128), F32),
            vmem((1, POINTS), jnp.int32),
        ] + sems() + sems(),
        compiler_params=pltpu.CompilerParams(
            collective_id=0, has_side_effects=True, vmem_limit_bytes=VMEM_LIMIT
        ),
        name="send_points",
    )(x, route, live)


def encode_kernel(
    tab_ref, nbr_ref, cnt_ref, w1_ref, wo_ref, sums_ref, waves_ref,
    lat_ref, z_ref, extra_ref,
    table, pos_rows, high_ref, share_ref, prod, z_rows,
):
    eye = identity(128)
    picks = lax.broadcasted_iota(jnp.int32, (8, 128), 0)
    lanes8 = lax.broadcasted_iota(jnp.int32, (8, 128), 1)
    wanted = jnp.where(picks < 3, picks + 64, jnp.where(picks < 6, picks + 61, picks + 61))
    chooser = jnp.where(lanes8 == wanted, 1.0, 0.0).astype(BF)
    pos_rows[...] = jnp.zeros(pos_rows.shape, F32)
    for h in range(8):
        rows = tab_ref[h * 256 : (h + 1) * 256, :]
        turned_rows = nt(eye, rows)
        table[h * 64 : (h + 1) * 64, :] = turned_rows[0:64].astype(BF)
        extra = nt(chooser, rows)
        extra_ref[h] = extra
        for d in range(3):
            pos_rows[d * 8 + h : d * 8 + h + 1, :] = extra[d : d + 1]
    table[512:544, :] = pos_rows[...].astype(BF)
    counts = cnt_ref[...].astype(F32)
    share_ref[...] = 1.0 / counts
    spread = nt(counts.astype(BF), sums_ref[...])
    places = (lax.broadcasted_iota(jnp.int32, (COLUMNS, 2048), 1) & 7).astype(F32)
    high_ref[...] = jnp.where(places < spread, nbr_ref[...] >> 8, 8)
    n = ENC_CHUNK

    def column(ij, carry):
        cx = ((ij >> 2).astype(F32) + 0.5) * 0.25 - 1.0
        cy = ((ij & 3).astype(F32) + 0.5) * 0.5 - 1.0

        def chunk(step, inner):
            off = pl.multiple_of(step * n, n)
            low = nbr_ref[pl.ds(ij, 1), pl.ds(off, n)] & 255
            high = high_ref[pl.ds(ij, 1), pl.ds(off, n)]
            hot = jnp.where(
                lax.broadcasted_iota(jnp.int32, (256, n), 0) == low, 1.0, 0.0
            ).astype(BF)
            found = mm(table[...], hot)
            high8 = jnp.broadcast_to(high, (8, n))
            near = jnp.zeros((8, 8, n), F32)
            for h in range(8):
                part = found[h * 64 : (h + 1) * 64].reshape(8, 8, n)
                near = jnp.where((high8 == h)[None], part, near)
            sub = lax.broadcasted_iota(jnp.int32, (8, n), 0)
            place = found[512:536].reshape(3, 8, n)
            place = jnp.where((high8 == sub)[None], place, 0.0).reshape(24, n)
            depth = ((lax.broadcasted_iota(jnp.int32, (8, n), 1) + off) >> 3).astype(F32)
            cz = (depth + 0.5) * (2.0 / DEPTH) - 1.0
            part3 = jnp.where(sub >= 3, sub - 3, sub)
            centre = jnp.where(
                sub >= 6, 1.0, jnp.where(part3 == 0, cx, jnp.where(part3 == 1, cy, cz))
            )
            stacked = jnp.concatenate([place, place, centre], 0).astype(BF)
            half = mm(w1_ref[...], stacked)
            hidden = (half + half * jnp.tanh(half)).astype(BF)
            kernel = mm(wo_ref[...], hidden)
            prod[:, pl.ds(off, n)] = (kernel * near.reshape(64, n)).astype(BF)
            return inner

        lax.fori_loop(0, 2048 // n, chunk, 0)
        latent = mm(prod[...], sums_ref[...]) * share_ref[pl.ds(ij, 1), :]
        latent = latent.astype(BF)
        lat_ref[pl.ds(pl.multiple_of(ij * 64, 64), 64), :] = latent
        both = nt(waves_ref[...], latent)
        z_rows[:, pl.ds(ij, 1), :] = jnp.concatenate([both[0:16], both[16:32]], 1).reshape(
            16, 1, 128
        )
        return carry

    lax.fori_loop(0, COLUMNS, column, 0)
    z_ref[...] = z_rows[...].astype(BF)


def encode(tab, nbr, cnt, w1, wo):
    return pl.pallas_call(
        encode_kernel,
        out_shape=(
            jax.ShapeDtypeStruct((COLUMNS * 64, DEPTH), BF),
            jax.ShapeDtypeStruct((GROUP, COLUMNS, 128), BF),
            jax.ShapeDtypeStruct((8, 8, 256), F32),
        ),
        in_specs=[whole()] * 7,
        out_specs=(whole(),) * 3,
        scratch_shapes=[
            vmem((544, 256), BF),
            vmem((32, 256), F32),
            vmem((COLUMNS, 2048), jnp.int32),
            vmem((COLUMNS, DEPTH), F32),
            vmem((64, 2048), BF),
            vmem((GROUP, COLUMNS, 128), F32),
        ],
        compiler_params=pltpu.CompilerParams(vmem_limit_bytes=VMEM_LIMIT),
        name="encode",
    )(tab, nbr, cnt, w1, wo, jnp.asarray(entry_sums()), jnp.asarray(depth_waves()))


def forward_tail(z_ref, ky_ref, kx_ref, recv_a, send_b, recv_b, s1, r1, s2, r2):
    exchange("py", z_ref, recv_a, s1, r1)
    u = mm(ky_ref[...], recv_a[...].reshape(512, 128))
    send_b[...] = turned(u[:256], u[256:], 1.0).astype(BF).reshape(GROUP, 16, 128)
    exchange("px", send_b, recv_b, s2, r2)
    u = mm(kx_ref[...], recv_b[...].reshape(256, 128))
    return turned(u[:64], u[64:], 1.0) * SCALING


def own_doubling():
    return jnp.where(lax.axis_index("py") == 0, 1.0, 2.0)


def mixed(modes, weight_ref):
    lanes = lax.broadcasted_iota(jnp.int32, (64, 128), 1)
    swapped = pltpu.roll(modes, CHANNELS, 1)
    real2 = jnp.where(lanes < CHANNELS, modes, swapped)
    imag2 = jnp.where(lanes < CHANNELS, swapped, modes)
    rows4 = lax.broadcasted_iota(jnp.int32, (64, 256), 0) & 3
    keep = (lax.broadcasted_iota(jnp.int32, (64, 256), 1) >> 6) == rows4
    real4 = jnp.where(keep, jnp.concatenate([real2, real2], 1), 0.0)
    imag4 = jnp.where(keep, jnp.concatenate([imag2, imag2], 1), 0.0)
    first = (lax.broadcasted_iota(jnp.int32, (16, 128), 0) & 7) < 4
    out = []
    for h in range(8):
        left = jnp.concatenate([real4[8 * h : 8 * h + 8], imag4[8 * h : 8 * h + 8]], 0)
        left = left.astype(BF)
        lower = mm(left, weight_ref[8 * h : 8 * h + 4].reshape(256, 128))
        upper = mm(left, weight_ref[8 * h + 4 : 8 * h + 8].reshape(256, 128))
        both = jnp.where(first, lower, upper)
        out.append(turned(both[0:8], both[8:16], -1.0))
    return jnp.concatenate(out, 0)


def fourier_kernel(
    z_ref, weight_ref, ky_ref, kx_ref, kxi_ref, kyi_ref, modes_ref, back_ref,
    recv_a, send_b, recv_b, send_c, recv_c, send_d, recv_d,
    s1, r1, s2, r2, s3, r3, s4, r4,
):
    greet()
    modes = forward_tail(z_ref, ky_ref, kx_ref, recv_a, send_b, recv_b, s1, r1, s2, r2)
    modes_ref[...] = modes
    v = mixed(modes, weight_ref) * (own_doubling() * SCALING)
    u = mm(kxi_ref[...], v.astype(BF))
    send_c[...] = turned(u[:256], u[256:], -1.0).astype(BF).reshape(GROUP, 16, 128)
    exchange("px", send_c, recv_c, s3, r3)
    u = mm(kyi_ref[...], recv_c[...].reshape(256, 128))
    send_d[...] = turned(u[:512], u[512:], -1.0).astype(BF).reshape(GROUP, COLUMNS, 128)
    exchange("py", send_d, recv_d, s4, r4)
    back_ref[...] = recv_d[...]


def fourier(z, weight):
    wide, narrow = (GROUP, COLUMNS, 128), (GROUP, 16, 128)
    return pl.pallas_call(
        fourier_kernel,
        out_shape=(
            jax.ShapeDtypeStruct((64, 128), F32),
            jax.ShapeDtypeStruct(wide, BF),
        ),
        in_specs=[whole()] * 6,
        out_specs=(whole(),) * 2,
        scratch_shapes=[
            vmem(wide, BF), vmem(narrow, BF), vmem(narrow, BF), vmem(narrow, BF),
            vmem(narrow, BF), vmem(wide, BF), vmem(wide, BF),
        ] + sems() * 4,
        compiler_params=pltpu.CompilerParams(
            collective_id=1, has_side_effects=True, vmem_limit_bytes=VMEM_LIMIT
        ),
        name="fourier",
    )(
        z, weight, jnp.asarray(kron_forward_y()), jnp.asarray(kron_forward_x()),
        jnp.asarray(kron_inverse_x()), jnp.asarray(kron_inverse_y()),
    )


def gradient_modes_kernel(
    z_ref, ky_ref, kx_ref, modes_ref, recv_a, send_b, recv_b, s1, r1, s2, r2
):
    greet()
    modes = forward_tail(z_ref, ky_ref, kx_ref, recv_a, send_b, recv_b, s1, r1, s2, r2)
    modes_ref[...] = modes * own_doubling()


def gradient_modes(z):
    wide, narrow = (GROUP, COLUMNS, 128), (GROUP, 16, 128)
    return pl.pallas_call(
        gradient_modes_kernel,
        out_shape=jax.ShapeDtypeStruct((64, 128), F32),
        in_specs=[whole()] * 3,
        out_specs=whole(),
        scratch_shapes=[vmem(wide, BF), vmem(narrow, BF), vmem(narrow, BF)] + sems() * 2,
        compiler_params=pltpu.CompilerParams(
            collective_id=2, has_side_effects=True, vmem_limit_bytes=VMEM_LIMIT
        ),
        name="gradient_modes",
    )(z, jnp.asarray(kron_forward_y()), jnp.asarray(kron_forward_x()))


def split_rows(row, parts):
    sub = lax.broadcasted_iota(jnp.int32, (8, row.shape[1]), 0)
    out = jnp.zeros((8, row.shape[1]), F32)
    rest = row
    for part in range(parts):
        rounded = rest.astype(BF).astype(F32)
        out = jnp.where(sub == part, rounded, out)
        rest = rest - rounded
    return out.astype(BF)


def decode_kernel(
    lat_ref, back_ref, extra_ref, list_ref, w1_ref, wo_ref, skip_ref, read_ref,
    pairs_ref, waves_ref, pred_ref, z_ref,
    back_t, basis, latent_g, kern, total,
):
    flipped = nt(identity(128), back_ref[...].reshape(512, 128))
    back_t[...] = jnp.concatenate([flipped[0:64], flipped[64:128]], 1).astype(BF)
    total[...] = jnp.zeros(total.shape, F32)
    n = 256

    def block(h, carry):
        extras = extra_ref[h]
        expanded = nt(extras.astype(BF), pairs_ref[...])

        for step in range(BLOCK_PAIRS // n):
            off = step * n
            cells = list_ref[:, pl.ds(pl.multiple_of(h * BLOCK_PAIRS + off, n), n)]
            low, column = cells & 255, cells >> 8
            hot = jnp.where(
                lax.broadcasted_iota(jnp.int32, (256, n), 0) == low, 1.0, 0.0
            ).astype(BF)
            found = mm(lat_ref[...], hot)
            column8 = jnp.broadcast_to(column, (8, n))
            near = jnp.zeros((8, 8, n), F32)
            for k in range(COLUMNS):
                part = found[k * 64 : (k + 1) * 64].reshape(8, 8, n)
                near = jnp.where((column8 == k)[None], part, near)
            latent_g[:, off : off + n] = near.reshape(64, n).astype(BF)
            tw = mm(waves_ref[...], hot)
            match = lax.broadcasted_iota(jnp.int32, (COLUMNS, n), 0) == column
            for q in range(32):
                basis[q * 32 : (q + 1) * 32, off : off + n] = jnp.where(
                    match, tw[q : q + 1], 0.0
                ).astype(BF)
            sub = lax.broadcasted_iota(jnp.int32, (8, n), 0)
            cx = ((column >> 2).astype(F32) + 0.5) * 0.25 - 1.0
            cy = ((column & 3).astype(F32) + 0.5) * 0.5 - 1.0
            cz = (low.astype(F32) + 0.5) * (2.0 / DEPTH) - 1.0
            part3 = jnp.where(sub >= 3, sub - 3, sub)
            centre = jnp.where(
                sub >= 6, 1.0, jnp.where(part3 == 0, cx, jnp.where(part3 == 1, cy, cz))
            )
            stacked = jnp.concatenate([expanded[:, off : off + n], centre], 0).astype(BF)
            half = mm(w1_ref[...], stacked)
            hidden = (half + half * jnp.tanh(half)).astype(BF)
            kern[:, off : off + n] = mm(wo_ref[...], hidden)

        before = mm(back_t[...], basis[...]) + mm(skip_ref[...], latent_g[...])
        phi = 0.5 * (1.0 + lax.erf(before * HALF_ROOT))
        slope = phi + before * jnp.exp(-0.5 * before * before) * GAUSS_NORM
        weighed = kern[...] * read_ref[...]
        dots = jnp.sum(weighed * (before * phi), axis=0, keepdims=True)
        summed = jnp.sum(mm(split_rows(dots, 3), pairs_ref[...]), axis=0, keepdims=True)
        target, living = extras[6:7], extras[7:8]
        pred = living * (summed * 0.25)
        pred_ref[:, pl.ds(pl.multiple_of(h * 256, 256), 256)] = pred
        residue = living * (pred - target) * 0.25
        spread = jnp.sum(nt(split_rows(residue, 2), pairs_ref[...]), axis=0, keepdims=True)
        shares = (weighed * slope * spread).astype(BF)
        total[...] += nt(shares, basis[...])
        return carry

    lax.fori_loop(0, SLOT_TOTAL * 4 // BLOCK_PAIRS, block, 0)
    out = jnp.concatenate([total[:, 0:512].T, total[:, 512:1024].T], 1)
    z_ref[...] = out.astype(BF).reshape(GROUP, COLUMNS, 128)


def decode(lat, back, extra, lists, w1, wo, skip, readout):
    return pl.pallas_call(
        decode_kernel,
        out_shape=(
            jax.ShapeDtypeStruct((1, SLOT_TOTAL), F32),
            jax.ShapeDtypeStruct((GROUP, COLUMNS, 128), BF),
        ),
        in_specs=[whole()] * 10,
        out_specs=(whole(),) * 2,
        scratch_shapes=[
            vmem((64, 1024), BF),
            vmem((1024, BLOCK_PAIRS), BF),
            vmem((64, BLOCK_PAIRS), BF),
            vmem((64, BLOCK_PAIRS), F32),
            vmem((64, 1024), F32),
        ],
        compiler_params=pltpu.CompilerParams(vmem_limit_bytes=VMEM_LIMIT),
        name="decode",
    )(
        lat, back, extra, lists, w1, wo, skip, readout,
        jnp.asarray(pair_sums()), jnp.asarray(depth_waves()),
    )


def outer_kernel(modes_ref, grad_ref, out_ref):
    modes_t = modes_ref[...].T
    grads = grad_ref[...]
    swapped = pltpu.roll(grads, CHANNELS, 1) * lane_sign(grads.shape)
    for m in range(8):
        out_ref[m] = (
            modes_t[0:64, m : m + 1] * grads[m : m + 1]
            + modes_t[64:128, m : m + 1] * swapped[m : m + 1]
        )


def outer(modes, grads):
    return pl.pallas_call(
        outer_kernel,
        grid=(8,),
        out_shape=jax.ShapeDtypeStruct((64, 64, 128), F32),
        in_specs=[pl.BlockSpec((8, 128), lambda i: (i, 0))] * 2,
        out_specs=pl.BlockSpec((8, 64, 128), lambda i: (i, 0, 0)),
        compiler_params=pltpu.CompilerParams(vmem_limit_bytes=VMEM_LIMIT),
        name="outer",
    )(modes, grads)


def two_parts(values):
    high = lax.reduce_precision(values, 8, 7)
    return high.astype(BF), (values - high).astype(BF)


def encoder_first(weight, bias):
    high, low = two_parts(weight * 0.5)
    bias_high, bias_low = two_parts(bias * 0.5)
    return jnp.concatenate(
        [
            jnp.repeat(high, 8, axis=0), jnp.repeat(low, 8, axis=0),
            -high, -low, bias_high[None], bias_low[None],
        ],
        0,
    ).T


def decoder_first(weight, bias):
    high, low = two_parts(weight * 0.5)
    bias_high, bias_low = two_parts(bias * 0.5)
    return jnp.concatenate(
        [
            high, low, jnp.zeros((2, weight.shape[1]), BF),
            -high, -low, bias_high[None], bias_low[None],
        ],
        0,
    ).T


def body(
    point_features, positions, targets, routes, live_counts, cell_neighbours, cell_counts,
    slot_neighbours, encoder_in, encoder_bias, encoder_out, decoder_in, decoder_bias,
    decoder_out, skip_weight, spectral_weight, readout_weight,
):
    x = jnp.concatenate(
        [
            point_features, positions, targets[:, None],
            jnp.ones((POINTS, 1), BF), jnp.zeros((POINTS, 59), BF),
        ],
        1,
    )
    tab = send_points(x, routes.reshape(1, POINTS), live_counts)
    lat, z, extra = encode(
        tab.reshape(SLOT_TOTAL, 128),
        cell_neighbours.reshape(COLUMNS, 2048),
        cell_counts.reshape(COLUMNS, DEPTH),
        encoder_first(encoder_in, encoder_bias),
        encoder_out.T,
    )
    modes, back = fourier(z, spectral_weight.reshape(64, 64, 128))
    pred, grad_z = decode(
        lat, back, extra, slot_neighbours,
        decoder_first(decoder_in, decoder_bias), decoder_out.T, skip_weight.T,
        readout_weight[:, None],
    )
    grads = gradient_modes(grad_z)
    return pred, outer(modes, grads).reshape(32, 2, 1, 64, 128)


def solution(mesh):
    in_specs = (
        P(("px", "py"), None), P(("px", "py"), None), P(("px", "py")), P(("px", "py"), None),
        P(("px", "py")), P("px", "py", None), P("px", "py", None), P(("px", "py"), None),
        P(), P(), P(), P(), P(), P(), P(),
        P(None, "px", "py", None, None), P(),
    )
    out_specs = (P(("px", "py"), None), P(None, "px", "py", None, None))
    return jax.shard_map(body, mesh=mesh, in_specs=in_specs, out_specs=out_specs, check_vma=False)
```

```python
import math
import types

import jax
import jax.numpy as jnp
import numpy as np
from jax import lax
from jax.experimental import pallas as pl
from jax.experimental.pallas import tpu as pltpu
from jax.sharding import PartitionSpec as P

MESH = pl.DeviceIdType.MESH
HALF_ROOT = 0.7071067811865476
GAUSS_NORM = 0.3989422804014327
BF = jnp.bfloat16
F32 = jnp.float32
GROUP = 16
CHANNELS = 64
COLUMNS = 32
DEPTH = 256
CAPACITY = 8
SLOT_TOTAL = 2048
POINTS = 1024
SCALING = 1.0 / math.sqrt(128 * 64 * 256)
VMEM_LIMIT = 60 * 1024 * 1024
ENC_COLUMNS = 2
PREP = 512
POST = 2048


def frequencies():
    counted = np.arange(32)
    return np.where(counted < 16, counted, counted - 32)


def wave(length, positions, frequency):
    angles = 2.0 * np.pi * ((positions[:, None] * frequency[None, :]) % length) / length
    return np.cos(angles), np.sin(angles)


def bf16_of(array):
    return np.asarray(array, np.float32).astype(BF)


def kron_forward_y():
    cos, sin = wave(64, np.arange(64), frequencies())
    out = []
    for part in (cos, sin):
        w = part.reshape(16, 4, 16, 2)
        full = np.einsum("cjdp,ik->dpicjk", w, np.eye(8)).transpose(0, 1, 2, 3, 5, 4)
        out.append(full.reshape(256, 512))
    return bf16_of(np.concatenate(out))


def kron_forward_x():
    cos, sin = wave(128, np.arange(128), frequencies())
    out = []
    for part in (cos, sin):
        w = part.reshape(16, 8, 32)
        full = np.einsum("air,ps->rpasi", w, np.eye(2))
        out.append(full.reshape(64, 256))
    return bf16_of(np.concatenate(out))


def kron_inverse_x():
    cos, sin = wave(128, np.arange(128), frequencies())
    out = []
    for part in (cos, sin):
        w = part.reshape(16, 8, 32)
        full = np.einsum("air,ps->apirs", w, np.eye(2))
        out.append(full.reshape(256, 64))
    return bf16_of(np.concatenate(out))


def kron_inverse_y():
    cos, sin = wave(64, np.arange(64), frequencies())
    out = []
    for part in (cos, sin):
        w = part.reshape(16, 4, 16, 2)
        full = np.einsum("cjdp,ik->cijdpk", w, np.eye(8))
        out.append(full.reshape(512, 256))
    return bf16_of(np.concatenate(out))


def depth_waves():
    cos, sin = wave(256, np.arange(16), np.arange(256))
    return bf16_of(np.concatenate([cos, -sin]))


def entry_sums():
    return bf16_of(np.arange(2048)[:, None] // 8 == np.arange(256)[None, :])


def pair_sums():
    return bf16_of(np.arange(1024)[:, None] // 4 == np.arange(256)[None, :])


def nt(left, right):
    return lax.dot_general(left, right, (((1,), (1,)), ((), ())), preferred_element_type=F32)


def mm(left, right):
    return jnp.dot(left, right, preferred_element_type=F32)


def identity(n):
    rows = lax.broadcasted_iota(jnp.int32, (n, n), 0)
    lanes = lax.broadcasted_iota(jnp.int32, (n, n), 1)
    return jnp.where(rows == lanes, 1.0, 0.0).astype(BF)


def lane_sign(shape):
    lanes = lax.broadcasted_iota(jnp.int32, shape, 1)
    return jnp.where(lanes < CHANNELS, 1.0, -1.0)


def turned(cos_part, sin_part, direction):
    swapped = pltpu.roll(sin_part, CHANNELS, 1)
    return cos_part + swapped * (lane_sign(swapped.shape) * direction)


def others():
    a, c = lax.axis_index("px"), lax.axis_index("py")
    return a, c


def greet():
    a, c = others()
    barrier = pltpu.get_barrier_semaphore()

    def greeting(d, carry):
        pl.semaphore_signal(barrier, inc=1, device_id=((a + d) & 15, c), device_id_type=MESH)
        pl.semaphore_signal(barrier, inc=1, device_id=(a, (c + d) & 15), device_id_type=MESH)
        return carry

    lax.fori_loop(1, GROUP, greeting, 0)


def greeted():
    pl.semaphore_wait(pltpu.get_barrier_semaphore(), 2 * (GROUP - 1))


def copy_to(axis, d, send, recv, send_sem, recv_sem):
    a, c = others()
    me = a if axis == "px" else c
    peer = (me + d) & 15
    return pltpu.make_async_remote_copy(
        src_ref=send.at[peer],
        dst_ref=recv.at[me],
        send_sem=send_sem.at[d],
        recv_sem=recv_sem.at[me],
        device_id=(peer, c) if axis == "px" else (a, peer),
        device_id_type=MESH,
    )


def start_all(axis, send, recv, send_sem, recv_sem):
    def start(d, carry):
        copy_to(axis, d, send, recv, send_sem, recv_sem).start()
        return carry

    lax.fori_loop(1, GROUP, start, 0)


def finish(axis, send, recv, send_sem, recv_sem):
    me = lax.axis_index(axis)
    recv[me] = send[me]

    def arrival(d, carry):
        copy_to(axis, d, send, recv, send_sem, recv_sem).wait_send()
        source = (me - d) & 15
        pltpu.make_async_remote_copy(
            src_ref=send.at[source],
            dst_ref=recv.at[source],
            send_sem=send_sem.at[d],
            recv_sem=recv_sem.at[source],
            device_id=others(),
            device_id_type=MESH,
        ).wait_recv()
        return carry

    lax.fori_loop(1, GROUP, arrival, 0)


def exchange(axis, send, recv, pair, meanwhile=None):
    start_all(axis, send, recv, *pair)
    if meanwhile is not None:
        meanwhile()
    finish(axis, send, recv, *pair)


def send_points(r):
    greet()
    live = r.live[0]
    lanes = lax.broadcasted_iota(jnp.int32, (1, POINTS), 1)
    target = jnp.where(lanes < live, r.route[...], 256)
    owners = lax.broadcasted_iota(jnp.int32, (256, POINTS), 0)
    named = jnp.where(owners == target, 1.0, 0.0)
    earlier = jnp.where(
        lax.broadcasted_iota(jnp.int32, (POINTS, POINTS), 0)
        < lax.broadcasted_iota(jnp.int32, (POINTS, POINTS), 1),
        1.0,
        0.0,
    ).astype(BF)
    counted = mm(named.astype(BF), earlier)
    rank = jnp.sum(named * counted, axis=0, keepdims=True)
    r.slot[...] = jnp.where(target < 256, target * CAPACITY + rank.astype(jnp.int32), -1)
    greeted()
    a = lax.axis_index("px")

    def pack(d, carry):
        peer = (a + d) & 15
        rows = lax.broadcasted_iota(jnp.int32, (128, POINTS), 0) + peer * 128
        hot = jnp.where(rows == r.slot[...], 1.0, 0.0).astype(BF)
        r.send1[peer] = mm(hot, r.x[...]).astype(BF)

        @pl.when(d > 0)
        def _():
            copy_to("px", d, r.send1, r.recv1, r.s1, r.r1).start()

        return carry

    lax.fori_loop(0, GROUP, pack, 0)
    finish("px", r.send1, r.recv1, r.s1, r.r1)
    for source in range(GROUP):
        r.regroup[source] = r.recv1[source].astype(F32).reshape(GROUP, CAPACITY, 128)
    for dest in range(GROUP):
        r.send2[dest] = r.regroup[:, dest].reshape(128, 128).astype(BF)
    exchange("py", r.send2, r.recv2, (r.s2, r.r2))
    for source in range(GROUP):
        r.regroup[source] = r.recv2[source].astype(F32).reshape(GROUP, CAPACITY, 128)
    for source in range(GROUP):
        r.tab[source * 128 : (source + 1) * 128, :] = (
            r.regroup[:, source].reshape(128, 128).astype(BF)
        )


def first_layer_centres(ij, depth, sub):
    cx = ((ij >> 2).astype(F32) + 0.5) * 0.25 - 1.0
    cy = ((ij & 3).astype(F32) + 0.5) * 0.5 - 1.0
    cz = (depth.astype(F32) + 0.5) * (2.0 / DEPTH) - 1.0
    part3 = jnp.where(sub >= 3, sub - 3, sub)
    return jnp.where(
        sub >= 6, 1.0, jnp.where(part3 == 0, cx, jnp.where(part3 == 1, cy, cz))
    )


def encode(r):
    eye = identity(128)
    picks = lax.broadcasted_iota(jnp.int32, (8, 128), 0)
    lanes8 = lax.broadcasted_iota(jnp.int32, (8, 128), 1)
    wanted = jnp.where(picks < 3, picks + 64, picks + 61)
    chooser = jnp.where(lanes8 == wanted, 1.0, 0.0).astype(BF)
    r.pos_rows[...] = jnp.zeros(r.pos_rows.shape, F32)
    for h in range(8):
        rows = r.tab[h * 256 : (h + 1) * 256, :]
        r.table[h * 64 : (h + 1) * 64, :] = nt(eye, rows)[0:64].astype(BF)
        extra = nt(chooser, rows)
        r.extra[h] = extra
        r.target[h : h + 1, :] = extra[6:7]
        r.living[h : h + 1, :] = extra[7:8]
        for d in range(3):
            r.pos_rows[d * 8 + h : d * 8 + h + 1, :] = extra[d : d + 1]
    r.table[512:544, :] = r.pos_rows[...].astype(BF)
    counts = r.cnt[...].astype(F32)
    steps = COLUMNS // ENC_COLUMNS
    places = (lax.broadcasted_iota(jnp.int32, (steps, 2048), 1) & 7).astype(F32)
    for k in range(ENC_COLUMNS):
        spread = nt(counts[:, k * DEPTH : (k + 1) * DEPTH].astype(BF), r.sums[...])
        ids = r.nbr[:, k * 2048 : (k + 1) * 2048]
        r.high[:, k * 2048 : (k + 1) * 2048] = jnp.where(places < spread, ids >> 8, 8)
    n = 2048 * ENC_COLUMNS

    def columns(step, carry):
        low = r.nbr[pl.ds(step, 1), :] & 255
        high = r.high[pl.ds(step, 1), :]
        hot = jnp.where(
            lax.broadcasted_iota(jnp.int32, (256, n), 0) == low, 1.0, 0.0
        ).astype(BF)
        found = mm(r.table[...], hot)
        high8 = jnp.broadcast_to(high, (8, n))
        near = jnp.zeros((8, 8, n), F32)
        for h in range(8):
            part = found[h * 64 : (h + 1) * 64].reshape(8, 8, n)
            near = jnp.where((high8 == h)[None], part, near)
        sub = lax.broadcasted_iota(jnp.int32, (8, n), 0)
        lane = lax.broadcasted_iota(jnp.int32, (8, n), 1)
        place = found[512:536].reshape(3, 8, n)
        place = jnp.where((high8 == sub)[None], place, 0.0).reshape(24, n)
        ij = (lane >> 11) + step * ENC_COLUMNS
        centre = first_layer_centres(ij, (lane & 2047) >> 3, sub)
        stacked = jnp.concatenate([place, place, centre], 0).astype(BF)
        half = mm(r.ew1[...], stacked)
        hidden = (half + half * jnp.tanh(half)).astype(BF)
        kernel = mm(r.ewo[...], hidden)
        shares = (kernel * near.reshape(64, n)).astype(BF)
        for k in range(ENC_COLUMNS):
            row = pl.multiple_of((step * ENC_COLUMNS + k) * 64, 64)
            r.prod[pl.ds(row, 64), :] = shares[:, k * 2048 : (k + 1) * 2048]
        return carry

    lax.fori_loop(0, steps, columns, 0)
    shares = 1.0 / counts
    group = 8
    for g in range(COLUMNS // group):
        latent = mm(r.prod[g * group * 64 : (g + 1) * group * 64, :], r.sums[...])
        for k in range(group):
            ij = g * group + k
            row, part = ij // ENC_COLUMNS, ij % ENC_COLUMNS
            share = shares[row : row + 1, part * DEPTH : (part + 1) * DEPTH]
            r.lat[ij * 64 : (ij + 1) * 64, :] = (
                latent[k * 64 : (k + 1) * 64] * share
            ).astype(BF)
    both = nt(r.waves[...], r.lat[...])
    for ij in range(COLUMNS):
        part = both[:, ij * 64 : (ij + 1) * 64]
        r.z_rows[:, ij : ij + 1, :] = jnp.concatenate([part[0:16], part[16:32]], 1).reshape(
            16, 1, 128
        )
    r.z[...] = r.z_rows[...].astype(BF)


def forward_modes(z, r, pairs, recv_a, send_b, recv_b, meanwhile):
    exchange("py", z, recv_a, pairs[0], meanwhile(0))
    u = mm(r.ky[...], recv_a[...].reshape(512, 128))
    send_b[...] = turned(u[:256], u[256:], 1.0).astype(BF).reshape(GROUP, 16, 128)
    exchange("px", send_b, recv_b, pairs[1], meanwhile(1))
    u = mm(r.kx[...], recv_b[...].reshape(256, 128))
    return turned(u[:64], u[64:], 1.0) * SCALING


def own_doubling():
    return jnp.where(lax.axis_index("py") == 0, 1.0, 2.0)


def mixed(modes, weight_ref):
    lanes = lax.broadcasted_iota(jnp.int32, (64, 128), 1)
    swapped = pltpu.roll(modes, CHANNELS, 1)
    real2 = jnp.where(lanes < CHANNELS, modes, swapped)
    imag2 = jnp.where(lanes < CHANNELS, swapped, modes)
    rows4 = lax.broadcasted_iota(jnp.int32, (64, 256), 0) & 3
    keep = (lax.broadcasted_iota(jnp.int32, (64, 256), 1) >> 6) == rows4
    real4 = jnp.where(keep, jnp.concatenate([real2, real2], 1), 0.0)
    imag4 = jnp.where(keep, jnp.concatenate([imag2, imag2], 1), 0.0)
    first = (lax.broadcasted_iota(jnp.int32, (16, 128), 0) & 7) < 4
    out = []
    for h in range(8):
        left = jnp.concatenate([real4[8 * h : 8 * h + 8], imag4[8 * h : 8 * h + 8]], 0)
        left = left.astype(BF)
        lower = mm(left, weight_ref[8 * h : 8 * h + 4].reshape(256, 128))
        upper = mm(left, weight_ref[8 * h + 4 : 8 * h + 8].reshape(256, 128))
        both = jnp.where(first, lower, upper)
        out.append(turned(both[0:8], both[8:16], -1.0))
    return jnp.concatenate(out, 0)


def fourier(r, meanwhile):
    modes = forward_modes(
        r.z, r, ((r.s3, r.r3), (r.s4, r.r4)), r.recv_a, r.send_b, r.recv_b, meanwhile
    )
    r.modes[...] = modes
    v = mixed(modes, r.weight) * (own_doubling() * SCALING)
    u = mm(r.kxi[...], v.astype(BF))
    r.send_c[...] = turned(u[:256], u[256:], -1.0).astype(BF).reshape(GROUP, 16, 128)
    exchange("px", r.send_c, r.recv_c, (r.s5, r.r5), meanwhile(2))
    u = mm(r.kyi[...], r.recv_c[...].reshape(256, 128))
    r.send_d[...] = turned(u[:512], u[512:], -1.0).astype(BF).reshape(GROUP, COLUMNS, 128)
    exchange("py", r.send_d, r.recv_d, (r.s6, r.r6), meanwhile(3))


def prepare(r, first, last):
    n = PREP

    def block(step, carry):
        off = pl.multiple_of(step * n, n)
        half_block = step & 1
        expanded = nt(
            r.extra[step >> 1].astype(BF),
            r.pairs[pl.ds(pl.multiple_of(half_block * n, n), n), :],
        )
        cells = r.lists[:, pl.ds(off, n)]
        low, column = cells & 255, cells >> 8
        hot = jnp.where(
            lax.broadcasted_iota(jnp.int32, (256, n), 0) == low, 1.0, 0.0
        ).astype(BF)
        found = mm(r.lat[...], hot)
        column8 = jnp.broadcast_to(column, (8, n))
        near = jnp.zeros((8, 8, n), F32)
        for k in range(COLUMNS):
            part = found[k * 64 : (k + 1) * 64].reshape(8, 8, n)
            near = jnp.where((column8 == k)[None], part, near)
        r.before[:, pl.ds(off, n)] = mm(r.skip[...], near.reshape(64, n).astype(BF))
        tw = mm(r.waves[...], hot)
        match = lax.broadcasted_iota(jnp.int32, (COLUMNS, n), 0) == column
        for q in range(32):
            r.basis[q * 32 : (q + 1) * 32, pl.ds(off, n)] = jnp.where(
                match, tw[q : q + 1], 0.0
            ).astype(BF)
        sub = lax.broadcasted_iota(jnp.int32, (8, n), 0)
        stacked = jnp.concatenate(
            [expanded, first_layer_centres(column, low, sub)], 0
        ).astype(BF)
        half = mm(r.dw1[...], stacked)
        hidden = (half + half * jnp.tanh(half)).astype(BF)
        r.kern[:, pl.ds(off, n)] = mm(r.dwo[...], hidden) * r.read[...]
        return carry

    lax.fori_loop(first, last, block, 0)


def parts_of(values, parts):
    out, rest = [], values
    for _ in range(parts):
        rounded = rest.astype(BF).astype(F32)
        out.append(rounded)
        rest = rest - rounded
    return jnp.concatenate(out, 0).astype(BF)


def decode(r):
    flipped = nt(identity(128), r.recv_d[...].reshape(512, 128))
    r.back_t[...] = jnp.concatenate([flipped[0:64], flipped[64:128]], 1).astype(BF)
    n = POST

    def forward(step, carry):
        off = pl.multiple_of(step * n, n)
        here = pl.ds(off, n)
        before = mm(r.back_t[...], r.basis[:, here]) + r.before[:, here]
        phi = 0.5 * (1.0 + lax.erf(before * HALF_ROOT))
        slope = phi + before * jnp.exp(-0.5 * before * before) * GAUSS_NORM
        weighed = r.kern[:, here]
        r.kern[:, here] = weighed * slope
        dots = jnp.sum(weighed * (before * phi), axis=0, keepdims=True)
        for k in range(n // 1024):
            r.dots[pl.ds(step * (n // 1024) + k, 1), :] = dots[:, k * 1024 : (k + 1) * 1024]
        return carry

    lax.fori_loop(0, 4 * SLOT_TOTAL // n, forward, 0)
    summed = mm(parts_of(r.dots[...], 3), r.pairs[...])
    summed = summed[0:8] + summed[8:16] + summed[16:24]
    living = r.living[...]
    pred = living * (summed * 0.25)
    for h in range(8):
        r.pred[:, h * 256 : (h + 1) * 256] = pred[h : h + 1]
    residue = living * (pred - r.target[...]) * 0.25
    spread = nt(parts_of(residue, 2), r.pairs[...])
    r.dots[...] = spread[0:8] + spread[8:16]
    r.total[...] = jnp.zeros(r.total.shape, F32)

    def backward(step, carry):
        here = pl.ds(pl.multiple_of(step * 1024, 1024), 1024)
        shares = (r.kern[:, here] * r.dots[pl.ds(step, 1), :]).astype(BF)
        r.total[...] += nt(shares, r.basis[:, here])
        return carry

    lax.fori_loop(0, 4 * SLOT_TOTAL // 1024, backward, 0)
    out = jnp.concatenate([r.total[:, 0:512].T, r.total[:, 512:1024].T], 1)
    r.grad_z[...] = out.astype(BF).reshape(GROUP, COLUMNS, 128)


WIDE, NARROW, POINT_BLOCK = (GROUP, COLUMNS, 128), (GROUP, 16, 128), (GROUP, 128, 128)
INPUTS = (
    "x", "route", "live", "nbr", "cnt", "lists", "ew1", "ewo", "dw1", "dwo", "skip", "read",
    "weight", "sums", "pairs", "waves", "ky", "kx", "kxi", "kyi",
)
OUTPUTS = {
    "pred": ((1, SLOT_TOTAL), F32), "modes": ((64, 128), F32), "grads": ((64, 128), F32),
}
SCRATCH = {
    "send1": (POINT_BLOCK, BF), "recv1": (POINT_BLOCK, BF),
    "send2": (POINT_BLOCK, BF), "recv2": (POINT_BLOCK, BF),
    "regroup": ((GROUP, GROUP, CAPACITY, 128), F32), "slot": ((1, POINTS), jnp.int32),
    "tab": ((SLOT_TOTAL, 128), BF), "table": ((544, 256), BF), "pos_rows": ((32, 256), F32),
    "extra": ((8, 8, 256), F32), "target": ((8, 256), F32), "living": ((8, 256), F32),
    "high": ((COLUMNS // ENC_COLUMNS, 2048 * ENC_COLUMNS), jnp.int32),
    "prod": ((COLUMNS * 64, 2048), BF), "lat": ((COLUMNS * 64, DEPTH), BF),
    "z_rows": (WIDE, F32), "z": (WIDE, BF), "recv_a": (WIDE, BF), "send_b": (NARROW, BF),
    "recv_b": (NARROW, BF), "send_c": (NARROW, BF), "recv_c": (NARROW, BF),
    "send_d": (WIDE, BF), "recv_d": (WIDE, BF),
    "before": ((64, 4 * SLOT_TOTAL), F32), "kern": ((64, 4 * SLOT_TOTAL), F32),
    "basis": ((1024, 4 * SLOT_TOTAL), BF), "back_t": ((64, 1024), BF),
    "dots": ((8, 1024), F32), "total": ((64, 1024), F32),
    "grad_z": (WIDE, BF), "recv_e": (WIDE, BF), "send_f": (NARROW, BF), "recv_f": (NARROW, BF),
}
EXCHANGES = 8


def step_kernel(*refs):
    names = list(INPUTS) + list(OUTPUTS) + list(SCRATCH)
    for k in range(1, EXCHANGES + 1):
        names += [f"s{k}", f"r{k}"]
    r = types.SimpleNamespace(**dict(zip(names, refs)))
    send_points(r)
    encode(r)
    blocks = 4 * SLOT_TOTAL // PREP // 4
    fourier(r, lambda k: lambda: prepare(r, k * blocks, (k + 1) * blocks))
    decode(r)
    grads = forward_modes(
        r.grad_z, r, ((r.s7, r.r7), (r.s8, r.r8)), r.recv_e, r.send_f, r.recv_f,
        lambda k: None,
    )
    r.grads[...] = grads * own_doubling()


def step(*inputs):
    whole = pl.BlockSpec(memory_space=pltpu.VMEM)
    in_specs = [whole] * len(INPUTS)
    in_specs[INPUTS.index("live")] = pl.BlockSpec(memory_space=pltpu.SMEM)
    semaphores = [pltpu.SemaphoreType.DMA((GROUP,))] * (2 * EXCHANGES)
    return pl.pallas_call(
        step_kernel,
        out_shape=tuple(jax.ShapeDtypeStruct(*v) for v in OUTPUTS.values()),
        in_specs=in_specs,
        out_specs=(whole,) * len(OUTPUTS),
        scratch_shapes=[pltpu.VMEM(*v) for v in SCRATCH.values()] + semaphores,
        compiler_params=pltpu.CompilerParams(
            collective_id=0, has_side_effects=True, vmem_limit_bytes=VMEM_LIMIT
        ),
        name="training_step",
    )(*inputs)


def outer_kernel(modes_ref, grad_ref, out_ref):
    modes_t = modes_ref[...].T
    grads = grad_ref[...]
    swapped = pltpu.roll(grads, CHANNELS, 1) * lane_sign(grads.shape)
    for m in range(8):
        out_ref[m] = (
            modes_t[0:64, m : m + 1] * grads[m : m + 1]
            + modes_t[64:128, m : m + 1] * swapped[m : m + 1]
        )


def outer(modes, grads):
    return pl.pallas_call(
        outer_kernel,
        grid=(8,),
        out_shape=jax.ShapeDtypeStruct((64, 64, 128), F32),
        in_specs=[pl.BlockSpec((8, 128), lambda i: (i, 0))] * 2,
        out_specs=pl.BlockSpec((8, 64, 128), lambda i: (i, 0, 0)),
        compiler_params=pltpu.CompilerParams(vmem_limit_bytes=VMEM_LIMIT),
        name="outer",
    )(modes, grads)


def two_parts(values):
    high = lax.reduce_precision(values, 8, 7)
    return high.astype(BF), (values - high).astype(BF)


def encoder_first(weight, bias):
    high, low = two_parts(weight * 0.5)
    bias_high, bias_low = two_parts(bias * 0.5)
    return jnp.concatenate(
        [
            jnp.repeat(high, 8, axis=0), jnp.repeat(low, 8, axis=0),
            -high, -low, bias_high[None], bias_low[None],
        ],
        0,
    ).T


def decoder_first(weight, bias):
    high, low = two_parts(weight * 0.5)
    bias_high, bias_low = two_parts(bias * 0.5)
    return jnp.concatenate(
        [
            high, low, jnp.zeros((2, weight.shape[1]), BF),
            -high, -low, bias_high[None], bias_low[None],
        ],
        0,
    ).T


def body(
    point_features, positions, targets, routes, live_counts, cell_neighbours, cell_counts,
    slot_neighbours, encoder_in, encoder_bias, encoder_out, decoder_in, decoder_bias,
    decoder_out, skip_weight, spectral_weight, readout_weight,
):
    x = jnp.concatenate(
        [
            point_features, positions, targets[:, None],
            jnp.ones((POINTS, 1), BF), jnp.zeros((POINTS, 59), BF),
        ],
        1,
    )
    steps = COLUMNS // ENC_COLUMNS
    pred, modes, grads = step(
        x, routes.reshape(1, POINTS), live_counts,
        cell_neighbours.reshape(steps, -1), cell_counts.reshape(steps, -1), slot_neighbours,
        encoder_first(encoder_in, encoder_bias), encoder_out.T,
        decoder_first(decoder_in, decoder_bias), decoder_out.T, skip_weight.T,
        readout_weight[:, None], spectral_weight.reshape(64, 64, 128),
        jnp.asarray(entry_sums()), jnp.asarray(pair_sums()), jnp.asarray(depth_waves()),
        jnp.asarray(kron_forward_y()), jnp.asarray(kron_forward_x()),
        jnp.asarray(kron_inverse_x()), jnp.asarray(kron_inverse_y()),
    )
    return pred, outer(modes, grads).reshape(32, 2, 1, 64, 128)


def solution(mesh):
    in_specs = (
        P(("px", "py"), None), P(("px", "py"), None), P(("px", "py")), P(("px", "py"), None),
        P(("px", "py")), P("px", "py", None), P("px", "py", None), P(("px", "py"), None),
        P(), P(), P(), P(), P(), P(), P(),
        P(None, "px", "py", None, None), P(),
    )
    out_specs = (P(("px", "py"), None), P(None, "px", "py", None, None))
    return jax.shard_map(body, mesh=mesh, in_specs=in_specs, out_specs=out_specs, check_vma=False)
```

```python
import math
import types

import jax
import jax.numpy as jnp
import numpy as np
from jax import lax
from jax.experimental import pallas as pl
from jax.experimental.pallas import tpu as pltpu
from jax.sharding import PartitionSpec as P

MESH = pl.DeviceIdType.MESH
HALF_ROOT = 0.7071067811865476
GAUSS_NORM = 0.3989422804014327
BF = jnp.bfloat16
F32 = jnp.float32
GROUP = 16
CHANNELS = 64
COLUMNS = 32
DEPTH = 256
CAPACITY = 8
SLOT_TOTAL = 2048
POINTS = 1024
SCALING = 1.0 / math.sqrt(128 * 64 * 256)
VMEM_LIMIT = 60 * 1024 * 1024
ENC_COLUMNS = 2
PREP = 512
OUTER = 16
POST = 2048


def frequencies():
    counted = np.arange(32)
    return np.where(counted < 16, counted, counted - 32)


def wave(length, positions, frequency):
    angles = 2.0 * np.pi * ((positions[:, None] * frequency[None, :]) % length) / length
    return np.cos(angles), np.sin(angles)


def bf16_of(array):
    return np.asarray(array, np.float32).astype(BF)


def kron_forward_y():
    cos, sin = wave(64, np.arange(64), frequencies())
    out = []
    for part in (cos, sin):
        w = part.reshape(16, 4, 16, 2)
        full = np.einsum("cjdp,ik->dpicjk", w, np.eye(8)).transpose(0, 1, 2, 3, 5, 4)
        out.append(full.reshape(256, 512))
    return bf16_of(np.concatenate(out))


def kron_forward_x():
    cos, sin = wave(128, np.arange(128), frequencies())
    out = []
    for part in (cos, sin):
        w = part.reshape(16, 8, 32)
        full = np.einsum("air,ps->rpasi", w, np.eye(2))
        out.append(full.reshape(64, 256))
    return bf16_of(np.concatenate(out))


def kron_inverse_x():
    cos, sin = wave(128, np.arange(128), frequencies())
    out = []
    for part in (cos, sin):
        w = part.reshape(16, 8, 32)
        full = np.einsum("air,ps->apirs", w, np.eye(2))
        out.append(full.reshape(256, 64))
    return bf16_of(np.concatenate(out))


def kron_inverse_y():
    cos, sin = wave(64, np.arange(64), frequencies())
    out = []
    for part in (cos, sin):
        w = part.reshape(16, 4, 16, 2)
        full = np.einsum("cjdp,ik->cijdpk", w, np.eye(8))
        out.append(full.reshape(512, 256))
    return bf16_of(np.concatenate(out))


def depth_waves():
    cos, sin = wave(256, np.arange(16), np.arange(256))
    return bf16_of(np.concatenate([cos, -sin]))


def nt(left, right):
    return lax.dot_general(left, right, (((1,), (1,)), ((), ())), preferred_element_type=F32)


def mm(left, right):
    return jnp.dot(left, right, preferred_element_type=F32)


def identity(n):
    rows = lax.broadcasted_iota(jnp.int32, (n, n), 0)
    lanes = lax.broadcasted_iota(jnp.int32, (n, n), 1)
    return jnp.where(rows == lanes, 1.0, 0.0).astype(BF)


def lane_sign(shape):
    lanes = lax.broadcasted_iota(jnp.int32, shape, 1)
    return jnp.where(lanes < CHANNELS, 1.0, -1.0)


def turned(cos_part, sin_part, direction):
    swapped = pltpu.roll(sin_part, CHANNELS, 1)
    return cos_part + swapped * (lane_sign(swapped.shape) * direction)


def others():
    a, c = lax.axis_index("px"), lax.axis_index("py")
    return a, c


def greet():
    a, c = others()
    barrier = pltpu.get_barrier_semaphore()

    def greeting(d, carry):
        pl.semaphore_signal(barrier, inc=1, device_id=((a + d) & 15, c), device_id_type=MESH)
        pl.semaphore_signal(barrier, inc=1, device_id=(a, (c + d) & 15), device_id_type=MESH)
        return carry

    lax.fori_loop(1, GROUP, greeting, 0)


def greeted():
    pl.semaphore_wait(pltpu.get_barrier_semaphore(), 2 * (GROUP - 1))


def copy_to(axis, d, send, recv, send_sem, recv_sem):
    a, c = others()
    me = a if axis == "px" else c
    peer = (me + d) & 15
    return pltpu.make_async_remote_copy(
        src_ref=send.at[peer],
        dst_ref=recv.at[me],
        send_sem=send_sem.at[d],
        recv_sem=recv_sem.at[me],
        device_id=(peer, c) if axis == "px" else (a, peer),
        device_id_type=MESH,
    )


def start_all(axis, send, recv, send_sem, recv_sem):
    def start(d, carry):
        copy_to(axis, d, send, recv, send_sem, recv_sem).start()
        return carry

    lax.fori_loop(1, GROUP, start, 0)


def finish(axis, send, recv, send_sem, recv_sem):
    me = lax.axis_index(axis)
    recv[me] = send[me]

    def arrival(d, carry):
        copy_to(axis, d, send, recv, send_sem, recv_sem).wait_send()
        source = (me - d) & 15
        pltpu.make_async_remote_copy(
            src_ref=send.at[source],
            dst_ref=recv.at[source],
            send_sem=send_sem.at[d],
            recv_sem=recv_sem.at[source],
            device_id=others(),
            device_id_type=MESH,
        ).wait_recv()
        return carry

    lax.fori_loop(1, GROUP, arrival, 0)


def exchange(axis, send, recv, pair, meanwhile=None):
    start_all(axis, send, recv, *pair)
    if meanwhile is not None:
        meanwhile()
    finish(axis, send, recv, *pair)


def pick_rows(rows, sub):
    out = jnp.zeros(sub.shape, F32)
    for k, row in enumerate(rows):
        out = jnp.where(sub == k, row, out)
    return out


def send_points(r, meanwhile):
    greet()
    live = r.live[0]
    lanes = lax.broadcasted_iota(jnp.int32, (1, POINTS), 1)
    target = jnp.where(lanes < live, r.route[...], 256)
    owners = lax.broadcasted_iota(jnp.int32, (256, POINTS), 0)
    named = jnp.where(owners == target, 1.0, 0.0)
    earlier = jnp.where(
        lax.broadcasted_iota(jnp.int32, (POINTS, POINTS), 0)
        < lax.broadcasted_iota(jnp.int32, (POINTS, POINTS), 1),
        1.0,
        0.0,
    ).astype(BF)
    counted = mm(named.astype(BF), earlier)
    rank = jnp.sum(named * counted, axis=0, keepdims=True).astype(jnp.int32)
    kept = target < 256
    r.slot[...] = jnp.where(kept, target * CAPACITY + rank, -1)
    features = r.features[...]
    r.twice[...] = jnp.concatenate([features, features], 0)
    sub = lax.broadcasted_iota(jnp.int32, (8, POINTS), 0)
    places = r.positions[...].astype(F32)
    rest = pick_rows(
        [places[0:1], places[1:2], places[2:3], r.targets[...].astype(F32), 1.0], sub
    )
    rows = lax.broadcasted_iota(jnp.int32, (128, POINTS), 0)
    spread = jnp.where((rows >> 3) == (target & 15), jnp.concatenate([rest] * 16, 0), 0.0)
    mine = jnp.where(kept, (target >> 4) * CAPACITY + rank, -1)
    hot = jnp.where(rows == mine, 1.0, 0.0).astype(BF)
    r.rest[...] = nt(hot, spread.astype(BF)).reshape(GROUP, 8, 128)
    greeted()
    a = lax.axis_index("px")
    low_lanes = lax.broadcasted_iota(jnp.int32, (64, 128), 1) < 64
    nothing = jnp.zeros((8, 128), F32)

    def pack(d, carry):
        peer = (a + d) & 15
        at = lax.broadcasted_iota(jnp.int32, (128, POINTS), 0) + peer * 128
        hot = jnp.where(at == r.slot[...], 1.0, 0.0).astype(BF)
        packed = nt(hot, r.twice[...])
        r.send1[peer, 0:64] = jnp.where(low_lanes, packed[0:64], packed[64:128]).astype(BF)
        r.send1[peer, 64:80] = jnp.concatenate([r.rest[peer], nothing], 0).astype(BF)

        @pl.when(d > 0)
        def _():
            copy_to("px", d, r.send1, r.recv1, r.s1, r.r1).start()

        return carry

    lax.fori_loop(0, GROUP, pack, 0)
    meanwhile(0)()
    finish("px", r.send1, r.recv1, r.s1, r.r1)
    for source in range(GROUP):
        r.regroup[source] = r.recv1[source, 0:64].astype(F32).reshape(8, CAPACITY, 128)
        r.rest[source] = r.recv1[source, 64:80].astype(F32)[0:8]
    eye = identity(128)
    rest = nt(eye, r.rest[...].reshape(128, 128).astype(BF))
    for c in range(8):
        first = r.regroup[0:8, c].reshape(64, 128)
        second = r.regroup[8:16, c].reshape(64, 128)
        r.send2[c, 0:64] = jnp.where(
            low_lanes, first, pltpu.roll(second, 64, 1)
        ).astype(BF)
        r.send2[c + 8, 0:64] = jnp.where(
            low_lanes, pltpu.roll(first, 64, 1), second
        ).astype(BF)
    for c in range(GROUP):
        r.send2[c, 64:80] = jnp.concatenate([rest[c * 8 : c * 8 + 8], nothing], 0).astype(BF)
    exchange("py", r.send2, r.recv2, (r.s2, r.r2), meanwhile(1))


def slot_tables(r):
    eye = identity(128)
    low_lanes = lax.broadcasted_iota(jnp.int32, (8, 128), 1) < 64
    r.pos_rows[...] = jnp.zeros(r.pos_rows.shape, F32)
    for h in range(8):
        rows = jnp.concatenate([r.recv2[2 * h, 0:64], r.recv2[2 * h + 1, 0:64]], 0)
        flipped = nt(eye, rows).astype(BF)
        r.table[h * 64 : (h + 1) * 64, 0:128] = flipped[0:64]
        r.table[h * 64 : (h + 1) * 64, 128:256] = flipped[64:128]
        even = r.recv2[2 * h, 64:80].astype(F32)[0:8]
        odd = r.recv2[2 * h + 1, 64:80].astype(F32)[0:8]
        r.rest[2 * h] = even
        r.rest[2 * h + 1] = odd
        left = jnp.where(low_lanes, even, pltpu.roll(odd, 64, 1))
        right = jnp.where(low_lanes, pltpu.roll(even, 64, 1), odd)
        for d in range(3):
            r.pos_rows[d * 8 + h : d * 8 + h + 1, 0:128] = left[d : d + 1]
            r.pos_rows[d * 8 + h : d * 8 + h + 1, 128:256] = right[d : d + 1]
    r.table[512:544, :] = r.pos_rows[...].astype(BF)
    by_slot = nt(eye, r.rest[...].reshape(128, 128).astype(BF))
    rows = lax.broadcasted_iota(jnp.int32, (128, 128), 0)
    lanes = lax.broadcasted_iota(jnp.int32, (128, 128), 1)
    same = (rows >> 3) == (lanes >> 3)
    sub = lax.broadcasted_iota(jnp.int32, (8, 128), 0)
    part = lax.broadcasted_iota(jnp.int32, (8, 128), 1) & 7
    wanted = jnp.where(sub < 3, sub, sub - 3)
    chooser = jnp.where(part == wanted, 1.0, 0.0).astype(BF)
    for a in range(GROUP):
        spread = jnp.concatenate([by_slot[a * 8 : a * 8 + 8]] * 16, 0)
        extra = nt(chooser, jnp.where(same, spread, 0.0).astype(BF))
        h, half = a // 2, (a % 2) * 128
        r.extra[h, :, half : half + 128] = extra
        r.target[h : h + 1, half : half + 128] = extra[6:7]
        r.living[h : h + 1, half : half + 128] = extra[7:8]


def group_sums(r):
    for ref, shift in ((r.sums, 3), (r.pairs, 2)):
        rows = lax.broadcasted_iota(jnp.int32, ref.shape, 0)
        lanes = lax.broadcasted_iota(jnp.int32, ref.shape, 1)
        ref[...] = jnp.where((rows >> shift) == lanes, 1.0, 0.0).astype(BF)


def first_layers(r):
    def halves(values):
        high = (values * 0.5).astype(BF).astype(F32)
        return high, values * 0.5 - high

    high, low = halves(r.ein[...])
    bias_high, bias_low = halves(r.ebias[...])
    sub = lax.broadcasted_iota(jnp.int32, (8, 80), 0)
    rows = [jnp.broadcast_to(part[d : d + 1], (8, 80)) for part in (high, low) for d in range(3)]
    rows.append(
        pick_rows(
            [-part[d : d + 1] for part in (high, low) for d in range(3)] + [bias_high, bias_low],
            sub,
        )
    )
    r.ew1[...] = nt(identity(80), jnp.concatenate(rows, 0).astype(BF)).astype(BF)
    high, low = halves(r.din[...])
    bias_high, bias_low = halves(r.dbias[...])
    sub = lax.broadcasted_iota(jnp.int32, (8, 256), 0)
    positive = [part[d : d + 1] for part in (high, low) for d in range(3)]
    negative = [-row for row in positive] + [bias_high, bias_low]
    rows = jnp.concatenate([pick_rows(positive, sub), pick_rows(negative, sub)], 0)
    r.dw1[...] = nt(identity(256), rows.astype(BF)).astype(BF)
    r.skip_t[...] = nt(identity(64), r.skip[...]).astype(BF)
    rows = lax.broadcasted_iota(jnp.int32, (64, 64), 0)
    lanes = lax.broadcasted_iota(jnp.int32, (64, 64), 1)
    r.read[...] = jnp.sum(
        jnp.where(rows == lanes, r.readout[...], 0.0), axis=1, keepdims=True
    )


def first_layer_centres(ij, depth, sub):
    cx = ((ij >> 2).astype(F32) + 0.5) * 0.25 - 1.0
    cy = ((ij & 3).astype(F32) + 0.5) * 0.5 - 1.0
    cz = (depth.astype(F32) + 0.5) * (2.0 / DEPTH) - 1.0
    part3 = jnp.where(sub >= 3, sub - 3, sub)
    return jnp.where(
        sub >= 6, 1.0, jnp.where(part3 == 0, cx, jnp.where(part3 == 1, cy, cz))
    )


def place_lists(r):
    for i in range(8):
        r.counts[i * 4 : (i + 1) * 4, :] = r.cnt[i].astype(F32)
        r.low[i * 4 : (i + 1) * 4, :] = r.nbr[i]
    spread = nt(r.counts[...].astype(BF), r.sums[...])
    places = (lax.broadcasted_iota(jnp.int32, (COLUMNS, 2048), 1) & 7).astype(F32)
    ids = r.low[...]
    r.high[...] = jnp.where(places < spread, (ids >> 4) & 7, 8)
    r.low[...] = (
        ((ids >> 10) << 7) + (((ids >> 3) & 1) << 6) + (((ids >> 7) & 7) << 3) + (ids & 7)
    )


def encode(r):
    n = 2048 * ENC_COLUMNS

    def columns(step, carry):
        rows = [step * ENC_COLUMNS + k for k in range(ENC_COLUMNS)]
        low = jnp.concatenate([r.low[pl.ds(row, 1), :] for row in rows], 1)
        high = jnp.concatenate([r.high[pl.ds(row, 1), :] for row in rows], 1)
        hot = jnp.where(
            lax.broadcasted_iota(jnp.int32, (256, n), 0) == low, 1.0, 0.0
        ).astype(BF)
        found = mm(r.table[...], hot)
        high8 = jnp.broadcast_to(high, (8, n))
        near = jnp.zeros((8, 8, n), F32)
        for h in range(8):
            part = found[h * 64 : (h + 1) * 64].reshape(8, 8, n)
            near = jnp.where((high8 == h)[None], part, near)
        sub = lax.broadcasted_iota(jnp.int32, (8, n), 0)
        lane = lax.broadcasted_iota(jnp.int32, (8, n), 1)
        place = found[512:536].reshape(3, 8, n)
        place = jnp.where((high8 == sub)[None], place, 0.0).reshape(24, n)
        ij = (lane >> 11) + step * ENC_COLUMNS
        centre = first_layer_centres(ij, (lane & 2047) >> 3, sub)
        stacked = jnp.concatenate([place, place, centre], 0).astype(BF)
        half = mm(r.ew1[...], stacked)
        hidden = (half + half * jnp.tanh(half)).astype(BF)
        kernel = mm(r.ewo[...], hidden)
        shares = (kernel * near.reshape(64, n)).astype(BF)
        for k in range(ENC_COLUMNS):
            row = pl.multiple_of((step * ENC_COLUMNS + k) * 64, 64)
            r.prod[pl.ds(row, 64), :] = shares[:, k * 2048 : (k + 1) * 2048]
        return carry

    lax.fori_loop(0, COLUMNS // ENC_COLUMNS, columns, 0)
    shares = 1.0 / r.counts[...]
    group = 8
    for g in range(COLUMNS // group):
        latent = mm(r.prod[g * group * 64 : (g + 1) * group * 64, :], r.sums[...])
        for k in range(group):
            ij = g * group + k
            r.lat[ij * 64 : (ij + 1) * 64, :] = (
                latent[k * 64 : (k + 1) * 64] * shares[ij : ij + 1]
            ).astype(BF)
    both = nt(r.waves[...], r.lat[...])
    for ij in range(COLUMNS):
        part = both[:, ij * 64 : (ij + 1) * 64]
        r.z_rows[:, ij : ij + 1, :] = jnp.concatenate([part[0:16], part[16:32]], 1).reshape(
            16, 1, 128
        )
    r.z[...] = r.z_rows[...].astype(BF)


def forward_modes(z, r, pairs, recv_a, send_b, recv_b, meanwhile):
    exchange("py", z, recv_a, pairs[0], meanwhile(0))
    u = mm(r.ky[...], recv_a[...].reshape(512, 128))
    send_b[...] = turned(u[:256], u[256:], 1.0).astype(BF).reshape(GROUP, 16, 128)
    exchange("px", send_b, recv_b, pairs[1], meanwhile(1))
    u = mm(r.kx[...], recv_b[...].reshape(256, 128))
    return turned(u[:64], u[64:], 1.0) * SCALING


def own_doubling():
    return jnp.where(lax.axis_index("py") == 0, 1.0, 2.0)


def mixed(modes, weight_ref):
    lanes = lax.broadcasted_iota(jnp.int32, (64, 128), 1)
    swapped = pltpu.roll(modes, CHANNELS, 1)
    real2 = jnp.where(lanes < CHANNELS, modes, swapped)
    imag2 = jnp.where(lanes < CHANNELS, swapped, modes)
    rows4 = lax.broadcasted_iota(jnp.int32, (64, 256), 0) & 3
    keep = (lax.broadcasted_iota(jnp.int32, (64, 256), 1) >> 6) == rows4
    real4 = jnp.where(keep, jnp.concatenate([real2, real2], 1), 0.0)
    imag4 = jnp.where(keep, jnp.concatenate([imag2, imag2], 1), 0.0)
    first = (lax.broadcasted_iota(jnp.int32, (16, 128), 0) & 7) < 4
    out = []
    for h in range(8):
        left = jnp.concatenate([real4[8 * h : 8 * h + 8], imag4[8 * h : 8 * h + 8]], 0)
        left = left.astype(BF)
        lower = mm(left, weight_ref[8 * h : 8 * h + 4].reshape(256, 128))
        upper = mm(left, weight_ref[8 * h + 4 : 8 * h + 8].reshape(256, 128))
        both = jnp.where(first, lower, upper)
        out.append(turned(both[0:8], both[8:16], -1.0))
    return jnp.concatenate(out, 0)


def fourier(r, meanwhile):
    modes = forward_modes(
        r.z, r, ((r.s3, r.r3), (r.s4, r.r4)), r.recv_a, r.send_b, r.recv_b, meanwhile
    )
    r.modes[...] = modes
    v = mixed(modes, r.weight) * (own_doubling() * SCALING)
    u = mm(r.kxi[...], v.astype(BF))
    r.send_c[...] = turned(u[:256], u[256:], -1.0).astype(BF).reshape(GROUP, 16, 128)
    exchange("px", r.send_c, r.recv_c, (r.s5, r.r5), meanwhile(2))
    u = mm(r.kyi[...], r.recv_c[...].reshape(256, 128))
    r.send_d[...] = turned(u[:512], u[512:], -1.0).astype(BF).reshape(GROUP, COLUMNS, 128)
    exchange("py", r.send_d, r.recv_d, (r.s6, r.r6), meanwhile(3))


def depth_basis(r):
    n = PREP

    def block(step, carry):
        here = pl.ds(pl.multiple_of(step * n, n), n)
        cells = r.lists[:, here]
        low, column = cells & 255, cells >> 8
        hot = jnp.where(
            lax.broadcasted_iota(jnp.int32, (256, n), 0) == low, 1.0, 0.0
        ).astype(BF)
        tw = mm(r.waves[...], hot)
        match = lax.broadcasted_iota(jnp.int32, (COLUMNS, n), 0) == column
        for q in range(32):
            r.basis[q * 32 : (q + 1) * 32, here] = jnp.where(match, tw[q : q + 1], 0.0).astype(BF)
        return carry

    lax.fori_loop(0, 4 * SLOT_TOTAL // n, block, 0)


def prepare(r, first, last):
    n = PREP

    def block(step, carry):
        off = pl.multiple_of(step * n, n)
        half_block = step & 1
        expanded = nt(
            r.extra[step >> 1].astype(BF),
            r.pairs[pl.ds(pl.multiple_of(half_block * n, n), n), :],
        )
        cells = r.lists[:, pl.ds(off, n)]
        low, column = cells & 255, cells >> 8
        hot = jnp.where(
            lax.broadcasted_iota(jnp.int32, (256, n), 0) == low, 1.0, 0.0
        ).astype(BF)
        found = mm(r.lat[...], hot)
        column8 = jnp.broadcast_to(column, (8, n))
        near = jnp.zeros((8, 8, n), F32)
        for k in range(COLUMNS):
            part = found[k * 64 : (k + 1) * 64].reshape(8, 8, n)
            near = jnp.where((column8 == k)[None], part, near)
        r.before[:, pl.ds(off, n)] = mm(r.skip_t[...], near.reshape(64, n).astype(BF))
        sub = lax.broadcasted_iota(jnp.int32, (8, n), 0)
        stacked = jnp.concatenate(
            [expanded, first_layer_centres(column, low, sub)], 0
        ).astype(BF)
        half = mm(r.dw1[...], stacked)
        hidden = (half + half * jnp.tanh(half)).astype(BF)
        r.kern[:, pl.ds(off, n)] = mm(r.dwo[...], hidden) * r.read[...]
        return carry

    lax.fori_loop(first, last, block, 0)


def parts_of(values, parts):
    out, rest = [], values
    for _ in range(parts):
        rounded = rest.astype(BF).astype(F32)
        out.append(rounded)
        rest = rest - rounded
    return jnp.concatenate(out, 0).astype(BF)


def decode(r):
    flipped = nt(identity(128), r.recv_d[...].reshape(512, 128))
    r.back_t[...] = jnp.concatenate([flipped[0:64], flipped[64:128]], 1).astype(BF)
    n = POST

    def forward(step, carry):
        off = pl.multiple_of(step * n, n)
        here = pl.ds(off, n)
        before = mm(r.back_t[...], r.basis[:, here]) + r.before[:, here]
        phi = 0.5 * (1.0 + lax.erf(before * HALF_ROOT))
        slope = phi + before * jnp.exp(-0.5 * before * before) * GAUSS_NORM
        weighed = r.kern[:, here]
        r.kern[:, here] = weighed * slope
        dots = jnp.sum(weighed * (before * phi), axis=0, keepdims=True)
        for k in range(n // 1024):
            r.dots[pl.ds(step * (n // 1024) + k, 1), :] = dots[:, k * 1024 : (k + 1) * 1024]
        return carry

    lax.fori_loop(0, 4 * SLOT_TOTAL // n, forward, 0)
    summed = mm(parts_of(r.dots[...], 3), r.pairs[...])
    summed = summed[0:8] + summed[8:16] + summed[16:24]
    living = r.living[...]
    pred = living * (summed * 0.25)
    for h in range(8):
        r.pred[:, h * 256 : (h + 1) * 256] = pred[h : h + 1]
    residue = living * (pred - r.target[...]) * 0.25
    spread = nt(parts_of(residue, 2), r.pairs[...])
    r.dots[...] = spread[0:8] + spread[8:16]
    r.total[...] = jnp.zeros(r.total.shape, F32)

    def backward(step, carry):
        here = pl.ds(pl.multiple_of(step * 1024, 1024), 1024)
        shares = (r.kern[:, here] * r.dots[pl.ds(step, 1), :]).astype(BF)
        r.total[...] += nt(shares, r.basis[:, here])
        return carry

    lax.fori_loop(0, 4 * SLOT_TOTAL // 1024, backward, 0)
    out = jnp.concatenate([r.total[:, 0:512].T, r.total[:, 512:1024].T], 1)
    r.grad_z[...] = out.astype(BF).reshape(GROUP, COLUMNS, 128)


WIDE, NARROW, POINT_BLOCK = (GROUP, COLUMNS, 128), (GROUP, 16, 128), (GROUP, 80, 128)
INPUTS = (
    "features", "positions", "targets", "route", "live", "nbr", "cnt", "lists",
    "ein", "ebias", "ewo", "din", "dbias", "dwo", "skip", "readout",
    "weight", "waves", "ky", "kx", "kxi", "kyi",
)
OUTPUTS = {
    "pred": ((1, SLOT_TOTAL), F32), "modes": ((64, 128), F32), "grads": ((64, 128), F32),
}
SCRATCH = {
    "send1": (POINT_BLOCK, BF), "recv1": (POINT_BLOCK, BF),
    "send2": (POINT_BLOCK, BF), "recv2": (POINT_BLOCK, BF),
    "regroup": ((GROUP, 8, CAPACITY, 128), F32), "rest": ((GROUP, 8, 128), F32),
    "slot": ((1, POINTS), jnp.int32), "twice": ((128, POINTS), BF),
    "sums": ((2048, 256), BF), "pairs": ((1024, 256), BF), "ew1": ((80, 56), BF), "dw1": ((256, 16), BF), "skip_t": ((64, 64), BF),
    "read": ((64, 1), F32), "counts": ((COLUMNS, DEPTH), F32), "low": ((COLUMNS, 2048), jnp.int32),
    "table": ((544, 256), BF), "pos_rows": ((32, 256), F32),
    "extra": ((8, 8, 256), F32), "target": ((8, 256), F32), "living": ((8, 256), F32),
    "high": ((COLUMNS, 2048), jnp.int32),
    "prod": ((COLUMNS * 64, 2048), BF), "lat": ((COLUMNS * 64, DEPTH), BF),
    "z_rows": (WIDE, F32), "z": (WIDE, BF), "recv_a": (WIDE, BF), "send_b": (NARROW, BF),
    "recv_b": (NARROW, BF), "send_c": (NARROW, BF), "recv_c": (NARROW, BF),
    "send_d": (WIDE, BF), "recv_d": (WIDE, BF),
    "before": ((64, 4 * SLOT_TOTAL), F32), "kern": ((64, 4 * SLOT_TOTAL), F32),
    "basis": ((1024, 4 * SLOT_TOTAL), BF), "back_t": ((64, 1024), BF),
    "dots": ((8, 1024), F32), "total": ((64, 1024), F32),
    "grad_z": (WIDE, BF), "recv_e": (WIDE, BF), "send_f": (NARROW, BF), "recv_f": (NARROW, BF),
}
EXCHANGES = 8


def step_kernel(*refs):
    names = list(INPUTS) + list(OUTPUTS) + list(SCRATCH)
    for k in range(1, EXCHANGES + 1):
        names += [f"s{k}", f"r{k}"]
    r = types.SimpleNamespace(**dict(zip(names, refs)))

    def before_points():
        group_sums(r)
        first_layers(r)
        place_lists(r)

    send_points(r, lambda k: before_points if k == 0 else lambda: depth_basis(r))
    slot_tables(r)
    encode(r)
    blocks = 4 * SLOT_TOTAL // PREP // 4
    fourier(r, lambda k: lambda: prepare(r, k * blocks, (k + 1) * blocks))
    decode(r)
    grads = forward_modes(
        r.grad_z, r, ((r.s7, r.r7), (r.s8, r.r8)), r.recv_e, r.send_f, r.recv_f,
        lambda k: None,
    )
    r.grads[...] = grads * own_doubling()


def step(*inputs):
    whole = pl.BlockSpec(memory_space=pltpu.VMEM)
    in_specs = [whole] * len(INPUTS)
    in_specs[INPUTS.index("live")] = pl.BlockSpec(memory_space=pltpu.SMEM)
    semaphores = [pltpu.SemaphoreType.DMA((GROUP,))] * (2 * EXCHANGES)
    return pl.pallas_call(
        step_kernel,
        out_shape=tuple(jax.ShapeDtypeStruct(*v) for v in OUTPUTS.values()),
        in_specs=in_specs,
        out_specs=(whole,) * len(OUTPUTS),
        scratch_shapes=[pltpu.VMEM(*v) for v in SCRATCH.values()] + semaphores,
        compiler_params=pltpu.CompilerParams(
            collective_id=0, has_side_effects=True, vmem_limit_bytes=VMEM_LIMIT
        ),
        name="training_step",
    )(*inputs)


def outer_kernel(modes_ref, grad_ref, out_ref):
    modes_t = modes_ref[...].T
    grads = grad_ref[...]
    swapped = pltpu.roll(grads, CHANNELS, 1) * lane_sign(grads.shape)
    for m in range(OUTER):
        out_ref[m] = (
            modes_t[0:64, m : m + 1] * grads[m : m + 1]
            + modes_t[64:128, m : m + 1] * swapped[m : m + 1]
        )


def outer(modes, grads):
    return pl.pallas_call(
        outer_kernel,
        grid=(64 // OUTER,),
        out_shape=jax.ShapeDtypeStruct((64, 64, 128), F32),
        in_specs=[pl.BlockSpec((OUTER, 128), lambda i: (i, 0))] * 2,
        out_specs=pl.BlockSpec((OUTER, 64, 128), lambda i: (i, 0, 0)),
        compiler_params=pltpu.CompilerParams(vmem_limit_bytes=VMEM_LIMIT),
        name="outer",
    )(modes, grads)


def body(
    point_features, positions, targets, routes, live_counts, cell_neighbours, cell_counts,
    slot_neighbours, encoder_in, encoder_bias, encoder_out, decoder_in, decoder_bias,
    decoder_out, skip_weight, spectral_weight, readout_weight,
):
    pred, modes, grads = step(
        point_features.T, positions.T, targets[None], routes.reshape(1, POINTS), live_counts,
        cell_neighbours, cell_counts, slot_neighbours,
        encoder_in, encoder_bias[None], encoder_out.T,
        decoder_in, decoder_bias[None], decoder_out.T, skip_weight, readout_weight[None],
        spectral_weight.reshape(64, 64, 128),
        jnp.asarray(depth_waves()),
        jnp.asarray(kron_forward_y()), jnp.asarray(kron_forward_x()),
        jnp.asarray(kron_inverse_x()), jnp.asarray(kron_inverse_y()),
    )
    return pred, outer(modes, grads).reshape(32, 2, 1, 64, 128)


def solution(mesh):
    in_specs = (
        P(("px", "py"), None), P(("px", "py"), None), P(("px", "py")), P(("px", "py"), None),
        P(("px", "py")), P("px", "py", None), P("px", "py", None), P(("px", "py"), None),
        P(), P(), P(), P(), P(), P(), P(),
        P(None, "px", "py", None, None), P(),
    )
    out_specs = (P(("px", "py"), None), P(None, "px", "py", None, None))
    return jax.shard_map(body, mesh=mesh, in_specs=in_specs, out_specs=out_specs, check_vma=False)
```

```python
import math
import types

import jax
import jax.numpy as jnp
import numpy as np
from jax import lax
from jax.experimental import pallas as pl
from jax.experimental.pallas import tpu as pltpu
from jax.sharding import PartitionSpec as P

MESH = pl.DeviceIdType.MESH
HALF_ROOT = 0.7071067811865476
GAUSS_NORM = 0.3989422804014327
BF = jnp.bfloat16
F32 = jnp.float32
GROUP = 16
CHANNELS = 64
COLUMNS = 32
DEPTH = 256
CAPACITY = 8
SLOT_TOTAL = 2048
POINTS = 1024
SCALING = 1.0 / math.sqrt(128 * 64 * 256)
VMEM_LIMIT = 60 * 1024 * 1024
ENC_COLUMNS = 2
PREP = 512
OUTER = 32
POST = 2048


def frequencies():
    counted = np.arange(32)
    return np.where(counted < 16, counted, counted - 32)


def wave(length, positions, frequency):
    angles = 2.0 * np.pi * ((positions[:, None] * frequency[None, :]) % length) / length
    return np.cos(angles), np.sin(angles)


def bf16_of(array):
    return np.asarray(array, np.float32).astype(BF)


def kron_forward_y():
    cos, sin = wave(64, np.arange(64), frequencies())
    out = []
    for part in (cos, sin):
        w = part.reshape(16, 4, 16, 2)
        full = np.einsum("cjdp,ik->dpicjk", w, np.eye(8)).transpose(0, 1, 2, 3, 5, 4)
        out.append(full.reshape(256, 512))
    return bf16_of(np.concatenate(out))


def kron_forward_x():
    cos, sin = wave(128, np.arange(128), frequencies())
    out = []
    for part in (cos, sin):
        w = part.reshape(16, 8, 32)
        full = np.einsum("air,ps->rpasi", w, np.eye(2))
        out.append(full.reshape(64, 256))
    return bf16_of(np.concatenate(out))


def kron_inverse_x():
    cos, sin = wave(128, np.arange(128), frequencies())
    out = []
    for part in (cos, sin):
        w = part.reshape(16, 8, 32)
        full = np.einsum("air,ps->apirs", w, np.eye(2))
        out.append(full.reshape(256, 64))
    return bf16_of(np.concatenate(out))


def kron_inverse_y():
    cos, sin = wave(64, np.arange(64), frequencies())
    out = []
    for part in (cos, sin):
        w = part.reshape(16, 4, 16, 2)
        full = np.einsum("cjdp,ik->cijdpk", w, np.eye(8))
        out.append(full.reshape(512, 256))
    return bf16_of(np.concatenate(out))


def depth_waves():
    cos, sin = wave(256, np.arange(16), np.arange(256))
    return bf16_of(np.concatenate([cos, -sin]))


def nt(left, right):
    return lax.dot_general(left, right, (((1,), (1,)), ((), ())), preferred_element_type=F32)


def mm(left, right):
    return jnp.dot(left, right, preferred_element_type=F32)


def identity(n):
    rows = lax.broadcasted_iota(jnp.int32, (n, n), 0)
    lanes = lax.broadcasted_iota(jnp.int32, (n, n), 1)
    return jnp.where(rows == lanes, 1.0, 0.0).astype(BF)


def lane_sign(shape):
    lanes = lax.broadcasted_iota(jnp.int32, shape, 1)
    return jnp.where(lanes < CHANNELS, 1.0, -1.0)


def turned(cos_part, sin_part, direction):
    swapped = pltpu.roll(sin_part, CHANNELS, 1)
    return cos_part + swapped * (lane_sign(swapped.shape) * direction)


def others():
    a, c = lax.axis_index("px"), lax.axis_index("py")
    return a, c


def greet():
    a, c = others()
    barrier = pltpu.get_barrier_semaphore()

    def greeting(d, carry):
        pl.semaphore_signal(barrier, inc=1, device_id=((a + d) & 15, c), device_id_type=MESH)
        pl.semaphore_signal(barrier, inc=1, device_id=(a, (c + d) & 15), device_id_type=MESH)
        return carry

    lax.fori_loop(1, GROUP, greeting, 0)


def greeted():
    pl.semaphore_wait(pltpu.get_barrier_semaphore(), 2 * (GROUP - 1))


def copy_to(axis, d, send, recv, send_sem, recv_sem):
    a, c = others()
    me = a if axis == "px" else c
    peer = (me + d) & 15
    return pltpu.make_async_remote_copy(
        src_ref=send.at[peer],
        dst_ref=recv.at[me],
        send_sem=send_sem.at[d],
        recv_sem=recv_sem.at[me],
        device_id=(peer, c) if axis == "px" else (a, peer),
        device_id_type=MESH,
    )


def start_all(axis, send, recv, send_sem, recv_sem):
    def start(d, carry):
        copy_to(axis, d, send, recv, send_sem, recv_sem).start()
        return carry

    lax.fori_loop(1, GROUP, start, 0)


def finish(axis, send, recv, send_sem, recv_sem):
    me = lax.axis_index(axis)
    recv[me] = send[me]

    def arrival(d, carry):
        copy_to(axis, d, send, recv, send_sem, recv_sem).wait_send()
        source = (me - d) & 15
        pltpu.make_async_remote_copy(
            src_ref=send.at[source],
            dst_ref=recv.at[source],
            send_sem=send_sem.at[d],
            recv_sem=recv_sem.at[source],
            device_id=others(),
            device_id_type=MESH,
        ).wait_recv()
        return carry

    lax.fori_loop(1, GROUP, arrival, 0)


def exchange(axis, send, recv, pair, meanwhile=None):
    start_all(axis, send, recv, *pair)
    if meanwhile is not None:
        meanwhile()
    finish(axis, send, recv, *pair)


def pick_rows(rows, sub):
    out = jnp.zeros(sub.shape, F32)
    for k, row in enumerate(rows):
        out = jnp.where(sub == k, row, out)
    return out


def send_points(r, meanwhile):
    greet()
    live = r.live[0]
    lanes = lax.broadcasted_iota(jnp.int32, (1, POINTS), 1)
    target = jnp.where(lanes < live, r.route[...], 256)
    owners = lax.broadcasted_iota(jnp.int32, (256, POINTS), 0)
    named = jnp.where(owners == target, 1.0, 0.0)
    earlier = jnp.where(
        lax.broadcasted_iota(jnp.int32, (POINTS, POINTS), 0)
        < lax.broadcasted_iota(jnp.int32, (POINTS, POINTS), 1),
        1.0,
        0.0,
    ).astype(BF)
    counted = mm(named.astype(BF), earlier)
    rank = jnp.sum(named * counted, axis=0, keepdims=True).astype(jnp.int32)
    kept = target < 256
    r.slot[...] = jnp.where(kept, target * CAPACITY + rank, -1)
    features = r.features[...]
    r.twice[...] = jnp.concatenate([features, features], 0)
    sub = lax.broadcasted_iota(jnp.int32, (8, POINTS), 0)
    places = r.positions[...].astype(F32)
    wanted = r.targets[...].astype(F32)
    wanted = jnp.concatenate([wanted[k : k + 1] for k in range(8)], 1)
    rest = pick_rows([places[0:1], places[1:2], places[2:3], wanted, 1.0], sub)
    rows = lax.broadcasted_iota(jnp.int32, (128, POINTS), 0)
    spread = jnp.where((rows >> 3) == (target & 15), jnp.concatenate([rest] * 16, 0), 0.0)
    mine = jnp.where(kept, (target >> 4) * CAPACITY + rank, -1)
    hot = jnp.where(rows == mine, 1.0, 0.0).astype(BF)
    r.rest[...] = nt(hot, spread.astype(BF)).reshape(GROUP, 8, 128)
    greeted()
    a = lax.axis_index("px")
    low_lanes = lax.broadcasted_iota(jnp.int32, (64, 128), 1) < 64
    nothing = jnp.zeros((8, 128), F32)

    def pack(step, carry):
        group = ((a >> 2) + 2 + step) & 3
        at = lax.broadcasted_iota(jnp.int32, (512, POINTS), 0) + group * 512
        hot = jnp.where(at == r.slot[...], 1.0, 0.0).astype(BF)
        packed = nt(hot, r.twice[...])
        for k in range(4):
            peer = group * 4 + k
            block = packed[k * 128 : (k + 1) * 128]
            r.send1[peer, 0:64] = jnp.where(low_lanes, block[0:64], block[64:128]).astype(BF)
            r.send1[peer, 64:80] = jnp.concatenate([r.rest[peer], nothing], 0).astype(BF)

            @pl.when(peer != a)
            def _():
                copy_to("px", (peer - a) & 15, r.send1, r.recv1, r.s1, r.r1).start()

        return carry

    lax.fori_loop(0, 4, pack, 0)
    meanwhile(0)()
    finish("px", r.send1, r.recv1, r.s1, r.r1)
    for source in range(GROUP):
        r.regroup[source] = r.recv1[source, 0:64].astype(F32).reshape(8, CAPACITY, 128)
        r.rest[source] = r.recv1[source, 64:80].astype(F32)[0:8]
    eye = identity(128)
    rest = nt(eye, r.rest[...].reshape(128, 128).astype(BF))
    for c in range(8):
        first = r.regroup[0:8, c].reshape(64, 128)
        second = r.regroup[8:16, c].reshape(64, 128)
        r.send2[c, 0:64] = jnp.where(
            low_lanes, first, pltpu.roll(second, 64, 1)
        ).astype(BF)
        r.send2[c + 8, 0:64] = jnp.where(
            low_lanes, pltpu.roll(first, 64, 1), second
        ).astype(BF)
    for c in range(GROUP):
        r.send2[c, 64:80] = jnp.concatenate([rest[c * 8 : c * 8 + 8], nothing], 0).astype(BF)
    exchange("py", r.send2, r.recv2, (r.s2, r.r2), meanwhile(1))


def slot_tables(r):
    eye = identity(128)
    low_lanes = lax.broadcasted_iota(jnp.int32, (8, 128), 1) < 64
    r.pos_rows[...] = jnp.zeros(r.pos_rows.shape, F32)
    for h in range(8):
        rows = jnp.concatenate([r.recv2[2 * h, 0:64], r.recv2[2 * h + 1, 0:64]], 0)
        flipped = nt(eye, rows).astype(BF)
        r.table[h * 64 : (h + 1) * 64, 0:128] = flipped[0:64]
        r.table[h * 64 : (h + 1) * 64, 128:256] = flipped[64:128]
        even = r.recv2[2 * h, 64:80].astype(F32)[0:8]
        odd = r.recv2[2 * h + 1, 64:80].astype(F32)[0:8]
        r.rest[2 * h] = even
        r.rest[2 * h + 1] = odd
        left = jnp.where(low_lanes, even, pltpu.roll(odd, 64, 1))
        right = jnp.where(low_lanes, pltpu.roll(even, 64, 1), odd)
        for d in range(3):
            r.pos_rows[d * 8 + h : d * 8 + h + 1, 0:128] = left[d : d + 1]
            r.pos_rows[d * 8 + h : d * 8 + h + 1, 128:256] = right[d : d + 1]
    r.table[512:544, :] = r.pos_rows[...].astype(BF)
    by_slot = nt(eye, r.rest[...].reshape(128, 128).astype(BF))
    rows = lax.broadcasted_iota(jnp.int32, (128, 128), 0)
    lanes = lax.broadcasted_iota(jnp.int32, (128, 128), 1)
    same = (rows >> 3) == (lanes >> 3)
    sub = lax.broadcasted_iota(jnp.int32, (8, 128), 0)
    part = lax.broadcasted_iota(jnp.int32, (8, 128), 1) & 7
    wanted = jnp.where(sub < 3, sub, sub - 3)
    chooser = jnp.where(part == wanted, 1.0, 0.0).astype(BF)
    for a in range(GROUP):
        spread = jnp.concatenate([by_slot[a * 8 : a * 8 + 8]] * 16, 0)
        extra = nt(chooser, jnp.where(same, spread, 0.0).astype(BF))
        h, half = a // 2, (a % 2) * 128
        r.extra[h, :, half : half + 128] = extra
        r.target[h : h + 1, half : half + 128] = extra[6:7]
        r.living[h : h + 1, half : half + 128] = extra[7:8]


def fetches(r):
    return [
        pltpu.make_async_copy(getattr(r, name + "_far"), getattr(r, name), r.fetched.at[k])
        for k, name in enumerate(FETCHED)
    ]


def group_sums(r):
    for ref, shift in ((r.sums, 3), (r.pairs, 2)):
        rows = lax.broadcasted_iota(jnp.int32, ref.shape, 0)
        lanes = lax.broadcasted_iota(jnp.int32, ref.shape, 1)
        ref[...] = jnp.where((rows >> shift) == lanes, 1.0, 0.0).astype(BF)


def first_layers(r):
    def halves(values):
        high = (values * 0.5).astype(BF).astype(F32)
        return high, values * 0.5 - high

    high, low = halves(r.ein[...])
    bias_high, bias_low = halves(r.ebias[...])
    sub = lax.broadcasted_iota(jnp.int32, (8, 80), 0)
    rows = [jnp.broadcast_to(part[d : d + 1], (8, 80)) for part in (high, low) for d in range(3)]
    rows.append(
        pick_rows(
            [-part[d : d + 1] for part in (high, low) for d in range(3)] + [bias_high, bias_low],
            sub,
        )
    )
    r.ew1[...] = nt(identity(80), jnp.concatenate(rows, 0).astype(BF)).astype(BF)
    high, low = halves(r.din[...])
    bias_high, bias_low = halves(r.dbias[...])
    sub = lax.broadcasted_iota(jnp.int32, (8, 256), 0)
    positive = [part[d : d + 1] for part in (high, low) for d in range(3)]
    negative = [-row for row in positive] + [bias_high, bias_low]
    rows = jnp.concatenate([pick_rows(positive, sub), pick_rows(negative, sub)], 0)
    r.dw1[...] = nt(identity(256), rows.astype(BF)).astype(BF)
    r.skip_t[...] = nt(identity(64), r.skip[...]).astype(BF)
    rows = lax.broadcasted_iota(jnp.int32, (64, 64), 0)
    lanes = lax.broadcasted_iota(jnp.int32, (64, 64), 1)
    r.read[...] = jnp.sum(
        jnp.where(rows == lanes, r.readout[...], 0.0), axis=1, keepdims=True
    )


def first_layer_centres(ij, depth, sub):
    cx = ((ij >> 2).astype(F32) + 0.5) * 0.25 - 1.0
    cy = ((ij & 3).astype(F32) + 0.5) * 0.5 - 1.0
    cz = (depth.astype(F32) + 0.5) * (2.0 / DEPTH) - 1.0
    part3 = jnp.where(sub >= 3, sub - 3, sub)
    return jnp.where(
        sub >= 6, 1.0, jnp.where(part3 == 0, cx, jnp.where(part3 == 1, cy, cz))
    )


def place_lists(r):
    for i in range(8):
        r.counts[i * 4 : (i + 1) * 4, :] = r.cnt[i].astype(F32)
        r.low[i * 4 : (i + 1) * 4, :] = r.nbr[i]
    spread = nt(r.counts[...].astype(BF), r.sums[...])
    places = (lax.broadcasted_iota(jnp.int32, (COLUMNS, 2048), 1) & 7).astype(F32)
    ids = r.low[...]
    r.high[...] = jnp.where(places < spread, (ids >> 4) & 7, 8)
    r.low[...] = (
        ((ids >> 10) << 7) + (((ids >> 3) & 1) << 6) + (((ids >> 7) & 7) << 3) + (ids & 7)
    )


def encode(r):
    n = 2048 * ENC_COLUMNS

    def columns(step, carry):
        rows = [step * ENC_COLUMNS + k for k in range(ENC_COLUMNS)]
        low = jnp.concatenate([r.low[pl.ds(row, 1), :] for row in rows], 1)
        high = jnp.concatenate([r.high[pl.ds(row, 1), :] for row in rows], 1)
        hot = jnp.where(
            lax.broadcasted_iota(jnp.int32, (256, n), 0) == low, 1.0, 0.0
        ).astype(BF)
        found = mm(r.table[...], hot)
        high8 = jnp.broadcast_to(high, (8, n))
        near = jnp.zeros((8, 8, n), F32)
        for h in range(8):
            part = found[h * 64 : (h + 1) * 64].reshape(8, 8, n)
            near = jnp.where((high8 == h)[None], part, near)
        sub = lax.broadcasted_iota(jnp.int32, (8, n), 0)
        lane = lax.broadcasted_iota(jnp.int32, (8, n), 1)
        place = found[512:536].reshape(3, 8, n)
        place = jnp.where((high8 == sub)[None], place, 0.0).reshape(24, n)
        ij = (lane >> 11) + step * ENC_COLUMNS
        centre = first_layer_centres(ij, (lane & 2047) >> 3, sub)
        stacked = jnp.concatenate([place, place, centre], 0).astype(BF)
        half = mm(r.ew1[...], stacked)
        hidden = (half + half * jnp.tanh(half)).astype(BF)
        kernel = mm(r.ewo[...], hidden)
        shares = (kernel * near.reshape(64, n)).astype(BF)
        for k in range(ENC_COLUMNS):
            row = pl.multiple_of((step * ENC_COLUMNS + k) * 64, 64)
            r.prod[pl.ds(row, 64), :] = shares[:, k * 2048 : (k + 1) * 2048]
        return carry

    lax.fori_loop(0, COLUMNS // ENC_COLUMNS, columns, 0)
    shares = 1.0 / r.counts[...]
    group = 8
    for g in range(COLUMNS // group):
        latent = mm(r.prod[g * group * 64 : (g + 1) * group * 64, :], r.sums[...])
        for k in range(group):
            ij = g * group + k
            r.lat[ij * 64 : (ij + 1) * 64, :] = (
                latent[k * 64 : (k + 1) * 64] * shares[ij : ij + 1]
            ).astype(BF)
    both = nt(r.waves[...], r.lat[...])
    for ij in range(COLUMNS):
        part = both[:, ij * 64 : (ij + 1) * 64]
        r.z_rows[:, ij : ij + 1, :] = jnp.concatenate([part[0:16], part[16:32]], 1).reshape(
            16, 1, 128
        )
    r.z[...] = r.z_rows[...].astype(BF)


def forward_modes(z, r, pairs, recv_a, send_b, recv_b, meanwhile):
    exchange("py", z, recv_a, pairs[0], meanwhile(0))
    u = mm(r.ky[...], recv_a[...].reshape(512, 128))
    send_b[...] = turned(u[:256], u[256:], 1.0).astype(BF).reshape(GROUP, 16, 128)
    exchange("px", send_b, recv_b, pairs[1], meanwhile(1))
    u = mm(r.kx[...], recv_b[...].reshape(256, 128))
    return turned(u[:64], u[64:], 1.0) * SCALING


def own_doubling():
    return jnp.where(lax.axis_index("py") == 0, 1.0, 2.0)


def mixed(modes, weight_ref):
    lanes = lax.broadcasted_iota(jnp.int32, (64, 128), 1)
    swapped = pltpu.roll(modes, CHANNELS, 1)
    real2 = jnp.where(lanes < CHANNELS, modes, swapped)
    imag2 = jnp.where(lanes < CHANNELS, swapped, modes)
    rows4 = lax.broadcasted_iota(jnp.int32, (64, 256), 0) & 3
    keep = (lax.broadcasted_iota(jnp.int32, (64, 256), 1) >> 6) == rows4
    real4 = jnp.where(keep, jnp.concatenate([real2, real2], 1), 0.0)
    imag4 = jnp.where(keep, jnp.concatenate([imag2, imag2], 1), 0.0)
    first = (lax.broadcasted_iota(jnp.int32, (16, 128), 0) & 7) < 4
    out = []
    for h in range(8):
        left = jnp.concatenate([real4[8 * h : 8 * h + 8], imag4[8 * h : 8 * h + 8]], 0)
        left = left.astype(BF)
        lower = mm(left, weight_ref[8 * h : 8 * h + 4].reshape(256, 128))
        upper = mm(left, weight_ref[8 * h + 4 : 8 * h + 8].reshape(256, 128))
        both = jnp.where(first, lower, upper)
        out.append(turned(both[0:8], both[8:16], -1.0))
    return jnp.concatenate(out, 0)


def fourier(r, meanwhile):
    modes = forward_modes(
        r.z, r, ((r.s3, r.r3), (r.s4, r.r4)), r.recv_a, r.send_b, r.recv_b, meanwhile
    )
    r.modes[...] = modes
    v = mixed(modes, r.weight) * (own_doubling() * SCALING)
    u = mm(r.kxi[...], v.astype(BF))
    r.send_c[...] = turned(u[:256], u[256:], -1.0).astype(BF).reshape(GROUP, 16, 128)
    exchange("px", r.send_c, r.recv_c, (r.s5, r.r5), meanwhile(2))
    u = mm(r.kyi[...], r.recv_c[...].reshape(256, 128))
    r.send_d[...] = turned(u[:512], u[512:], -1.0).astype(BF).reshape(GROUP, COLUMNS, 128)
    exchange("py", r.send_d, r.recv_d, (r.s6, r.r6), meanwhile(3))


def depth_basis(r):
    n = PREP

    def block(step, carry):
        here = pl.ds(pl.multiple_of(step * n, n), n)
        cells = r.lists[:, here]
        low, column = cells & 255, cells >> 8
        hot = jnp.where(
            lax.broadcasted_iota(jnp.int32, (256, n), 0) == low, 1.0, 0.0
        ).astype(BF)
        tw = mm(r.waves[...], hot)
        match = lax.broadcasted_iota(jnp.int32, (COLUMNS, n), 0) == column
        for q in range(32):
            r.basis[q * 32 : (q + 1) * 32, here] = jnp.where(match, tw[q : q + 1], 0.0).astype(BF)
        return carry

    lax.fori_loop(0, 4 * SLOT_TOTAL // n, block, 0)


def prepare(r, first, last):
    n = PREP

    def block(step, carry):
        off = pl.multiple_of(step * n, n)
        half_block = step & 1
        expanded = nt(
            r.extra[step >> 1].astype(BF),
            r.pairs[pl.ds(pl.multiple_of(half_block * n, n), n), :],
        )
        cells = r.lists[:, pl.ds(off, n)]
        low, column = cells & 255, cells >> 8
        hot = jnp.where(
            lax.broadcasted_iota(jnp.int32, (256, n), 0) == low, 1.0, 0.0
        ).astype(BF)
        found = mm(r.lat[...], hot)
        column8 = jnp.broadcast_to(column, (8, n))
        near = jnp.zeros((8, 8, n), F32)
        for k in range(COLUMNS):
            part = found[k * 64 : (k + 1) * 64].reshape(8, 8, n)
            near = jnp.where((column8 == k)[None], part, near)
        r.before[:, pl.ds(off, n)] = mm(r.skip_t[...], near.reshape(64, n).astype(BF))
        sub = lax.broadcasted_iota(jnp.int32, (8, n), 0)
        stacked = jnp.concatenate(
            [expanded, first_layer_centres(column, low, sub)], 0
        ).astype(BF)
        half = mm(r.dw1[...], stacked)
        hidden = (half + half * jnp.tanh(half)).astype(BF)
        r.kern[:, pl.ds(off, n)] = mm(r.dwo[...], hidden) * r.read[...]
        return carry

    lax.fori_loop(first, last, block, 0)


def parts_of(values, parts):
    out, rest = [], values
    for _ in range(parts):
        rounded = rest.astype(BF).astype(F32)
        out.append(rounded)
        rest = rest - rounded
    return jnp.concatenate(out, 0).astype(BF)


def decode(r):
    flipped = nt(identity(128), r.recv_d[...].reshape(512, 128))
    r.back_t[...] = jnp.concatenate([flipped[0:64], flipped[64:128]], 1).astype(BF)
    n = POST

    def forward(step, carry):
        off = pl.multiple_of(step * n, n)
        here = pl.ds(off, n)
        before = mm(r.back_t[...], r.basis[:, here]) + r.before[:, here]
        phi = 0.5 * (1.0 + lax.erf(before * HALF_ROOT))
        slope = phi + before * jnp.exp(-0.5 * before * before) * GAUSS_NORM
        weighed = r.kern[:, here]
        r.kern[:, here] = weighed * slope
        dots = jnp.sum(weighed * (before * phi), axis=0, keepdims=True)
        for k in range(n // 1024):
            r.dots[pl.ds(step * (n // 1024) + k, 1), :] = dots[:, k * 1024 : (k + 1) * 1024]
        return carry

    lax.fori_loop(0, 4 * SLOT_TOTAL // n, forward, 0)
    summed = mm(parts_of(r.dots[...], 3), r.pairs[...])
    summed = summed[0:8] + summed[8:16] + summed[16:24]
    living = r.living[...]
    pred = living * (summed * 0.25)
    for h in range(8):
        r.pred[:, h * 256 : (h + 1) * 256] = pred[h : h + 1]
    residue = living * (pred - r.target[...]) * 0.25
    spread = nt(parts_of(residue, 2), r.pairs[...])
    r.dots[...] = spread[0:8] + spread[8:16]
    n = 4 * 1024
    for step in range(4 * SLOT_TOTAL // n):
        here = slice(step * n, (step + 1) * n)
        rows = [r.dots[k : k + 1] for k in range(step * (n // 1024), (step + 1) * (n // 1024))]
        shares = (r.kern[:, here] * jnp.concatenate(rows, 1)).astype(BF)
        part = nt(r.basis[:, here], shares)
        r.total[...] = part if step == 0 else r.total[...] + part
    out = jnp.concatenate([r.total[0:512], r.total[512:1024]], 1)
    r.grad_z[...] = out.astype(BF).reshape(GROUP, COLUMNS, 128)


WIDE, NARROW, POINT_BLOCK = (GROUP, COLUMNS, 128), (GROUP, 16, 128), (GROUP, 80, 128)
INPUTS = (
    "features", "positions", "targets", "route", "live", "nbr", "cnt", "lists",
    "ein", "ebias", "ewo", "din", "dbias", "dwo", "skip", "readout",
    "waves", "weight_far", "ky_far", "kx_far", "kxi_far", "kyi_far",
)
FETCHED = {
    "weight": (64, 64, 128), "ky": (512, 512), "kx": (128, 256), "kxi": (512, 64),
    "kyi": (1024, 256),
}
OUTPUTS = {
    "pred": ((1, SLOT_TOTAL), F32), "modes": ((64, 128), F32), "grads": ((64, 128), F32),
}
SCRATCH = {
    "send1": (POINT_BLOCK, BF), "recv1": (POINT_BLOCK, BF),
    "send2": (POINT_BLOCK, BF), "recv2": (POINT_BLOCK, BF),
    "regroup": ((GROUP, 8, CAPACITY, 128), F32), "rest": ((GROUP, 8, 128), F32),
    "slot": ((1, POINTS), jnp.int32), "twice": ((128, POINTS), BF),
    "sums": ((2048, 256), BF), "pairs": ((1024, 256), BF), "ew1": ((80, 56), BF), "dw1": ((256, 16), BF), "skip_t": ((64, 64), BF),
    "read": ((64, 1), F32), "counts": ((COLUMNS, DEPTH), F32), "low": ((COLUMNS, 2048), jnp.int32),
    "table": ((544, 256), BF), "pos_rows": ((32, 256), F32),
    "extra": ((8, 8, 256), F32), "target": ((8, 256), F32), "living": ((8, 256), F32),
    "high": ((COLUMNS, 2048), jnp.int32),
    "prod": ((COLUMNS * 64, 2048), BF), "lat": ((COLUMNS * 64, DEPTH), BF),
    "z_rows": (WIDE, F32), "z": (WIDE, BF), "recv_a": (WIDE, BF), "send_b": (NARROW, BF),
    "recv_b": (NARROW, BF), "send_c": (NARROW, BF), "recv_c": (NARROW, BF),
    "send_d": (WIDE, BF), "recv_d": (WIDE, BF),
    "before": ((64, 4 * SLOT_TOTAL), F32), "kern": ((64, 4 * SLOT_TOTAL), F32),
    "basis": ((1024, 4 * SLOT_TOTAL), BF), "back_t": ((64, 1024), BF),
    "dots": ((8, 1024), F32), "total": ((1024, 64), F32),
    "grad_z": (WIDE, BF), "recv_e": (WIDE, BF), "send_f": (NARROW, BF), "recv_f": (NARROW, BF),
    **{name: (shape, BF) for name, shape in FETCHED.items()},
}
EXCHANGES = 8


def step_kernel(*refs):
    names = list(INPUTS) + list(OUTPUTS) + list(SCRATCH)
    for k in range(1, EXCHANGES + 1):
        names += [f"s{k}", f"r{k}"]
    names.append("fetched")
    r = types.SimpleNamespace(**dict(zip(names, refs)))

    def before_points():
        group_sums(r)
        first_layers(r)
        place_lists(r)

    for fetch in fetches(r):
        fetch.start()
    send_points(r, lambda k: before_points if k == 0 else lambda: depth_basis(r))
    slot_tables(r)
    encode(r)
    for fetch in fetches(r):
        fetch.wait()
    blocks = 4 * SLOT_TOTAL // PREP // 4
    fourier(r, lambda k: lambda: prepare(r, k * blocks, (k + 1) * blocks))
    decode(r)
    grads = forward_modes(
        r.grad_z, r, ((r.s7, r.r7), (r.s8, r.r8)), r.recv_e, r.send_f, r.recv_f,
        lambda k: None,
    )
    r.grads[...] = grads * own_doubling()


def step(*inputs):
    whole = pl.BlockSpec(memory_space=pltpu.VMEM)
    in_specs = [whole] * len(INPUTS)
    in_specs[INPUTS.index("live")] = pl.BlockSpec(memory_space=pltpu.SMEM)
    for name in FETCHED:
        in_specs[INPUTS.index(name + "_far")] = pl.BlockSpec(memory_space=pl.ANY)
    semaphores = [pltpu.SemaphoreType.DMA((GROUP,))] * (2 * EXCHANGES)
    semaphores.append(pltpu.SemaphoreType.DMA((len(FETCHED),)))
    return pl.pallas_call(
        step_kernel,
        out_shape=tuple(jax.ShapeDtypeStruct(*v) for v in OUTPUTS.values()),
        in_specs=in_specs,
        out_specs=(whole,) * len(OUTPUTS),
        scratch_shapes=[pltpu.VMEM(*v) for v in SCRATCH.values()] + semaphores,
        compiler_params=pltpu.CompilerParams(
            collective_id=0, has_side_effects=True, vmem_limit_bytes=VMEM_LIMIT
        ),
        name="training_step",
    )(*inputs)


def outer_kernel(modes_ref, grad_ref, out_ref):
    modes_t = modes_ref[...].T
    grads = grad_ref[...]
    swapped = pltpu.roll(grads, CHANNELS, 1) * lane_sign(grads.shape)
    for m in range(OUTER):
        out_ref[m] = (
            modes_t[0:64, m : m + 1] * grads[m : m + 1]
            + modes_t[64:128, m : m + 1] * swapped[m : m + 1]
        )


def outer(modes, grads):
    return pl.pallas_call(
        outer_kernel,
        grid=(64 // OUTER,),
        out_shape=jax.ShapeDtypeStruct((64, 64, 128), F32),
        in_specs=[pl.BlockSpec((OUTER, 128), lambda i: (i, 0))] * 2,
        out_specs=pl.BlockSpec((OUTER, 64, 128), lambda i: (i, 0, 0)),
        compiler_params=pltpu.CompilerParams(vmem_limit_bytes=VMEM_LIMIT),
        name="outer",
    )(modes, grads)


def body(
    point_features, positions, targets, routes, live_counts, cell_neighbours, cell_counts,
    slot_neighbours, encoder_in, encoder_bias, encoder_out, decoder_in, decoder_bias,
    decoder_out, skip_weight, spectral_weight, readout_weight,
):
    pred, modes, grads = step(
        point_features.T, positions.T, targets.reshape(8, 128), routes.reshape(1, POINTS), live_counts,
        cell_neighbours, cell_counts, slot_neighbours,
        encoder_in, encoder_bias[None], encoder_out.T,
        decoder_in, decoder_bias[None], decoder_out.T, skip_weight, readout_weight[None],
        jnp.asarray(depth_waves()), spectral_weight.reshape(64, 64, 128),
        jnp.asarray(kron_forward_y()), jnp.asarray(kron_forward_x()),
        jnp.asarray(kron_inverse_x()), jnp.asarray(kron_inverse_y()),
    )
    return pred, outer(modes, grads).reshape(32, 2, 1, 64, 128)


def solution(mesh):
    in_specs = (
        P(("px", "py"), None), P(("px", "py"), None), P(("px", "py")), P(("px", "py"), None),
        P(("px", "py")), P("px", "py", None), P("px", "py", None), P(("px", "py"), None),
        P(), P(), P(), P(), P(), P(), P(),
        P(None, "px", "py", None, None), P(),
    )
    out_specs = (P(("px", "py"), None), P(None, "px", "py", None, None))
    return jax.shard_map(body, mesh=mesh, in_specs=in_specs, out_specs=out_specs, check_vma=False)
```

```python
import math
import types

import jax
import jax.numpy as jnp
import numpy as np
from jax import lax
from jax.experimental import pallas as pl
from jax.experimental.pallas import tpu as pltpu
from jax.sharding import PartitionSpec as P

MESH = pl.DeviceIdType.MESH
HALF_ROOT = 0.7071067811865476
GAUSS_NORM = 0.3989422804014327
BF = jnp.bfloat16
F32 = jnp.float32
GROUP = 16
CHANNELS = 64
COLUMNS = 32
DEPTH = 256
CAPACITY = 8
SLOT_TOTAL = 2048
POINTS = 1024
SCALING = 1.0 / math.sqrt(128 * 64 * 256)
VMEM_LIMIT = 60 * 1024 * 1024
ENC_COLUMNS = 2
PREP = 512
OUTER = 16
POST = 2048


def frequencies():
    counted = np.arange(32)
    return np.where(counted < 16, counted, counted - 32)


def wave(length, positions, frequency):
    angles = 2.0 * np.pi * ((positions[:, None] * frequency[None, :]) % length) / length
    return np.cos(angles), np.sin(angles)


def bf16_of(array):
    return np.asarray(array, np.float32).astype(BF)


def kron_forward_y():
    cos, sin = wave(64, np.arange(64), frequencies())
    out = []
    for part in (cos, sin):
        w = part.reshape(16, 4, 16, 2)
        full = np.einsum("cjdp,ik->dpicjk", w, np.eye(8)).transpose(0, 1, 2, 3, 5, 4)
        out.append(full.reshape(256, 512))
    return bf16_of(np.concatenate(out))


def kron_forward_x():
    cos, sin = wave(128, np.arange(128), frequencies())
    out = []
    for part in (cos, sin):
        w = part.reshape(16, 8, 32)
        full = np.einsum("air,ps->rpasi", w, np.eye(2))
        out.append(full.reshape(64, 256))
    return bf16_of(np.concatenate(out))


def kron_inverse_x():
    cos, sin = wave(128, np.arange(128), frequencies())
    out = []
    for part in (cos, sin):
        w = part.reshape(16, 8, 32)
        full = np.einsum("air,ps->apirs", w, np.eye(2))
        out.append(full.reshape(256, 64))
    return bf16_of(np.concatenate(out))


def kron_inverse_y():
    cos, sin = wave(64, np.arange(64), frequencies())
    out = []
    for part in (cos, sin):
        w = part.reshape(16, 4, 16, 2)
        full = np.einsum("cjdp,ik->cijdpk", w, np.eye(8))
        out.append(full.reshape(512, 256))
    return bf16_of(np.concatenate(out))


def depth_waves():
    cos, sin = wave(256, np.arange(16), np.arange(256))
    return bf16_of(np.concatenate([cos, -sin]))


def nt(left, right):
    return lax.dot_general(left, right, (((1,), (1,)), ((), ())), preferred_element_type=F32)


def mm(left, right):
    return jnp.dot(left, right, preferred_element_type=F32)


def identity(n):
    rows = lax.broadcasted_iota(jnp.int32, (n, n), 0)
    lanes = lax.broadcasted_iota(jnp.int32, (n, n), 1)
    return jnp.where(rows == lanes, 1.0, 0.0).astype(BF)


def lane_sign(shape):
    lanes = lax.broadcasted_iota(jnp.int32, shape, 1)
    return jnp.where(lanes < CHANNELS, 1.0, -1.0)


def turned(cos_part, sin_part, direction):
    swapped = pltpu.roll(sin_part, CHANNELS, 1)
    return cos_part + swapped * (lane_sign(swapped.shape) * direction)


def others():
    a, c = lax.axis_index("px"), lax.axis_index("py")
    return a, c


def greet():
    a, c = others()
    barrier = pltpu.get_barrier_semaphore()

    def greeting(d, carry):
        pl.semaphore_signal(barrier, inc=1, device_id=((a + d) & 15, c), device_id_type=MESH)
        pl.semaphore_signal(barrier, inc=1, device_id=(a, (c + d) & 15), device_id_type=MESH)
        return carry

    lax.fori_loop(1, GROUP, greeting, 0)


def greeted():
    pl.semaphore_wait(pltpu.get_barrier_semaphore(), 2 * (GROUP - 1))


def copy_to(axis, d, send, recv, send_sem, recv_sem):
    a, c = others()
    me = a if axis == "px" else c
    peer = (me + d) & 15
    return pltpu.make_async_remote_copy(
        src_ref=send.at[peer],
        dst_ref=recv.at[me],
        send_sem=send_sem.at[d],
        recv_sem=recv_sem.at[me],
        device_id=(peer, c) if axis == "px" else (a, peer),
        device_id_type=MESH,
    )


def start_all(axis, send, recv, send_sem, recv_sem):
    def start(d, carry):
        copy_to(axis, d, send, recv, send_sem, recv_sem).start()
        return carry

    lax.fori_loop(1, GROUP, start, 0)


def finish(axis, send, recv, send_sem, recv_sem):
    me = lax.axis_index(axis)
    recv[me] = send[me]

    def arrival(d, carry):
        copy_to(axis, d, send, recv, send_sem, recv_sem).wait_send()
        source = (me - d) & 15
        pltpu.make_async_remote_copy(
            src_ref=send.at[source],
            dst_ref=recv.at[source],
            send_sem=send_sem.at[d],
            recv_sem=recv_sem.at[source],
            device_id=others(),
            device_id_type=MESH,
        ).wait_recv()
        return carry

    lax.fori_loop(1, GROUP, arrival, 0)


def exchange(axis, send, recv, pair, meanwhile=None):
    start_all(axis, send, recv, *pair)
    if meanwhile is not None:
        meanwhile()
    finish(axis, send, recv, *pair)


def pick_rows(rows, sub):
    out = jnp.zeros(sub.shape, F32)
    for k, row in enumerate(rows):
        out = jnp.where(sub == k, row, out)
    return out


def send_points(r, meanwhile):
    greet()
    live = r.live[0]
    lanes = lax.broadcasted_iota(jnp.int32, (1, POINTS), 1)
    target = jnp.where(lanes < live, r.route[...], 256)
    owners = lax.broadcasted_iota(jnp.int32, (256, POINTS), 0)
    named = jnp.where(owners == target, 1.0, 0.0)
    earlier = jnp.where(
        lax.broadcasted_iota(jnp.int32, (POINTS, POINTS), 0)
        < lax.broadcasted_iota(jnp.int32, (POINTS, POINTS), 1),
        1.0,
        0.0,
    ).astype(BF)
    counted = mm(named.astype(BF), earlier)
    rank = jnp.sum(named * counted, axis=0, keepdims=True).astype(jnp.int32)
    kept = target < 256
    r.slot[...] = jnp.where(kept, target * CAPACITY + rank, -1)
    features = r.features[...]
    r.twice[...] = jnp.concatenate([features, features], 0)
    sub = lax.broadcasted_iota(jnp.int32, (8, POINTS), 0)
    places = r.positions[...].astype(F32)
    wanted = r.targets[...].astype(F32)
    wanted = jnp.concatenate([wanted[k : k + 1] for k in range(8)], 1)
    rest = pick_rows([places[0:1], places[1:2], places[2:3], wanted, 1.0], sub)
    rows = lax.broadcasted_iota(jnp.int32, (128, POINTS), 0)
    spread = jnp.where((rows >> 3) == (target & 15), jnp.concatenate([rest] * 16, 0), 0.0)
    mine = jnp.where(kept, (target >> 4) * CAPACITY + rank, -1)
    hot = jnp.where(rows == mine, 1.0, 0.0).astype(BF)
    r.rest[...] = nt(hot, spread.astype(BF)).reshape(GROUP, 8, 128)
    greeted()
    a = lax.axis_index("px")
    low_lanes = lax.broadcasted_iota(jnp.int32, (64, 128), 1) < 64
    nothing = jnp.zeros((8, 128), F32)

    def pack(step, carry):
        group = ((a >> 2) + 2 + step) & 3
        at = lax.broadcasted_iota(jnp.int32, (512, POINTS), 0) + group * 512
        hot = jnp.where(at == r.slot[...], 1.0, 0.0).astype(BF)
        packed = nt(hot, r.twice[...])
        for k in range(4):
            peer = group * 4 + k
            block = packed[k * 128 : (k + 1) * 128]
            r.send1[peer, 0:64] = jnp.where(low_lanes, block[0:64], block[64:128]).astype(BF)
            r.send1[peer, 64:80] = jnp.concatenate([r.rest[peer], nothing], 0).astype(BF)

            @pl.when(peer != a)
            def _():
                copy_to("px", (peer - a) & 15, r.send1, r.recv1, r.s1, r.r1).start()

        return carry

    lax.fori_loop(0, 4, pack, 0)
    meanwhile(0)()
    finish("px", r.send1, r.recv1, r.s1, r.r1)
    for source in range(GROUP):
        r.regroup[source] = r.recv1[source, 0:64].astype(F32).reshape(8, CAPACITY, 128)
        r.rest[source] = r.recv1[source, 64:80].astype(F32)[0:8]
    eye = identity(128)
    rest = nt(eye, r.rest[...].reshape(128, 128).astype(BF))
    for c in range(8):
        first = r.regroup[0:8, c].reshape(64, 128)
        second = r.regroup[8:16, c].reshape(64, 128)
        r.send2[c, 0:64] = jnp.where(
            low_lanes, first, pltpu.roll(second, 64, 1)
        ).astype(BF)
        r.send2[c + 8, 0:64] = jnp.where(
            low_lanes, pltpu.roll(first, 64, 1), second
        ).astype(BF)
    for c in range(GROUP):
        r.send2[c, 64:80] = jnp.concatenate([rest[c * 8 : c * 8 + 8], nothing], 0).astype(BF)
    exchange("py", r.send2, r.recv2, (r.s2, r.r2), meanwhile(1))


def slot_tables(r):
    eye = identity(128)
    low_lanes = lax.broadcasted_iota(jnp.int32, (8, 128), 1) < 64
    r.pos_rows[...] = jnp.zeros(r.pos_rows.shape, F32)
    for h in range(8):
        rows = jnp.concatenate([r.recv2[2 * h, 0:64], r.recv2[2 * h + 1, 0:64]], 0)
        flipped = nt(eye, rows).astype(BF)
        r.table[h * 64 : (h + 1) * 64, 0:128] = flipped[0:64]
        r.table[h * 64 : (h + 1) * 64, 128:256] = flipped[64:128]
        even = r.recv2[2 * h, 64:80].astype(F32)[0:8]
        odd = r.recv2[2 * h + 1, 64:80].astype(F32)[0:8]
        r.rest[2 * h] = even
        r.rest[2 * h + 1] = odd
        left = jnp.where(low_lanes, even, pltpu.roll(odd, 64, 1))
        right = jnp.where(low_lanes, pltpu.roll(even, 64, 1), odd)
        for d in range(3):
            r.pos_rows[d * 8 + h : d * 8 + h + 1, 0:128] = left[d : d + 1]
            r.pos_rows[d * 8 + h : d * 8 + h + 1, 128:256] = right[d : d + 1]
    r.table[512:544, :] = r.pos_rows[...].astype(BF)
    by_slot = nt(eye, r.rest[...].reshape(128, 128).astype(BF))
    rows = lax.broadcasted_iota(jnp.int32, (128, 128), 0)
    lanes = lax.broadcasted_iota(jnp.int32, (128, 128), 1)
    same = (rows >> 3) == (lanes >> 3)
    sub = lax.broadcasted_iota(jnp.int32, (8, 128), 0)
    part = lax.broadcasted_iota(jnp.int32, (8, 128), 1) & 7
    wanted = jnp.where(sub < 3, sub, sub - 3)
    chooser = jnp.where(part == wanted, 1.0, 0.0).astype(BF)
    for a in range(GROUP):
        spread = jnp.concatenate([by_slot[a * 8 : a * 8 + 8]] * 16, 0)
        extra = nt(chooser, jnp.where(same, spread, 0.0).astype(BF))
        h, half = a // 2, (a % 2) * 128
        r.extra[h, :, half : half + 128] = extra
        r.target[h : h + 1, half : half + 128] = extra[6:7]
        r.living[h : h + 1, half : half + 128] = extra[7:8]


def fetches(r):
    return [
        pltpu.make_async_copy(getattr(r, name + "_far"), getattr(r, name), r.fetched.at[k])
        for k, name in enumerate(FETCHED)
    ]


def group_sums(r):
    for ref, shift in ((r.sums, 3), (r.pairs, 2)):
        rows = lax.broadcasted_iota(jnp.int32, ref.shape, 0)
        lanes = lax.broadcasted_iota(jnp.int32, ref.shape, 1)
        ref[...] = jnp.where((rows >> shift) == lanes, 1.0, 0.0).astype(BF)


def first_layers(r):
    def halves(values):
        high = (values * 0.5).astype(BF).astype(F32)
        return high, values * 0.5 - high

    high, low = halves(r.ein[...])
    bias_high, bias_low = halves(r.ebias[...])
    sub = lax.broadcasted_iota(jnp.int32, (8, 80), 0)
    rows = [jnp.broadcast_to(part[d : d + 1], (8, 80)) for part in (high, low) for d in range(3)]
    rows.append(
        pick_rows(
            [-part[d : d + 1] for part in (high, low) for d in range(3)] + [bias_high, bias_low],
            sub,
        )
    )
    r.ew1[...] = nt(identity(80), jnp.concatenate(rows, 0).astype(BF)).astype(BF)
    high, low = halves(r.din[...])
    bias_high, bias_low = halves(r.dbias[...])
    sub = lax.broadcasted_iota(jnp.int32, (8, 256), 0)
    positive = [part[d : d + 1] for part in (high, low) for d in range(3)]
    negative = [-row for row in positive] + [bias_high, bias_low]
    rows = jnp.concatenate([pick_rows(positive, sub), pick_rows(negative, sub)], 0)
    r.dw1[...] = nt(identity(256), rows.astype(BF)).astype(BF)
    r.skip_t[...] = nt(identity(64), r.skip[...]).astype(BF)
    rows = lax.broadcasted_iota(jnp.int32, (64, 64), 0)
    lanes = lax.broadcasted_iota(jnp.int32, (64, 64), 1)
    r.read[...] = jnp.sum(
        jnp.where(rows == lanes, r.readout[...], 0.0), axis=1, keepdims=True
    )


def first_layer_centres(ij, depth, sub):
    cx = ((ij >> 2).astype(F32) + 0.5) * 0.25 - 1.0
    cy = ((ij & 3).astype(F32) + 0.5) * 0.5 - 1.0
    cz = (depth.astype(F32) + 0.5) * (2.0 / DEPTH) - 1.0
    part3 = jnp.where(sub >= 3, sub - 3, sub)
    return jnp.where(
        sub >= 6, 1.0, jnp.where(part3 == 0, cx, jnp.where(part3 == 1, cy, cz))
    )


def place_lists(r):
    for i in range(8):
        r.counts[i * 4 : (i + 1) * 4, :] = r.cnt[i].astype(F32)
        r.low[i * 4 : (i + 1) * 4, :] = r.nbr[i]
    spread = nt(r.counts[...].astype(BF), r.sums[...])
    places = (lax.broadcasted_iota(jnp.int32, (COLUMNS, 2048), 1) & 7).astype(F32)
    ids = r.low[...]
    r.high[...] = jnp.where(places < spread, (ids >> 4) & 7, 8)
    r.low[...] = (
        ((ids >> 10) << 7) + (((ids >> 3) & 1) << 6) + (((ids >> 7) & 7) << 3) + (ids & 7)
    )


def encode(r):
    n = 2048 * ENC_COLUMNS

    def columns(step, carry):
        rows = [step * ENC_COLUMNS + k for k in range(ENC_COLUMNS)]
        low = jnp.concatenate([r.low[pl.ds(row, 1), :] for row in rows], 1)
        high = jnp.concatenate([r.high[pl.ds(row, 1), :] for row in rows], 1)
        hot = jnp.where(
            lax.broadcasted_iota(jnp.int32, (256, n), 0) == low, 1.0, 0.0
        ).astype(BF)
        found = mm(r.table[...], hot)
        high8 = jnp.broadcast_to(high, (8, n))
        near = jnp.zeros((8, 8, n), F32)
        for h in range(8):
            part = found[h * 64 : (h + 1) * 64].reshape(8, 8, n)
            near = jnp.where((high8 == h)[None], part, near)
        sub = lax.broadcasted_iota(jnp.int32, (8, n), 0)
        lane = lax.broadcasted_iota(jnp.int32, (8, n), 1)
        place = found[512:536].reshape(3, 8, n)
        place = jnp.where((high8 == sub)[None], place, 0.0).reshape(24, n)
        ij = (lane >> 11) + step * ENC_COLUMNS
        centre = first_layer_centres(ij, (lane & 2047) >> 3, sub)
        stacked = jnp.concatenate([place, place, centre], 0).astype(BF)
        half = mm(r.ew1[...], stacked)
        hidden = (half + half * jnp.tanh(half)).astype(BF)
        kernel = mm(r.ewo[...], hidden)
        shares = (kernel * near.reshape(64, n)).astype(BF)
        for k in range(ENC_COLUMNS):
            row = pl.multiple_of((step * ENC_COLUMNS + k) * 64, 64)
            r.prod[pl.ds(row, 64), :] = shares[:, k * 2048 : (k + 1) * 2048]
        return carry

    lax.fori_loop(0, COLUMNS // ENC_COLUMNS, columns, 0, unroll=2)
    shares = 1.0 / r.counts[...]
    group = 8
    for g in range(COLUMNS // group):
        latent = mm(r.prod[g * group * 64 : (g + 1) * group * 64, :], r.sums[...])
        for k in range(group):
            ij = g * group + k
            r.lat[ij * 64 : (ij + 1) * 64, :] = (
                latent[k * 64 : (k + 1) * 64] * shares[ij : ij + 1]
            ).astype(BF)
    both = nt(r.waves[...], r.lat[...])
    for ij in range(COLUMNS):
        part = both[:, ij * 64 : (ij + 1) * 64]
        r.z_rows[:, ij : ij + 1, :] = jnp.concatenate([part[0:16], part[16:32]], 1).reshape(
            16, 1, 128
        )
    r.z[...] = r.z_rows[...].astype(BF)


def forward_modes(z, r, pairs, recv_a, send_b, recv_b, meanwhile):
    meanwhile(0)()
    finish("py", z, recv_a, *pairs[0])
    u = mm(r.ky[...], recv_a[...].reshape(512, 128))
    send_b[...] = turned(u[:256], u[256:], 1.0).astype(BF).reshape(GROUP, 16, 128)
    exchange("px", send_b, recv_b, pairs[1], meanwhile(1))
    u = mm(r.kx[...], recv_b[...].reshape(256, 128))
    return turned(u[:64], u[64:], 1.0) * SCALING


def own_doubling():
    return jnp.where(lax.axis_index("py") == 0, 1.0, 2.0)


def mixed(modes, weight_ref):
    lanes = lax.broadcasted_iota(jnp.int32, (64, 128), 1)
    swapped = pltpu.roll(modes, CHANNELS, 1)
    real2 = jnp.where(lanes < CHANNELS, modes, swapped)
    imag2 = jnp.where(lanes < CHANNELS, swapped, modes)
    rows4 = lax.broadcasted_iota(jnp.int32, (64, 256), 0) & 3
    keep = (lax.broadcasted_iota(jnp.int32, (64, 256), 1) >> 6) == rows4
    real4 = jnp.where(keep, jnp.concatenate([real2, real2], 1), 0.0)
    imag4 = jnp.where(keep, jnp.concatenate([imag2, imag2], 1), 0.0)
    first = (lax.broadcasted_iota(jnp.int32, (16, 128), 0) & 7) < 4
    out = []
    for h in range(8):
        left = jnp.concatenate([real4[8 * h : 8 * h + 8], imag4[8 * h : 8 * h + 8]], 0)
        left = left.astype(BF)
        lower = mm(left, weight_ref[8 * h : 8 * h + 4].reshape(256, 128))
        upper = mm(left, weight_ref[8 * h + 4 : 8 * h + 8].reshape(256, 128))
        both = jnp.where(first, lower, upper)
        out.append(turned(both[0:8], both[8:16], -1.0))
    return jnp.concatenate(out, 0)


def fourier(r, meanwhile):
    start_all("py", r.z, r.recv_a, r.s3, r.r3)
    modes = forward_modes(
        r.z, r, ((r.s3, r.r3), (r.s4, r.r4)), r.recv_a, r.send_b, r.recv_b, meanwhile
    )
    r.modes[...] = modes
    v = mixed(modes, r.weight) * (own_doubling() * SCALING)
    u = mm(r.kxi[...], v.astype(BF))
    r.send_c[...] = turned(u[:256], u[256:], -1.0).astype(BF).reshape(GROUP, 16, 128)
    exchange("px", r.send_c, r.recv_c, (r.s5, r.r5), meanwhile(2))
    u = mm(r.kyi[...], r.recv_c[...].reshape(256, 128))
    r.send_d[...] = turned(u[:512], u[512:], -1.0).astype(BF).reshape(GROUP, COLUMNS, 128)
    exchange("py", r.send_d, r.recv_d, (r.s6, r.r6), meanwhile(3))


def depth_basis(r):
    n = PREP

    def block(step, carry):
        here = pl.ds(pl.multiple_of(step * n, n), n)
        cells = r.lists[:, here]
        low, column = cells & 255, cells >> 8
        hot = jnp.where(
            lax.broadcasted_iota(jnp.int32, (256, n), 0) == low, 1.0, 0.0
        ).astype(BF)
        tw = mm(r.waves[...], hot)
        match = lax.broadcasted_iota(jnp.int32, (COLUMNS, n), 0) == column
        for q in range(32):
            r.basis[q * 32 : (q + 1) * 32, here] = jnp.where(match, tw[q : q + 1], 0.0).astype(BF)
        return carry

    lax.fori_loop(0, 4 * SLOT_TOTAL // n, block, 0)


def prepare(r, first, last):
    n = PREP

    def block(step, carry):
        off = pl.multiple_of(step * n, n)
        half_block = step & 1
        expanded = nt(
            r.extra[step >> 1].astype(BF),
            r.pairs[pl.ds(pl.multiple_of(half_block * n, n), n), :],
        )
        cells = r.lists[:, pl.ds(off, n)]
        low, column = cells & 255, cells >> 8
        hot = jnp.where(
            lax.broadcasted_iota(jnp.int32, (256, n), 0) == low, 1.0, 0.0
        ).astype(BF)
        found = mm(r.lat[...], hot)
        column8 = jnp.broadcast_to(column, (8, n))
        near = jnp.zeros((8, 8, n), F32)
        for k in range(COLUMNS):
            part = found[k * 64 : (k + 1) * 64].reshape(8, 8, n)
            near = jnp.where((column8 == k)[None], part, near)
        r.before[:, pl.ds(off, n)] = mm(r.skip_t[...], near.reshape(64, n).astype(BF))
        sub = lax.broadcasted_iota(jnp.int32, (8, n), 0)
        stacked = jnp.concatenate(
            [expanded, first_layer_centres(column, low, sub)], 0
        ).astype(BF)
        half = mm(r.dw1[...], stacked)
        hidden = (half + half * jnp.tanh(half)).astype(BF)
        r.kern[:, pl.ds(off, n)] = mm(r.dwo[...], hidden) * r.read[...]
        return carry

    lax.fori_loop(first, last, block, 0)


def parts_of(values, parts):
    out, rest = [], values
    for _ in range(parts):
        rounded = rest.astype(BF).astype(F32)
        out.append(rounded)
        rest = rest - rounded
    return jnp.concatenate(out, 0).astype(BF)


def decode(r):
    flipped = nt(identity(128), r.recv_d[...].reshape(512, 128))
    r.back_t[...] = jnp.concatenate([flipped[0:64], flipped[64:128]], 1).astype(BF)
    n = POST

    def forward(step, carry):
        off = pl.multiple_of(step * n, n)
        here = pl.ds(off, n)
        before = mm(r.back_t[...], r.basis[:, here]) + r.before[:, here]
        phi = 0.5 * (1.0 + lax.erf(before * HALF_ROOT))
        slope = phi + before * jnp.exp(-0.5 * before * before) * GAUSS_NORM
        weighed = r.kern[:, here]
        r.kern[:, here] = weighed * slope
        dots = jnp.sum(weighed * (before * phi), axis=0, keepdims=True)
        for k in range(n // 1024):
            r.dots[pl.ds(step * (n // 1024) + k, 1), :] = dots[:, k * 1024 : (k + 1) * 1024]
        return carry

    lax.fori_loop(0, 4 * SLOT_TOTAL // n, forward, 0)
    summed = mm(parts_of(r.dots[...], 3), r.pairs[...])
    summed = summed[0:8] + summed[8:16] + summed[16:24]
    living = r.living[...]
    pred = living * (summed * 0.25)
    for h in range(8):
        r.pred[:, h * 256 : (h + 1) * 256] = pred[h : h + 1]
    residue = living * (pred - r.target[...]) * 0.25
    spread = nt(parts_of(residue, 2), r.pairs[...])
    r.dots[...] = spread[0:8] + spread[8:16]
    for h in range(8):
        here = slice(h * 1024, (h + 1) * 1024)
        r.shares[:, here] = (r.kern[:, here] * r.dots[h : h + 1]).astype(BF)


def gradient_depth_modes(r):
    me = lax.axis_index("py")
    n = 4 * 1024

    def half(first):
        depths = [(me + first + k) & 15 for k in range(8)]
        starts = [pl.multiple_of(part * 512 + q * 32, 32) for part in range(2) for q in depths]
        for step in range(4 * SLOT_TOTAL // n):
            here = slice(step * n, (step + 1) * n)
            waves = jnp.concatenate([r.basis[pl.ds(start, 32), here] for start in starts], 0)
            part = nt(waves, r.shares[:, here])
            r.total[...] = part if step == 0 else r.total[...] + part
        for k, q in enumerate(depths):
            real, imag = (r.total[256 * p + k * 32 : 256 * p + k * 32 + 32] for p in range(2))
            r.grad_z[q] = jnp.concatenate([real, imag], 1).astype(BF)

    def send(first, last):
        def start(d, carry):
            copy_to("py", d, r.grad_z, r.recv_e, r.s7, r.r7).start()
            return carry

        lax.fori_loop(first, last, start, 0)

    half(4)
    send(4, 12)
    half(12)
    send(12, 16)
    send(1, 4)


WIDE, NARROW, POINT_BLOCK = (GROUP, COLUMNS, 128), (GROUP, 16, 128), (GROUP, 80, 128)
INPUTS = (
    "features", "positions", "targets", "route", "live", "nbr", "cnt", "lists",
    "ein", "ebias", "ewo", "din", "dbias", "dwo", "skip", "readout",
    "waves", "weight_far", "ky_far", "kx_far", "kxi_far", "kyi_far",
)
FETCHED = {
    "weight": (64, 64, 128), "ky": (512, 512), "kx": (128, 256), "kxi": (512, 64),
    "kyi": (1024, 256),
}
OUTPUTS = {
    "pred": ((1, SLOT_TOTAL), F32), "modes": ((64, 128), F32), "grads": ((64, 128), F32),
}
SCRATCH = {
    "send1": (POINT_BLOCK, BF), "recv1": (POINT_BLOCK, BF),
    "send2": (POINT_BLOCK, BF), "recv2": (POINT_BLOCK, BF),
    "regroup": ((GROUP, 8, CAPACITY, 128), F32), "rest": ((GROUP, 8, 128), F32),
    "slot": ((1, POINTS), jnp.int32), "twice": ((128, POINTS), BF),
    "sums": ((2048, 256), BF), "pairs": ((1024, 256), BF), "ew1": ((80, 56), BF), "dw1": ((256, 16), BF), "skip_t": ((64, 64), BF),
    "read": ((64, 1), F32), "counts": ((COLUMNS, DEPTH), F32), "low": ((COLUMNS, 2048), jnp.int32),
    "table": ((544, 256), BF), "pos_rows": ((32, 256), F32),
    "extra": ((8, 8, 256), F32), "target": ((8, 256), F32), "living": ((8, 256), F32),
    "high": ((COLUMNS, 2048), jnp.int32),
    "prod": ((COLUMNS * 64, 2048), BF), "lat": ((COLUMNS * 64, DEPTH), BF),
    "z_rows": (WIDE, F32), "z": (WIDE, BF), "recv_a": (WIDE, BF), "send_b": (NARROW, BF),
    "recv_b": (NARROW, BF), "send_c": (NARROW, BF), "recv_c": (NARROW, BF),
    "send_d": (WIDE, BF), "recv_d": (WIDE, BF),
    "before": ((64, 4 * SLOT_TOTAL), F32), "kern": ((64, 4 * SLOT_TOTAL), F32),
    "basis": ((1024, 4 * SLOT_TOTAL), BF), "back_t": ((64, 1024), BF),
    "dots": ((8, 1024), F32), "total": ((512, 64), F32), "shares": ((64, 4 * SLOT_TOTAL), BF),
    "grad_z": (WIDE, BF), "recv_e": (WIDE, BF), "send_f": (NARROW, BF), "recv_f": (NARROW, BF),
    **{name: (shape, BF) for name, shape in FETCHED.items()},
}
EXCHANGES = 8


def step_kernel(*refs):
    names = list(INPUTS) + list(OUTPUTS) + list(SCRATCH)
    for k in range(1, EXCHANGES + 1):
        names += [f"s{k}", f"r{k}"]
    names.append("fetched")
    r = types.SimpleNamespace(**dict(zip(names, refs)))

    def before_points():
        group_sums(r)
        first_layers(r)
        place_lists(r)

    for fetch in fetches(r):
        fetch.start()
    send_points(r, lambda k: before_points if k == 0 else lambda: depth_basis(r))
    slot_tables(r)
    encode(r)
    for fetch in fetches(r):
        fetch.wait()
    blocks = 4 * SLOT_TOTAL // PREP // 4
    fourier(r, lambda k: lambda: prepare(r, k * blocks, (k + 1) * blocks))
    decode(r)
    gradient_depth_modes(r)
    grads = forward_modes(
        r.grad_z, r, ((r.s7, r.r7), (r.s8, r.r8)), r.recv_e, r.send_f, r.recv_f,
        lambda k: lambda: None,
    )
    r.grads[...] = grads * own_doubling()


def step(*inputs):
    whole = pl.BlockSpec(memory_space=pltpu.VMEM)
    in_specs = [whole] * len(INPUTS)
    in_specs[INPUTS.index("live")] = pl.BlockSpec(memory_space=pltpu.SMEM)
    for name in FETCHED:
        in_specs[INPUTS.index(name + "_far")] = pl.BlockSpec(memory_space=pl.ANY)
    semaphores = [pltpu.SemaphoreType.DMA((GROUP,))] * (2 * EXCHANGES)
    semaphores.append(pltpu.SemaphoreType.DMA((len(FETCHED),)))
    return pl.pallas_call(
        step_kernel,
        out_shape=tuple(jax.ShapeDtypeStruct(*v) for v in OUTPUTS.values()),
        in_specs=in_specs,
        out_specs=(whole,) * len(OUTPUTS),
        scratch_shapes=[pltpu.VMEM(*v) for v in SCRATCH.values()] + semaphores,
        compiler_params=pltpu.CompilerParams(
            collective_id=0, has_side_effects=True, vmem_limit_bytes=VMEM_LIMIT
        ),
        name="training_step",
    )(*inputs)


def outer_kernel(modes_ref, grads_ref, pred_in, out_far, pred_out, out, sent):
    pred_out[...] = pred_in[...]
    modes_t = modes_ref[...].T
    grads = grads_ref[...]
    swapped = pltpu.roll(grads, CHANNELS, 1) * lane_sign(grads.shape)
    copies = []
    for k in range(64 // OUTER):
        for m in range(k * OUTER, (k + 1) * OUTER):
            out[m] = (
                modes_t[0:64, m : m + 1] * grads[m : m + 1]
                + modes_t[64:128, m : m + 1] * swapped[m : m + 1]
            )
        here = pl.ds(k * OUTER, OUTER)
        copies.append(pltpu.make_async_copy(out.at[here], out_far.at[here], sent.at[k]))
        copies[-1].start()
    for copy in copies:
        copy.wait()


def outer(modes, grads, pred):
    whole = pl.BlockSpec(memory_space=pltpu.VMEM)
    return pl.pallas_call(
        outer_kernel,
        out_shape=(
            jax.ShapeDtypeStruct((64, 64, 128), F32),
            jax.ShapeDtypeStruct(pred.shape, F32),
        ),
        in_specs=[whole] * 3,
        out_specs=(pl.BlockSpec(memory_space=pl.ANY), whole),
        scratch_shapes=[
            pltpu.VMEM((64, 64, 128), F32), pltpu.SemaphoreType.DMA((64 // OUTER,))
        ],
        compiler_params=pltpu.CompilerParams(vmem_limit_bytes=VMEM_LIMIT),
        name="outer",
    )(modes, grads, pred)


def body(
    point_features, positions, targets, routes, live_counts, cell_neighbours, cell_counts,
    slot_neighbours, encoder_in, encoder_bias, encoder_out, decoder_in, decoder_bias,
    decoder_out, skip_weight, spectral_weight, readout_weight,
):
    pred, modes, grads = step(
        point_features.T, positions.T, targets.reshape(8, 128), routes.reshape(1, POINTS), live_counts,
        cell_neighbours, cell_counts, slot_neighbours,
        encoder_in, encoder_bias[None], encoder_out.T,
        decoder_in, decoder_bias[None], decoder_out.T, skip_weight, readout_weight[None],
        jnp.asarray(depth_waves()), spectral_weight.reshape(64, 64, 128),
        jnp.asarray(kron_forward_y()), jnp.asarray(kron_forward_x()),
        jnp.asarray(kron_inverse_x()), jnp.asarray(kron_inverse_y()),
    )
    gradient, pred = outer(modes, grads, pred)
    return pred, gradient.reshape(32, 2, 1, 64, 128)


def solution(mesh):
    in_specs = (
        P(("px", "py"), None), P(("px", "py"), None), P(("px", "py")), P(("px", "py"), None),
        P(("px", "py")), P("px", "py", None), P("px", "py", None), P(("px", "py"), None),
        P(), P(), P(), P(), P(), P(), P(),
        P(None, "px", "py", None, None), P(),
    )
    out_specs = (P(("px", "py"), None), P(None, "px", "py", None, None))
    return jax.shard_map(body, mesh=mesh, in_specs=in_specs, out_specs=out_specs, check_vma=False)
```

```python
import math
import types

import jax
import jax.numpy as jnp
import numpy as np
from jax import lax
from jax.experimental import pallas as pl
from jax.experimental.pallas import tpu as pltpu
from jax.sharding import PartitionSpec as P

MESH = pl.DeviceIdType.MESH
HALF_ROOT = 0.7071067811865476
GAUSS_NORM = 0.3989422804014327
BF = jnp.bfloat16
F32 = jnp.float32
GROUP = 16
CHANNELS = 64
COLUMNS = 32
DEPTH = 256
CAPACITY = 8
SLOT_TOTAL = 2048
POINTS = 1024
SCALING = 1.0 / math.sqrt(128 * 64 * 256)
VMEM_LIMIT = 60 * 1024 * 1024
ENC_COLUMNS = 2
PREP = 512
OUTER = 16
POST = 4096


def frequencies():
    counted = np.arange(32)
    return np.where(counted < 16, counted, counted - 32)


def wave(length, positions, frequency):
    angles = 2.0 * np.pi * ((positions[:, None] * frequency[None, :]) % length) / length
    return np.cos(angles), np.sin(angles)


def bf16_of(array):
    return np.asarray(array, np.float32).astype(BF)


def kron_forward_y():
    cos, sin = wave(64, np.arange(64), frequencies())
    out = []
    for part in (cos, sin):
        w = part.reshape(16, 4, 16, 2)
        full = np.einsum("cjdp,ik->dpicjk", w, np.eye(8)).transpose(0, 1, 2, 3, 5, 4)
        out.append(full.reshape(256, 512))
    return bf16_of(np.concatenate(out))


def kron_forward_x():
    cos, sin = wave(128, np.arange(128), frequencies())
    out = []
    for part in (cos, sin):
        w = part.reshape(16, 8, 32)
        full = np.einsum("air,ps->rpasi", w, np.eye(2))
        out.append(full.reshape(64, 256))
    return bf16_of(np.concatenate(out))


def kron_inverse_x():
    cos, sin = wave(128, np.arange(128), frequencies())
    out = []
    for part in (cos, sin):
        w = part.reshape(16, 8, 32)
        full = np.einsum("air,ps->apirs", w, np.eye(2))
        out.append(full.reshape(256, 64))
    return bf16_of(np.concatenate(out))


def kron_inverse_y():
    cos, sin = wave(64, np.arange(64), frequencies())
    out = []
    for part in (cos, sin):
        w = part.reshape(16, 4, 16, 2)
        full = np.einsum("cjdp,ik->cijdpk", w, np.eye(8))
        out.append(full.reshape(512, 256))
    return bf16_of(np.concatenate(out))


def depth_waves():
    cos, sin = wave(256, np.arange(16), np.arange(256))
    return bf16_of(np.concatenate([cos, -sin]))


def nt(left, right):
    return lax.dot_general(left, right, (((1,), (1,)), ((), ())), preferred_element_type=F32)


def mm(left, right):
    return jnp.dot(left, right, preferred_element_type=F32)


def identity(n):
    rows = lax.broadcasted_iota(jnp.int32, (n, n), 0)
    lanes = lax.broadcasted_iota(jnp.int32, (n, n), 1)
    return jnp.where(rows == lanes, 1.0, 0.0).astype(BF)


def lane_sign(shape):
    lanes = lax.broadcasted_iota(jnp.int32, shape, 1)
    return jnp.where(lanes < CHANNELS, 1.0, -1.0)


def turned(cos_part, sin_part, direction):
    swapped = pltpu.roll(sin_part, CHANNELS, 1)
    return cos_part + swapped * (lane_sign(swapped.shape) * direction)


def others():
    a, c = lax.axis_index("px"), lax.axis_index("py")
    return a, c


def greet():
    a, c = others()
    barrier = pltpu.get_barrier_semaphore()

    def greeting(d, carry):
        pl.semaphore_signal(barrier, inc=1, device_id=((a + d) & 15, c), device_id_type=MESH)
        pl.semaphore_signal(barrier, inc=1, device_id=(a, (c + d) & 15), device_id_type=MESH)
        return carry

    lax.fori_loop(1, GROUP, greeting, 0)


def greeted():
    pl.semaphore_wait(pltpu.get_barrier_semaphore(), 2 * (GROUP - 1))


def copy_to(axis, d, send, recv, send_sem, recv_sem):
    a, c = others()
    me = a if axis == "px" else c
    peer = (me + d) & 15
    return pltpu.make_async_remote_copy(
        src_ref=send.at[peer],
        dst_ref=recv.at[me],
        send_sem=send_sem.at[d],
        recv_sem=recv_sem.at[me],
        device_id=(peer, c) if axis == "px" else (a, peer),
        device_id_type=MESH,
    )


def start_all(axis, send, recv, send_sem, recv_sem):
    def start(d, carry):
        copy_to(axis, d, send, recv, send_sem, recv_sem).start()
        return carry

    lax.fori_loop(1, GROUP, start, 0)


def finish(axis, send, recv, send_sem, recv_sem):
    me = lax.axis_index(axis)
    recv[me] = send[me]

    def arrival(d, carry):
        copy_to(axis, d, send, recv, send_sem, recv_sem).wait_send()
        source = (me - d) & 15
        pltpu.make_async_remote_copy(
            src_ref=send.at[source],
            dst_ref=recv.at[source],
            send_sem=send_sem.at[d],
            recv_sem=recv_sem.at[source],
            device_id=others(),
            device_id_type=MESH,
        ).wait_recv()
        return carry

    lax.fori_loop(1, GROUP, arrival, 0)


def exchange(axis, send, recv, pair, meanwhile=None):
    start_all(axis, send, recv, *pair)
    if meanwhile is not None:
        meanwhile()
    finish(axis, send, recv, *pair)


def pick_rows(rows, sub):
    out = jnp.zeros(sub.shape, F32)
    for k, row in enumerate(rows):
        out = jnp.where(sub == k, row, out)
    return out


def send_points(r, meanwhile):
    greet()
    live = r.live[0]
    lanes = lax.broadcasted_iota(jnp.int32, (1, POINTS), 1)
    target = jnp.where(lanes < live, r.route[...], 256)
    owners = lax.broadcasted_iota(jnp.int32, (256, POINTS), 0)
    named = jnp.where(owners == target, 1.0, 0.0)
    earlier = jnp.where(
        lax.broadcasted_iota(jnp.int32, (POINTS, POINTS), 0)
        < lax.broadcasted_iota(jnp.int32, (POINTS, POINTS), 1),
        1.0,
        0.0,
    ).astype(BF)
    counted = mm(named.astype(BF), earlier)
    rank = jnp.sum(named * counted, axis=0, keepdims=True).astype(jnp.int32)
    kept = target < 256
    r.slot[...] = jnp.where(kept, target * CAPACITY + rank, -1)
    features = r.features[...]
    r.twice[...] = jnp.concatenate([features, features], 0)
    sub = lax.broadcasted_iota(jnp.int32, (8, POINTS), 0)
    places = r.positions[...].astype(F32)
    wanted = r.targets[...].astype(F32)
    wanted = jnp.concatenate([wanted[k : k + 1] for k in range(8)], 1)
    rest = pick_rows([places[0:1], places[1:2], places[2:3], wanted, 1.0], sub)
    rows = lax.broadcasted_iota(jnp.int32, (128, POINTS), 0)
    spread = jnp.where((rows >> 3) == (target & 15), jnp.concatenate([rest] * 16, 0), 0.0)
    mine = jnp.where(kept, (target >> 4) * CAPACITY + rank, -1)
    hot = jnp.where(rows == mine, 1.0, 0.0).astype(BF)
    r.rest[...] = nt(hot, spread.astype(BF)).reshape(GROUP, 8, 128)
    greeted()
    a = lax.axis_index("px")
    low_lanes = lax.broadcasted_iota(jnp.int32, (64, 128), 1) < 64
    nothing = jnp.zeros((8, 128), F32)

    def pack(step, carry):
        group = ((a >> 2) + 2 + step) & 3
        at = lax.broadcasted_iota(jnp.int32, (512, POINTS), 0) + group * 512
        hot = jnp.where(at == r.slot[...], 1.0, 0.0).astype(BF)
        packed = nt(hot, r.twice[...])
        for k in range(4):
            peer = group * 4 + k
            block = packed[k * 128 : (k + 1) * 128]
            r.send1[peer, 0:64] = jnp.where(low_lanes, block[0:64], block[64:128]).astype(BF)
            r.send1[peer, 64:80] = jnp.concatenate([r.rest[peer], nothing], 0).astype(BF)

            @pl.when(peer != a)
            def _():
                copy_to("px", (peer - a) & 15, r.send1, r.recv1, r.s1, r.r1).start()

        return carry

    lax.fori_loop(0, 4, pack, 0)
    meanwhile(0)()
    finish("px", r.send1, r.recv1, r.s1, r.r1)
    for source in range(GROUP):
        r.regroup[source] = r.recv1[source, 0:64].astype(F32).reshape(8, CAPACITY, 128)
        r.rest[source] = r.recv1[source, 64:80].astype(F32)[0:8]
    eye = identity(128)
    rest = nt(eye, r.rest[...].reshape(128, 128).astype(BF))
    for c in range(8):
        first = r.regroup[0:8, c].reshape(64, 128)
        second = r.regroup[8:16, c].reshape(64, 128)
        r.send2[c, 0:64] = jnp.where(
            low_lanes, first, pltpu.roll(second, 64, 1)
        ).astype(BF)
        r.send2[c + 8, 0:64] = jnp.where(
            low_lanes, pltpu.roll(first, 64, 1), second
        ).astype(BF)
    for c in range(GROUP):
        r.send2[c, 64:80] = jnp.concatenate([rest[c * 8 : c * 8 + 8], nothing], 0).astype(BF)
    exchange("py", r.send2, r.recv2, (r.s2, r.r2), meanwhile(1))


def slot_tables(r):
    eye = identity(128)
    low_lanes = lax.broadcasted_iota(jnp.int32, (8, 128), 1) < 64
    r.pos_rows[...] = jnp.zeros(r.pos_rows.shape, F32)
    for h in range(8):
        rows = jnp.concatenate([r.recv2[2 * h, 0:64], r.recv2[2 * h + 1, 0:64]], 0)
        flipped = nt(eye, rows).astype(BF)
        r.table[h * 64 : (h + 1) * 64, 0:128] = flipped[0:64]
        r.table[h * 64 : (h + 1) * 64, 128:256] = flipped[64:128]
        even = r.recv2[2 * h, 64:80].astype(F32)[0:8]
        odd = r.recv2[2 * h + 1, 64:80].astype(F32)[0:8]
        r.rest[2 * h] = even
        r.rest[2 * h + 1] = odd
        left = jnp.where(low_lanes, even, pltpu.roll(odd, 64, 1))
        right = jnp.where(low_lanes, pltpu.roll(even, 64, 1), odd)
        for d in range(3):
            r.pos_rows[d * 8 + h : d * 8 + h + 1, 0:128] = left[d : d + 1]
            r.pos_rows[d * 8 + h : d * 8 + h + 1, 128:256] = right[d : d + 1]
    r.table[512:544, :] = r.pos_rows[...].astype(BF)
    by_slot = nt(eye, r.rest[...].reshape(128, 128).astype(BF))
    rows = lax.broadcasted_iota(jnp.int32, (128, 128), 0)
    lanes = lax.broadcasted_iota(jnp.int32, (128, 128), 1)
    same = (rows >> 3) == (lanes >> 3)
    sub = lax.broadcasted_iota(jnp.int32, (8, 128), 0)
    part = lax.broadcasted_iota(jnp.int32, (8, 128), 1) & 7
    wanted = jnp.where(sub < 3, sub, sub - 3)
    chooser = jnp.where(part == wanted, 1.0, 0.0).astype(BF)
    for a in range(GROUP):
        spread = jnp.concatenate([by_slot[a * 8 : a * 8 + 8]] * 16, 0)
        extra = nt(chooser, jnp.where(same, spread, 0.0).astype(BF))
        h, half = a // 2, (a % 2) * 128
        r.extra[h, :, half : half + 128] = extra
        r.target[h : h + 1, half : half + 128] = extra[6:7]
        r.living[h : h + 1, half : half + 128] = extra[7:8]


def fetches(r, names):
    order = list(FETCHED)
    return [
        pltpu.make_async_copy(
            getattr(r, name + "_far"), getattr(r, name), r.fetched.at[order.index(name)]
        )
        for name in names
    ]


def group_sums(r):
    for ref, shift in ((r.sums, 3), (r.pairs, 2)):
        rows = lax.broadcasted_iota(jnp.int32, ref.shape, 0)
        lanes = lax.broadcasted_iota(jnp.int32, ref.shape, 1)
        ref[...] = jnp.where((rows >> shift) == lanes, 1.0, 0.0).astype(BF)


def first_layers(r):
    def halves(values):
        high = (values * 0.5).astype(BF).astype(F32)
        return high, values * 0.5 - high

    high, low = halves(r.ein[...])
    bias_high, bias_low = halves(r.ebias[...])
    sub = lax.broadcasted_iota(jnp.int32, (8, 80), 0)
    rows = [jnp.broadcast_to(part[d : d + 1], (8, 80)) for part in (high, low) for d in range(3)]
    rows.append(
        pick_rows(
            [-part[d : d + 1] for part in (high, low) for d in range(3)] + [bias_high, bias_low],
            sub,
        )
    )
    r.ew1[...] = nt(identity(80), jnp.concatenate(rows, 0).astype(BF)).astype(BF)
    high, low = halves(r.din[...])
    bias_high, bias_low = halves(r.dbias[...])
    sub = lax.broadcasted_iota(jnp.int32, (8, 256), 0)
    positive = [part[d : d + 1] for part in (high, low) for d in range(3)]
    negative = [-row for row in positive] + [bias_high, bias_low]
    rows = jnp.concatenate([pick_rows(positive, sub), pick_rows(negative, sub)], 0)
    r.dw1[...] = nt(identity(256), rows.astype(BF)).astype(BF)
    r.skip_t[...] = nt(identity(64), r.skip[...]).astype(BF)
    rows = lax.broadcasted_iota(jnp.int32, (64, 64), 0)
    lanes = lax.broadcasted_iota(jnp.int32, (64, 64), 1)
    r.read[...] = jnp.sum(
        jnp.where(rows == lanes, r.readout[...], 0.0), axis=1, keepdims=True
    )


def first_layer_centres(ij, depth, sub):
    cx = ((ij >> 2).astype(F32) + 0.5) * 0.25 - 1.0
    cy = ((ij & 3).astype(F32) + 0.5) * 0.5 - 1.0
    cz = (depth.astype(F32) + 0.5) * (2.0 / DEPTH) - 1.0
    part3 = jnp.where(sub >= 3, sub - 3, sub)
    return jnp.where(
        sub >= 6, 1.0, jnp.where(part3 == 0, cx, jnp.where(part3 == 1, cy, cz))
    )


def place_lists(r):
    for i in range(8):
        r.counts[i * 4 : (i + 1) * 4, :] = r.cnt[i].astype(F32)
        r.low[i * 4 : (i + 1) * 4, :] = r.nbr[i]
    spread = nt(r.counts[...].astype(BF), r.sums[...])
    places = (lax.broadcasted_iota(jnp.int32, (COLUMNS, 2048), 1) & 7).astype(F32)
    ids = r.low[...]
    r.high[...] = jnp.where(places < spread, (ids >> 4) & 7, 8)
    r.low[...] = (
        ((ids >> 10) << 7) + (((ids >> 3) & 1) << 6) + (((ids >> 7) & 7) << 3) + (ids & 7)
    )


def encode(r):
    n = 2048 * ENC_COLUMNS

    def columns(step, carry):
        rows = [step * ENC_COLUMNS + k for k in range(ENC_COLUMNS)]
        low = jnp.concatenate([r.low[pl.ds(row, 1), :] for row in rows], 1)
        high = jnp.concatenate([r.high[pl.ds(row, 1), :] for row in rows], 1)
        cells = lax.broadcasted_iota(jnp.int32, (256, n), 0).astype(F32).astype(BF)
        hot = jnp.where(
            cells == low.astype(F32).astype(BF), jnp.asarray(1.0, BF), jnp.asarray(0.0, BF)
        )
        found = mm(r.table[...], hot)
        high8 = jnp.broadcast_to(high, (8, n))
        near = jnp.zeros((8, 8, n), F32)
        for h in range(8):
            part = found[h * 64 : (h + 1) * 64].reshape(8, 8, n)
            near = jnp.where((high8 == h)[None], part, near)
        sub = lax.broadcasted_iota(jnp.int32, (8, n), 0)
        lane = lax.broadcasted_iota(jnp.int32, (8, n), 1)
        place = found[512:536].reshape(3, 8, n)
        place = jnp.where((high8 == sub)[None], place, 0.0).reshape(24, n)
        ij = (lane >> 11) + step * ENC_COLUMNS
        centre = first_layer_centres(ij, (lane & 2047) >> 3, sub)
        stacked = jnp.concatenate([place, place, centre], 0).astype(BF)
        half = mm(r.ew1[...], stacked)
        hidden = (half + half * jnp.tanh(half)).astype(BF)
        kernel = mm(r.ewo[...], hidden)
        shares = (kernel * near.reshape(64, n)).astype(BF)
        for k in range(ENC_COLUMNS):
            row = pl.multiple_of((step * ENC_COLUMNS + k) * 64, 64)
            r.prod[pl.ds(row, 64), :] = shares[:, k * 2048 : (k + 1) * 2048]
        return carry

    lax.fori_loop(0, COLUMNS // ENC_COLUMNS, columns, 0, unroll=4)
    shares = 1.0 / r.counts[...]
    group = 8
    for g in range(COLUMNS // group):
        latent = mm(r.prod[g * group * 64 : (g + 1) * group * 64, :], r.sums[...])
        for k in range(group):
            ij = g * group + k
            r.lat[ij * 64 : (ij + 1) * 64, :] = (
                latent[k * 64 : (k + 1) * 64] * shares[ij : ij + 1]
            ).astype(BF)
    both = nt(r.waves[...], r.lat[...])
    for ij in range(COLUMNS):
        part = both[:, ij * 64 : (ij + 1) * 64]
        r.z_rows[:, ij : ij + 1, :] = jnp.concatenate([part[0:16], part[16:32]], 1).reshape(
            16, 1, 128
        )
    r.z[...] = r.z_rows[...].astype(BF)


def forward_modes(z, r, pairs, recv_a, send_b, recv_b, meanwhile):
    meanwhile(0)()
    finish("py", z, recv_a, *pairs[0])
    u = mm(r.ky[...], recv_a[...].reshape(512, 128))
    send_b[...] = turned(u[:256], u[256:], 1.0).astype(BF).reshape(GROUP, 16, 128)
    exchange("px", send_b, recv_b, pairs[1], meanwhile(1))
    u = mm(r.kx[...], recv_b[...].reshape(256, 128))
    return turned(u[:64], u[64:], 1.0) * SCALING


def own_doubling():
    return jnp.where(lax.axis_index("py") == 0, 1.0, 2.0)


def mixed(modes, weight_ref):
    lanes = lax.broadcasted_iota(jnp.int32, (64, 128), 1)
    swapped = pltpu.roll(modes, CHANNELS, 1)
    real2 = jnp.where(lanes < CHANNELS, modes, swapped)
    imag2 = jnp.where(lanes < CHANNELS, swapped, modes)
    rows4 = lax.broadcasted_iota(jnp.int32, (64, 256), 0) & 3
    keep = (lax.broadcasted_iota(jnp.int32, (64, 256), 1) >> 6) == rows4
    real4 = jnp.where(keep, jnp.concatenate([real2, real2], 1), 0.0)
    imag4 = jnp.where(keep, jnp.concatenate([imag2, imag2], 1), 0.0)
    first = (lax.broadcasted_iota(jnp.int32, (16, 128), 0) & 7) < 4
    out = []
    for h in range(8):
        left = jnp.concatenate([real4[8 * h : 8 * h + 8], imag4[8 * h : 8 * h + 8]], 0)
        left = left.astype(BF)
        lower = mm(left, weight_ref[8 * h : 8 * h + 4].reshape(256, 128))
        upper = mm(left, weight_ref[8 * h + 4 : 8 * h + 8].reshape(256, 128))
        both = jnp.where(first, lower, upper)
        out.append(turned(both[0:8], both[8:16], -1.0))
    return jnp.concatenate(out, 0)


def fourier(r, meanwhile):
    start_all("py", r.z, r.recv_a, r.s3, r.r3)
    modes = forward_modes(
        r.z, r, ((r.s3, r.r3), (r.s4, r.r4)), r.recv_a, r.send_b, r.recv_b, meanwhile
    )
    r.modes[...] = modes
    v = mixed(modes, r.weight) * (own_doubling() * SCALING)
    u = mm(r.kxi[...], v.astype(BF))
    r.send_c[...] = turned(u[:256], u[256:], -1.0).astype(BF).reshape(GROUP, 16, 128)
    exchange("px", r.send_c, r.recv_c, (r.s5, r.r5), meanwhile(2))
    u = mm(r.kyi[...], r.recv_c[...].reshape(256, 128))
    r.send_d[...] = turned(u[:512], u[512:], -1.0).astype(BF).reshape(GROUP, COLUMNS, 128)
    exchange("py", r.send_d, r.recv_d, (r.s6, r.r6), meanwhile(3))


def depth_basis(r):
    n = PREP

    def block(step, carry):
        here = pl.ds(pl.multiple_of(step * n, n), n)
        ids = r.lists[:, here]
        low, column = ids & 255, ids >> 8
        cells = lax.broadcasted_iota(jnp.int32, (256, n), 0).astype(F32).astype(BF)
        hot = jnp.where(
            cells == low.astype(F32).astype(BF), jnp.asarray(1.0, BF), jnp.asarray(0.0, BF)
        )
        tw = mm(r.waves[...], hot)
        match = lax.broadcasted_iota(jnp.int32, (COLUMNS, n), 0) == column
        for q in range(32):
            r.basis[q * 32 : (q + 1) * 32, here] = jnp.where(match, tw[q : q + 1], 0.0).astype(BF)
        return carry

    lax.fori_loop(0, 4 * SLOT_TOTAL // n, block, 0)


def prepare(r, first, last):
    n = PREP

    def block(step, carry):
        off = pl.multiple_of(step * n, n)
        half_block = step & 1
        expanded = nt(
            r.extra[step >> 1].astype(BF),
            r.pairs[pl.ds(pl.multiple_of(half_block * n, n), n), :],
        )
        ids = r.lists[:, pl.ds(off, n)]
        low, column = ids & 255, ids >> 8
        cells = lax.broadcasted_iota(jnp.int32, (256, n), 0).astype(F32).astype(BF)
        hot = jnp.where(
            cells == low.astype(F32).astype(BF), jnp.asarray(1.0, BF), jnp.asarray(0.0, BF)
        )
        found = mm(r.lat[...], hot)
        column8 = jnp.broadcast_to(column, (8, n))
        near = jnp.zeros((8, 8, n), F32)
        for k in range(COLUMNS):
            part = found[k * 64 : (k + 1) * 64].reshape(8, 8, n)
            near = jnp.where((column8 == k)[None], part, near)
        r.before[:, pl.ds(off, n)] = mm(r.skip_t[...], near.reshape(64, n).astype(BF))
        sub = lax.broadcasted_iota(jnp.int32, (8, n), 0)
        stacked = jnp.concatenate(
            [expanded, first_layer_centres(column, low, sub)], 0
        ).astype(BF)
        half = mm(r.dw1[...], stacked)
        hidden = (half + half * jnp.tanh(half)).astype(BF)
        r.kern[:, pl.ds(off, n)] = mm(r.dwo[...], hidden) * r.read[...]
        return carry

    lax.fori_loop(first, last, block, 0)


def parts_of(values, parts):
    out, rest = [], values
    for _ in range(parts):
        rounded = rest.astype(BF).astype(F32)
        out.append(rounded)
        rest = rest - rounded
    return jnp.concatenate(out, 0).astype(BF)


def decode(r):
    flipped = nt(identity(128), r.recv_d[...].reshape(512, 128))
    r.back_t[...] = jnp.concatenate([flipped[0:64], flipped[64:128]], 1).astype(BF)
    n = POST

    def forward(step, carry):
        off = pl.multiple_of(step * n, n)
        here = pl.ds(off, n)
        before = mm(r.back_t[...], r.basis[:, here]) + r.before[:, here]
        phi = 0.5 * (1.0 + lax.erf(before * HALF_ROOT))
        slope = phi + before * jnp.exp(-0.5 * before * before) * GAUSS_NORM
        weighed = r.kern[:, here]
        r.kern[:, here] = weighed * slope
        dots = jnp.sum(weighed * (before * phi), axis=0, keepdims=True)
        for k in range(n // 1024):
            r.dots[pl.ds(step * (n // 1024) + k, 1), :] = dots[:, k * 1024 : (k + 1) * 1024]
        return carry

    lax.fori_loop(0, 4 * SLOT_TOTAL // n, forward, 0)
    summed = mm(parts_of(r.dots[...], 3), r.pairs[...])
    summed = summed[0:8] + summed[8:16] + summed[16:24]
    living = r.living[...]
    pred = living * (summed * 0.25)
    for h in range(8):
        r.pred[:, h * 256 : (h + 1) * 256] = pred[h : h + 1]
    residue = living * (pred - r.target[...]) * 0.25
    spread = nt(parts_of(residue, 2), r.pairs[...])
    r.dots[...] = spread[0:8] + spread[8:16]
    for h in range(8):
        here = slice(h * 1024, (h + 1) * 1024)
        r.shares[:, here] = (r.kern[:, here] * r.dots[h : h + 1]).astype(BF)


def gradient_depth_modes(r):
    me = lax.axis_index("py")
    n = 4 * 1024

    def half(first):
        depths = [(me + first + k) & 15 for k in range(8)]
        starts = [pl.multiple_of(part * 512 + q * 32, 32) for part in range(2) for q in depths]
        for step in range(4 * SLOT_TOTAL // n):
            here = slice(step * n, (step + 1) * n)
            waves = jnp.concatenate([r.basis[pl.ds(start, 32), here] for start in starts], 0)
            part = nt(waves, r.shares[:, here])
            r.total[...] = part if step == 0 else r.total[...] + part
        for k, q in enumerate(depths):
            real, imag = (r.total[256 * p + k * 32 : 256 * p + k * 32 + 32] for p in range(2))
            r.grad_z[q] = jnp.concatenate([real, imag], 1).astype(BF)

    def send(first, last):
        def start(d, carry):
            copy_to("py", d, r.grad_z, r.recv_e, r.s7, r.r7).start()
            return carry

        lax.fori_loop(first, last, start, 0)

    half(4)
    send(4, 12)
    half(12)
    send(12, 16)
    send(1, 4)


WIDE, NARROW, POINT_BLOCK = (GROUP, COLUMNS, 128), (GROUP, 16, 128), (GROUP, 80, 128)
INPUTS = (
    "features", "positions", "targets", "route", "live", "nbr_far", "cnt_far", "lists_far",
    "ein", "ebias", "ewo", "din", "dbias", "dwo", "skip", "readout",
    "waves", "weight_far", "ky_far", "kx_far", "kxi_far", "kyi_far",
)
FETCHED = {
    "nbr": ((8, 4, 2048), jnp.int32), "cnt": ((8, 4, 256), jnp.int32),
    "lists": ((1, 4 * SLOT_TOTAL), jnp.int32), "weight": ((64, 64, 128), BF),
    "ky": ((512, 512), BF), "kx": ((128, 256), BF), "kxi": ((512, 64), BF),
    "kyi": ((1024, 256), BF),
}
EARLY = ("nbr", "cnt", "lists")
OUTPUTS = {
    "pred": ((1, SLOT_TOTAL), F32), "modes": ((64, 128), F32), "grads": ((64, 128), F32),
}
SCRATCH = {
    "send1": (POINT_BLOCK, BF), "recv1": (POINT_BLOCK, BF),
    "send2": (POINT_BLOCK, BF), "recv2": (POINT_BLOCK, BF),
    "regroup": ((GROUP, 8, CAPACITY, 128), F32), "rest": ((GROUP, 8, 128), F32),
    "slot": ((1, POINTS), jnp.int32), "twice": ((128, POINTS), BF),
    "sums": ((2048, 256), BF), "pairs": ((1024, 256), BF), "ew1": ((80, 56), BF), "dw1": ((256, 16), BF), "skip_t": ((64, 64), BF),
    "read": ((64, 1), F32), "counts": ((COLUMNS, DEPTH), F32), "low": ((COLUMNS, 2048), jnp.int32),
    "table": ((544, 256), BF), "pos_rows": ((32, 256), F32),
    "extra": ((8, 8, 256), F32), "target": ((8, 256), F32), "living": ((8, 256), F32),
    "high": ((COLUMNS, 2048), jnp.int32),
    "prod": ((COLUMNS * 64, 2048), BF), "lat": ((COLUMNS * 64, DEPTH), BF),
    "z_rows": (WIDE, F32), "z": (WIDE, BF), "recv_a": (WIDE, BF), "send_b": (NARROW, BF),
    "recv_b": (NARROW, BF), "send_c": (NARROW, BF), "recv_c": (NARROW, BF),
    "send_d": (WIDE, BF), "recv_d": (WIDE, BF),
    "before": ((64, 4 * SLOT_TOTAL), F32), "kern": ((64, 4 * SLOT_TOTAL), F32),
    "basis": ((1024, 4 * SLOT_TOTAL), BF), "back_t": ((64, 1024), BF),
    "dots": ((8, 1024), F32), "total": ((512, 64), F32), "shares": ((64, 4 * SLOT_TOTAL), BF),
    "grad_z": (WIDE, BF), "recv_e": (WIDE, BF), "send_f": (NARROW, BF), "recv_f": (NARROW, BF),
    **FETCHED,
}
EXCHANGES = 8


def step_kernel(*refs):
    names = list(INPUTS) + list(OUTPUTS) + list(SCRATCH)
    for k in range(1, EXCHANGES + 1):
        names += [f"s{k}", f"r{k}"]
    names.append("fetched")
    r = types.SimpleNamespace(**dict(zip(names, refs)))

    def before_points():
        for fetch in fetches(r, EARLY):
            fetch.wait()
        group_sums(r)
        first_layers(r)
        place_lists(r)

    for fetch in fetches(r, FETCHED):
        fetch.start()
    send_points(r, lambda k: before_points if k == 0 else lambda: depth_basis(r))
    slot_tables(r)
    encode(r)
    for fetch in fetches(r, [name for name in FETCHED if name not in EARLY]):
        fetch.wait()
    blocks = 4 * SLOT_TOTAL // PREP // 4
    fourier(r, lambda k: lambda: prepare(r, k * blocks, (k + 1) * blocks))
    decode(r)
    gradient_depth_modes(r)
    grads = forward_modes(
        r.grad_z, r, ((r.s7, r.r7), (r.s8, r.r8)), r.recv_e, r.send_f, r.recv_f,
        lambda k: lambda: None,
    )
    r.grads[...] = grads * own_doubling()


def step(*inputs):
    whole = pl.BlockSpec(memory_space=pltpu.VMEM)
    in_specs = [whole] * len(INPUTS)
    in_specs[INPUTS.index("live")] = pl.BlockSpec(memory_space=pltpu.SMEM)
    for name in FETCHED:
        in_specs[INPUTS.index(name + "_far")] = pl.BlockSpec(memory_space=pl.ANY)
    semaphores = [pltpu.SemaphoreType.DMA((GROUP,))] * (2 * EXCHANGES)
    semaphores.append(pltpu.SemaphoreType.DMA((len(FETCHED),)))
    return pl.pallas_call(
        step_kernel,
        out_shape=tuple(jax.ShapeDtypeStruct(*v) for v in OUTPUTS.values()),
        in_specs=in_specs,
        out_specs=(whole,) * len(OUTPUTS),
        scratch_shapes=[pltpu.VMEM(*v) for v in SCRATCH.values()] + semaphores,
        compiler_params=pltpu.CompilerParams(
            collective_id=0, has_side_effects=True, vmem_limit_bytes=VMEM_LIMIT
        ),
        name="training_step",
    )(*inputs)


def outer_kernel(modes_ref, grads_ref, pred_in, out_far, pred_out, out, sent):
    pred_out[...] = pred_in[...]
    modes_t = modes_ref[...].T
    grads = grads_ref[...]
    swapped = pltpu.roll(grads, CHANNELS, 1) * lane_sign(grads.shape)
    copies = []
    for k in range(64 // OUTER):
        for m in range(k * OUTER, (k + 1) * OUTER):
            out[m] = (
                modes_t[0:64, m : m + 1] * grads[m : m + 1]
                + modes_t[64:128, m : m + 1] * swapped[m : m + 1]
            )
        here = pl.ds(k * OUTER, OUTER)
        copies.append(pltpu.make_async_copy(out.at[here], out_far.at[here], sent.at[k]))
        copies[-1].start()
    for copy in copies:
        copy.wait()


def outer(modes, grads, pred):
    whole = pl.BlockSpec(memory_space=pltpu.VMEM)
    return pl.pallas_call(
        outer_kernel,
        out_shape=(
            jax.ShapeDtypeStruct((64, 64, 128), F32),
            jax.ShapeDtypeStruct(pred.shape, F32),
        ),
        in_specs=[whole] * 3,
        out_specs=(pl.BlockSpec(memory_space=pl.ANY), whole),
        scratch_shapes=[
            pltpu.VMEM((64, 64, 128), F32), pltpu.SemaphoreType.DMA((64 // OUTER,))
        ],
        compiler_params=pltpu.CompilerParams(vmem_limit_bytes=VMEM_LIMIT),
        name="outer",
    )(modes, grads, pred)


def body(
    point_features, positions, targets, routes, live_counts, cell_neighbours, cell_counts,
    slot_neighbours, encoder_in, encoder_bias, encoder_out, decoder_in, decoder_bias,
    decoder_out, skip_weight, spectral_weight, readout_weight,
):
    pred, modes, grads = step(
        point_features.T, positions.T, targets.reshape(8, 128), routes.reshape(1, POINTS), live_counts,
        cell_neighbours, cell_counts, slot_neighbours,
        encoder_in, encoder_bias[None], encoder_out.T,
        decoder_in, decoder_bias[None], decoder_out.T, skip_weight, readout_weight[None],
        jnp.asarray(depth_waves()), spectral_weight.reshape(64, 64, 128),
        jnp.asarray(kron_forward_y()), jnp.asarray(kron_forward_x()),
        jnp.asarray(kron_inverse_x()), jnp.asarray(kron_inverse_y()),
    )
    gradient, pred = outer(modes, grads, pred)
    return pred, gradient.reshape(32, 2, 1, 64, 128)


def solution(mesh):
    in_specs = (
        P(("px", "py"), None), P(("px", "py"), None), P(("px", "py")), P(("px", "py"), None),
        P(("px", "py")), P("px", "py", None), P("px", "py", None), P(("px", "py"), None),
        P(), P(), P(), P(), P(), P(), P(),
        P(None, "px", "py", None, None), P(),
    )
    out_specs = (P(("px", "py"), None), P(None, "px", "py", None, None))
    return jax.shard_map(body, mesh=mesh, in_specs=in_specs, out_specs=out_specs, check_vma=False)
```
